32 devices in a mesh: sector: 4 (over y, core), inner: 8 (over z, x).
Axes of the slice: x: 2, y: 2, z: 4, core: 2. Of those that a mesh axis runs over, the one named last changes fastest.
Arguments:
- density: float32 [128, 64, 8192], P('inner', None, 'sector'), may hold values from -6 to 6
- source_sector: int32 [8, 4, 16], P('inner'), may hold values from 0 to 3, as said below
- source_tile: int32 [8, 4, 16], P('inner'), may hold values from 0 to 15
- matrix_id: int32 [8, 4, 16], P('inner'), may hold values from 0 to 31
- cubic_weights: float32 [32, 128, 128], replicated, may hold values from -0.6 to 1.5, as said below
- bin_cells: int32 [4, 8], P('sector'), may hold values from 1 to 512, 2048 in all within a row
- wave_level: float32 [4, 8], P('sector'), may hold values from 0.15 to 1
- energy_rate: float32 [128, 64], replicated, may hold values from 0.01 to 0.12
- pitch_rate: float32 [128, 64], replicated, may hold values from 0.01 to 0.12
Outputs:
- advanced: float32 [128, 64, 8192], P('inner', None, 'sector')
The draws below stay inside these ranges and needn't reach their ends.
Inputs may be any that keep to these rules, and one draw needn't show every extreme that they name: `source_sector`: for every energy block and destination sector, at most 6 of its 16 tiles depart from any one sector, exactly 6 depart from one sector, and that sector lies one to three sectors below the destination, cyclically. `cubic_weights`: every row of every matrix sums to one.
All inputs are finite; a program needn't handle non-finite values.
Results may differ from the reference program's by a relative error of at most 0.000096.
Values sent between devices are 32-bit elements; how exact they have to be, the bound alone decides.
No kernel may reach another device: no remote copies, remote signals or barrier semaphores. Data moves between devices by JAX's collectives and lax.ppermute only.
A program may use at most 128 MiB of HBM per device.

```python
import math
import jax
import jax.numpy as jnp
import numpy as np
from jax import lax

E = 128
P_SIZE = 64
TILE = 128
NW = 32
PASSES = 12
NT = 16
EB = 16
CAP = 6
MAXC = 512
CELLS = 8192
N_SECTOR = 4
N_INNER = 8


def draw_source_sector(key, part):
    key_back, key_score, key_order = jax.random.split(jax.random.fold_in(key, 7), 3)
    rows = N_INNER * N_SECTOR
    dest = jnp.tile(jnp.arange(N_SECTOR, dtype=jnp.int32), N_INNER)
    back = jax.random.randint(key_back, (rows,), 0, 3)
    favoured = (dest - 1 - back) % N_SECTOR
    slot_sector = jnp.arange(N_SECTOR * CAP, dtype=jnp.int32) // CAP
    scores = jax.random.randint(key_score, (rows, N_SECTOR * CAP), 0, 1 << 20)
    scores = scores + jnp.where(slot_sector[None, :] == favoured[:, None], 1 << 21, 0)
    order = jnp.argsort(-scores, axis=1, stable=True)[:, :NT]
    chosen = slot_sector[order]
    shuffle = jax.random.randint(key_order, (rows, NT), 0, 1 << 20) * NT + jnp.arange(NT, dtype=jnp.int32)[None, :]
    mixed = jnp.take_along_axis(chosen, jnp.argsort(shuffle, axis=1), axis=1)
    return mixed.reshape(N_INNER, N_SECTOR, NT).astype(jnp.int32)


def draw_cubic_weights(key, part):
    frac = jax.random.uniform(jax.random.fold_in(key, 11), (NW, 1, 1), minval=0.15, maxval=0.85, dtype=jnp.float32)
    rows = jnp.arange(TILE, dtype=jnp.int32)[None, :, None]
    cols = jnp.arange(TILE, dtype=jnp.int32)[None, None, :]
    coeffs = [-frac * (frac - 1.0) * (frac - 2.0) / 6.0, (frac + 1.0) * (frac - 1.0) * (frac - 2.0) / 2.0, -(frac + 1.0) * frac * (frac - 2.0) / 2.0, (frac + 1.0) * frac * (frac - 1.0) / 6.0]
    total = jnp.zeros((NW, TILE, TILE), jnp.float32)
    for place in range(4):
        target = jnp.clip(rows + place - 1, 0, TILE - 1)
        total = total + coeffs[place] * (cols == target).astype(jnp.float32)
    spread = 0.3 * TILE ** (-0.5)
    noise_key = jax.random.fold_in(key, 13)
    noise = jnp.clip(jax.random.normal(noise_key, (NW, TILE, TILE), dtype=jnp.float32) * spread, -3.0 * spread, 3.0 * spread)
    noise = noise - jnp.mean(noise, axis=2, keepdims=True)
    return total + noise


def plant(array, key, smallest, top_value):
    longest = array.shape.index(max(array.shape))
    spots = []
    for shift in (0, 1):
        where = [jax.random.randint(jax.random.fold_in(key, axis), (), 0, length) for axis, length in enumerate(array.shape)]
        where[longest] = (where[longest] + shift) % array.shape[longest]
        spots.append(tuple(where))
    return array.at[spots[0]].set(smallest).at[spots[1]].set(top_value)


def block_scale(key, shape, pieces, low, largest):
    factor_of = 1.0
    for axis_at, blocks in pieces:
        heights = jax.random.uniform(jax.random.fold_in(jax.random.fold_in(key, 6), axis_at), (blocks,), jnp.float32, low / len(pieces), largest / len(pieces))
        factor_of = factor_of * jnp.repeat(jnp.exp(heights), shape[axis_at] // blocks).reshape((-1,) + (1,) * (len(shape) - 1 - axis_at))
    return factor_of


def split_up(number_of, total, most, slope):
    loads = [(1 << 20) // math.isqrt(grade ** slope) + 1 for grade in range(2, number_of + 1)]
    spare, counts = total - most - (number_of - 1), [1] * (number_of - 1)
    while spare > 0:
        free = [i for i in range(number_of - 1) if counts[i] < most]
        whole, remaining = sum([loads[i] for i in free]), spare
        for i in free:
            more = min(most - counts[i], max(1, remaining * loads[i] // whole), spare)
            counts[i] = counts[i] + more
            spare = spare - more
    return np.array([most] + counts)


def uneven_parts(stream_key, amount, total, bound, skew):
    if amount == 2:
        one = jax.random.randint(stream_key, (), max(1, total - bound), min(bound, total - 1) + 1)
        return jnp.stack([one, total - one])
    lengths = jnp.asarray(split_up(amount, total, bound, skew), jnp.int32)
    twos = (amount - 1) // 2
    giver, taker = lengths[1:1 + 2 * twos:2], lengths[2:2 + 2 * twos:2]
    room = jnp.minimum(giver - 1, bound - taker)
    shifted = jax.random.randint(jax.random.fold_in(stream_key, 1), (twos,), 0, 1 << 20) % (room + 1)
    lengths = lengths.at[1:1 + 2 * twos:2].set(giver - shifted).at[2:2 + 2 * twos:2].set(taker + shifted)
    return lengths[jax.random.permutation(jax.random.fold_in(stream_key, 2), amount)]


def normal_values(rng, shape, width, limit, shards=(), kind=jnp.bfloat16):
    drawn = width * jax.random.normal(rng, shape, jnp.float32)
    if shards:
        drawn = drawn * block_scale(rng, shape, shards, -0.22, 0.18)
    return jnp.clip(drawn, -limit, limit).astype(kind)


def setup_inputs(seed: int = 0) -> dict:
    seeds = jax.random.split(jax.random.key(seed), 10)
    return {
        "density": normal_values(seeds[0], (E, P_SIZE, CELLS), 1.0, 6.0, ((0, 8), (2, 4)), jnp.float32),
        "source_sector": draw_source_sector(jax.random.fold_in(seeds[9], 71), 0),
        "source_tile": plant(jax.random.randint(seeds[2], (N_INNER, N_SECTOR, NT), 0, NT), jax.random.fold_in(seeds[2], 1), 0, NT - 1).astype(jnp.int32),
        "matrix_id": plant(jax.random.randint(seeds[3], (N_INNER, N_SECTOR, NT), 0, NW), jax.random.fold_in(seeds[3], 1), 0, NW - 1).astype(jnp.int32),
        "cubic_weights": draw_cubic_weights(jax.random.fold_in(seeds[9], 71), 0),
        "bin_cells": jax.vmap(lambda own: uneven_parts(own, N_INNER, NT * TILE, MAXC, 2))(jax.random.split(seeds[5], N_SECTOR)).reshape((N_SECTOR, N_INNER)).astype(jnp.int32),
        "wave_level": jnp.clip(jnp.exp(math.log(1.0) - 1.89712 * jax.random.uniform(seeds[6], (N_SECTOR, N_INNER), jnp.float32) ** block_scale(seeds[6], (N_SECTOR, N_INNER), ((0, 4),), -0.2, 0.2)), 0.15, 1.0),
        "energy_rate": jnp.clip(jnp.exp(jax.random.uniform(seeds[7], (E, P_SIZE), jnp.float32, math.log(0.01), math.log(0.12))), 0.01, 0.12),
        "pitch_rate": jnp.clip(jnp.exp(jax.random.uniform(seeds[8], (E, P_SIZE), jnp.float32, math.log(0.01), math.log(0.12))), 0.01, 0.12),
    }


def drift_step(density, source_sector, source_tile, matrix_id, cubic_weights):
    shaped = density.reshape(N_INNER, EB, P_SIZE, N_SECTOR, NT, TILE)

    def one_block(block):
        local = shaped[block]
        sources = source_sector[block]
        departing = local[:, :, sources, source_tile[block], :]
        matrices = cubic_weights[matrix_id[block]]
        return jnp.einsum("epstj,stij->epsti", departing, matrices, precision=lax.Precision.HIGHEST)

    moved = lax.map(one_block, jnp.arange(N_INNER, dtype=jnp.int32))
    return moved.reshape(E, P_SIZE, CELLS)


def one_pass(field, rate_cell, energy_rate, pitch_rate):
    flux_e = energy_rate[:-1, :, None] * (field[1:] - field[:-1])
    flux_p = pitch_rate[:, :-1, None] * (field[:, 1:] - field[:, :-1])
    change_e = jnp.pad(flux_e, ((0, 1), (0, 0), (0, 0))) - jnp.pad(flux_e, ((1, 0), (0, 0), (0, 0)))
    change_p = jnp.pad(flux_p, ((0, 0), (0, 1), (0, 0))) - jnp.pad(flux_p, ((0, 0), (1, 0), (0, 0)))
    return field + rate_cell[None, None, :] * (change_e + change_p)


def reference(density, source_sector, source_tile, matrix_id, cubic_weights, bin_cells, wave_level, energy_rate, pitch_rate):
    cell_total = NT * TILE
    bin_ends = jnp.cumsum(bin_cells, axis=1)
    positions = jnp.arange(cell_total, dtype=jnp.int32)
    bin_of = jnp.sum((bin_ends[:, None, :] <= positions[None, :, None]).astype(jnp.int32), axis=2).astype(jnp.int32)
    levels = jnp.take_along_axis(wave_level, bin_of, axis=1)
    first = drift_step(density, source_sector, source_tile, matrix_id, cubic_weights)
    per_sector = jnp.moveaxis(first.reshape(E, P_SIZE, N_SECTOR, cell_total), 2, 0)

    def diffuse_sector(inputs):
        field, rate_cell = inputs

        def loop_body(step, current):
            return one_pass(current, rate_cell, energy_rate, pitch_rate)

        return lax.fori_loop(0, PASSES, loop_body, field)

    diffused = lax.map(diffuse_sector, (per_sector, levels))
    diffused = jnp.moveaxis(diffused, 0, 2).reshape(E, P_SIZE, CELLS)
    return drift_step(diffused, source_sector, source_tile, matrix_id, cubic_weights)
```

```python
import functools

import jax
import jax.numpy as jnp
from jax import lax
from jax.experimental import pallas as pl
from jax.experimental.pallas import tpu as pltpu
from jax.sharding import PartitionSpec as P

PASSES = 12
CHUNKS = 4
VMEM_LIMIT = 58 * 1024 * 1024
ANY = pl.BlockSpec(memory_space=pl.ANY)
SMEM = pl.BlockSpec(memory_space=pltpu.SMEM)
VMEM = pl.BlockSpec(memory_space=pltpu.VMEM)
F32 = jnp.float32
BF16 = jnp.bfloat16


def params():
    return pltpu.CompilerParams(vmem_limit_bytes=VMEM_LIMIT)


def cost(flops, bytes_accessed):
    return pl.CostEstimate(flops=flops, bytes_accessed=bytes_accessed, transcendentals=0)


def weights_kernel(mid_ref, w_ref, out_ref, raw, sems):
    tiles, side = raw.shape[0], raw.shape[1]
    me = lax.axis_index("sector")

    def copy(t):
        return pltpu.make_async_copy(w_ref.at[mid_ref[0, me, t]], raw.at[t], sems.at[t])

    @pl.loop(0, tiles)
    def _(t):
        copy(t).start()

    @pl.loop(0, tiles)
    def _(t):
        copy(t).wait()
        turned = jnp.transpose(raw[t])
        high = turned.astype(BF16)
        low = (turned - high.astype(F32)).astype(BF16)
        out_ref[t, :side, :side] = high
        out_ref[t, side:, :side] = high
        out_ref[t, :side, side:] = low
        out_ref[t, side:, side:] = jnp.zeros((side, side), BF16)


def split_weights(matrix_id, cubic_weights):
    tiles, side = matrix_id.shape[2], cubic_weights.shape[1]
    return pl.pallas_call(
        weights_kernel,
        out_shape=jax.ShapeDtypeStruct((tiles, 2 * side, 2 * side), BF16),
        in_specs=[SMEM, ANY],
        out_specs=VMEM,
        scratch_shapes=[
            pltpu.VMEM((tiles, side, side), F32),
            pltpu.SemaphoreType.DMA((tiles,)),
        ],
        compiler_params=params(),
        cost_estimate=cost(tiles * side * side * 8, tiles * side * side * 12),
        name="split_weights",
    )(matrix_id, cubic_weights)


def pack_kernel(find, n_arrays, sec_ref, til_ref, *refs):
    sectors, tiles = sec_ref.shape[1], sec_ref.shape[2]
    sends, sems = refs[-sectors:-1], refs[-1]
    pieces = find(*refs[:n_arrays])
    me = lax.axis_index("sector")
    counts = []
    for d in range(1, sectors):
        dest = me ^ d

        def body(t, count, d=d, dest=dest):
            hit = sec_ref[0, dest, t] == me

            @pl.when(hit)
            def _():
                for guard, piece in pieces(til_ref[0, dest, t]):

                    @pl.when(guard)
                    def _():
                        pltpu.make_async_copy(piece(), sends[d - 1].at[count], sems.at[d - 1, count]).start()

            return count + hit.astype(jnp.int32)

        counts.append(lax.fori_loop(0, tiles, body, jnp.int32(0)))
    for d in range(1, sectors):

        @pl.loop(0, counts[d - 1])
        def _(slot, d=d):
            there = sends[d - 1].at[slot]
            pltpu.make_async_copy(there, there, sems.at[d - 1, slot]).wait()


def pack(find, cap, source_sector, source_tile, arrays, piece, after=()):
    sectors = source_sector.shape[1]
    send = jax.ShapeDtypeStruct((cap,) + piece, F32)
    size = 4 * cap * (sectors - 1) * piece[0] * piece[1] * piece[2]
    return pl.pallas_call(
        functools.partial(pack_kernel, find, len(arrays)),
        out_shape=[send] * (sectors - 1),
        in_specs=[SMEM, SMEM] + [ANY] * (len(arrays) + len(after)),
        out_specs=[ANY] * (sectors - 1),
        scratch_shapes=[pltpu.SemaphoreType.DMA((sectors - 1, cap))],
        compiler_params=params(),
        cost_estimate=cost(0, 2 * size),
        name="pack_tiles",
    )(source_sector, source_tile, *arrays, *after)


def sector_exchange(sends):
    sectors = lax.axis_size("sector")
    return [
        lax.ppermute(send, "sector", [(s, s ^ (d + 1)) for s in range(sectors)])
        for d, send in enumerate(sends)
    ]


def drift_kernel(find, place, n_local, sec_ref, til_ref, w_ref, *refs):
    sectors, tiles = sec_ref.shape[1], sec_ref.shape[2]
    local, recvs = refs[:n_local], refs[n_local : n_local + sectors - 1]
    outs = refs[n_local + sectors - 1 : -4]
    taken, made, in_sems, out_sems = refs[-4:]
    pieces = find(*local)
    put = place(*outs)
    me = lax.axis_index("sector")
    rows, side = taken.shape[1] * taken.shape[2], taken.shape[3]

    def fetch(t, counts):
        d = sec_ref[0, me, t] ^ me

        @pl.when(d == 0)
        def _():
            for guard, piece in pieces(til_ref[0, me, t]):

                @pl.when(guard)
                def _():
                    pltpu.make_async_copy(piece(), taken.at[t], in_sems.at[t]).start()

        for other in range(1, sectors):

            @pl.when(d == other)
            def _(other=other):
                pltpu.make_async_copy(
                    recvs[other - 1].at[counts[other - 1]], taken.at[t], in_sems.at[t]
                ).start()

        return tuple(c + (d == i + 1).astype(jnp.int32) for i, c in enumerate(counts))

    lax.fori_loop(0, tiles, fetch, (jnp.int32(0),) * (sectors - 1))

    @pl.loop(0, tiles)
    def _(t):
        pltpu.make_async_copy(taken.at[t], taken.at[t], in_sems.at[t]).wait()
        value = taken[t].reshape(rows, side)
        high = value.astype(BF16)
        low = (value - high.astype(F32)).astype(BF16)
        both = jnp.dot(jnp.concatenate([high, low], axis=1), w_ref[t], preferred_element_type=F32)
        made[t] = (both[:, :side] + both[:, side:]).reshape(taken.shape[1:])
        for guard, there in put(t):

            @pl.when(guard)
            def _():
                pltpu.make_async_copy(made.at[t], there(), out_sems.at[t]).start()

    @pl.loop(0, tiles)
    def _(t):
        pltpu.make_async_copy(made.at[t], made.at[t], out_sems.at[t]).wait()


def drift(find, place, tables, weights, local, recvs, outs, piece, carried=None):
    source_sector, source_tile = tables
    sectors, tiles = source_sector.shape[1], source_sector.shape[2]
    n_local = len(local)
    rows, side = piece[0] * piece[1], piece[2]
    ins = [source_sector, source_tile, weights, *local, *recvs]
    specs = [SMEM, SMEM, VMEM] + [ANY] * (n_local + sectors - 1)
    aliases = {}
    body = functools.partial(drift_kernel, find, place, n_local)
    if carried is not None:
        aliases = {len(ins): 0}
        ins.append(carried)
        specs.append(ANY)
        at = len(ins) - 1

        def body(*refs):
            drift_kernel(find, place, n_local, *refs[:at], *refs[at + 1 :])

    return pl.pallas_call(
        body,
        out_shape=outs,
        in_specs=specs,
        out_specs=[ANY] * len(outs),
        scratch_shapes=[
            pltpu.VMEM((tiles,) + piece, F32),
            pltpu.VMEM((tiles,) + piece, F32),
            pltpu.SemaphoreType.DMA((tiles,)),
            pltpu.SemaphoreType.DMA((tiles,)),
        ],
        input_output_aliases=aliases,
        compiler_params=params(),
        cost_estimate=cost(tiles * rows * side * side * 8, tiles * rows * side * 8 + weights.size * 2),
        name="drift_chunk",
    )(*ins)


def diffusion_kernel(
    chunks, halo_chunks, rate_ref, a_ref, b_ref, *refs
):
    n_in = 2 * chunks + 2 * halo_chunks
    ins, keep, sends = refs[:n_in], refs[n_in], refs[n_in + 1 : n_in + 1 + chunks]
    field, work, done, in_sems, out_sems = refs[n_in + 1 + chunks :]
    tiles, step = ins[0].shape[0], ins[0].shape[1]
    frame, pitches, side = work.shape
    halo = halo_chunks * step
    block = chunks * step
    vregs = pitches // 8
    flip = lax.axis_index("inner") % 2
    order = (
        list(range(chunks))
        + [2 * chunks - 1 - k for k in range(chunks)]
        + [2 * chunks + k for k in range(halo_chunks)]
        + [-1 - k for k in range(halo_chunks)]
    )

    def fetch(g, slot):
        copies = []
        for i, position in enumerate(order):
            straight = (position + halo_chunks) * step
            mirrored = (2 * chunks - 1 - position + halo_chunks) * step
            at = jnp.where(flip == 0, straight, mirrored)
            copies.append(
                pltpu.make_async_copy(
                    ins[i].at[g], field.at[slot, pl.ds(at, step)], in_sems.at[slot, i]
                )
            )
        return copies

    def store(g, slot):
        copies = [
            pltpu.make_async_copy(
                done.at[slot, pl.ds(flip * block, block)], keep.at[g], out_sems.at[slot, chunks]
            )
        ]
        for k in range(chunks):
            copies.append(
                pltpu.make_async_copy(
                    done.at[slot, pl.ds((1 - flip) * block + k * step, step)],
                    sends[k].at[g],
                    out_sems.at[slot, k],
                )
            )
        return copies

    for copy in fetch(0, 0):
        copy.start()

    @pl.loop(0, tiles)
    def _(g):
        slot = g % 2

        @pl.when(g + 1 < tiles)
        def _():
            for copy in fetch(g + 1, 1 - slot):
                copy.start()

        for copy in fetch(g, slot):
            copy.wait()

        @pl.when(g >= 2)
        def _():
            for copy in store(g - 2, slot):
                copy.wait()

        rate = rate_ref[g]

        def read_work(e):
            return [work[e, 8 * v : 8 * v + 8, :] for v in range(vregs)]

        def write_work(e, rows):
            for v in range(vregs):
                work[e, 8 * v : 8 * v + 8, :] = rows[v]

        def read_field(e):
            return [field[slot, e, pl.ds(v, 8, stride=vregs), :] for v in range(vregs)]

        def write_done(e, rows):
            for v in range(vregs):
                done[slot, e - halo, pl.ds(v, 8, stride=vregs), :] = rows[v]

        def sweep(first, count, read, write):
            def energy(e, here, below):
                after = read(e + 1)
                above = [
                    a_ref[e, 8 * v : 8 * v + 8, :] * (after[v] - here[v]) for v in range(vregs)
                ]
                nearby = here[1:] + [pltpu.roll(here[0], 7, 0)]
                pitch = [
                    b_ref[e, 8 * v : 8 * v + 8, :] * (nearby[v] - here[v]) for v in range(vregs)
                ]
                before = [pltpu.roll(pitch[-1], 1, 0)] + pitch[:-1]
                write(
                    e,
                    [
                        here[v] + rate * ((above[v] - below[v]) + (pitch[v] - before[v]))
                        for v in range(vregs)
                    ],
                )
                return after, above

            edge = read(first - 1)
            here = read(first)
            below = [
                a_ref[first - 1, 8 * v : 8 * v + 8, :] * (here[v] - edge[v]) for v in range(vregs)
            ]

            def two(i, carry):
                here, below = list(carry[:vregs]), list(carry[vregs:])
                e = first + 2 * i
                here, below = energy(e, here, below)
                here, below = energy(e + 1, here, below)
                return (*here, *below)

            lax.fori_loop(0, count // 2, two, (*here, *below))

        sweep(1, frame - 2, read_field, write_work)

        @pl.loop(1, PASSES - 1)
        def _(n):
            sweep(n + 1, frame - 2 - 2 * n, read_work, write_work)

        sweep(PASSES, frame - 2 * PASSES, read_work, write_done)

        for copy in store(g, slot):
            copy.start()

    for g in range(max(0, tiles - 2), tiles):
        for copy in store(g, g % 2):
            copy.wait()


def diffuse(rate, a, b, own, got, own_halo, got_halo):
    chunks, halo_chunks = len(own), len(own_halo)
    tiles, step, pitches, side = own[0].shape
    frame = a.shape[0]
    block = chunks * step
    n_in = 2 * (chunks + halo_chunks)
    keep = jax.ShapeDtypeStruct((tiles, block, pitches, side), F32)
    send = jax.ShapeDtypeStruct((tiles, step, pitches, side), F32)
    size = tiles * frame * pitches * side
    out = pl.pallas_call(
        functools.partial(diffusion_kernel, chunks, halo_chunks),
        out_shape=[keep] + [send] * chunks,
        in_specs=[VMEM] * 3 + [ANY] * n_in,
        out_specs=[ANY] * (1 + chunks),
        scratch_shapes=[
            pltpu.VMEM((2, frame, pitches, side), F32),
            pltpu.VMEM((frame, pitches, side), F32),
            pltpu.VMEM((2, 2 * block, pitches, side), F32),
            pltpu.SemaphoreType.DMA((2, n_in)),
            pltpu.SemaphoreType.DMA((2, chunks + 1)),
        ],
        compiler_params=params(),
        cost_estimate=cost(size * PASSES * 10, size * 8),
        name="diffuse_tiles",
    )(rate, a, b, *own, *got, *own_halo, *got_halo)
    return out[0], out[1:]


def across_lanes(window, side):
    frame, pitches = window.shape
    turned = window.reshape(frame, 8, pitches // 8).transpose(0, 2, 1).reshape(frame, pitches)
    return jnp.broadcast_to(turned[:, :, None], (frame, pitches, side))


def paired_shards(
    density,
    source_sector,
    source_tile,
    matrix_id,
    cubic_weights,
    bin_cells,
    wave_level,
    energy_rate,
    pitch_rate,
):
    sectors, inner = lax.axis_size("sector"), lax.axis_size("inner")
    inner_here = lax.axis_index("inner")
    flip, group = inner_here % 2, inner_here // 2
    block, pitches, cell_count = density.shape
    side = cubic_weights.shape[1]
    tiles = cell_count // side
    half = tiles // 2
    step = block // CHUNKS
    halo_chunks = PASSES // step
    cap = slots(tiles, sectors)
    tables = (source_sector, source_tile)
    piece = (step, pitches, side)
    part = jax.ShapeDtypeStruct((half,) + piece, F32)
    yes = None

    weights = split_weights(matrix_id, cubic_weights)

    def at_lanes(t):
        return pl.ds(pl.multiple_of(t * side, side), side)

    def side_here():
        return lax.axis_index("inner") % 2

    swap = [(i, i ^ 1) for i in range(inner)]
    own_pairs, got_pairs = [], []
    for i in range(inner):
        for pairs, shift in ((own_pairs, -2 if i % 2 == 0 else 2), (got_pairs, 2 if i % 2 == 0 else -2)):
            if 0 <= i + shift < inner:
                pairs.append((i, i + shift))

    own, got, own_halo, got_halo = [], [], [], []
    for k in range(CHUNKS):

        def find(field, k=k):
            here = side_here()
            first = here * (block - step * (k + 1)) + (1 - here) * (step * k)
            return lambda t: [(t >= 0, lambda: field.at[pl.ds(first, step), :, at_lanes(t)])]

        def place(kept, sent):
            here = side_here()
            mine = lambda t: (t // half) == here
            return lambda t: [
                (mine(t), lambda: kept.at[t % half]),
                (jnp.logical_not(mine(t)), lambda: sent.at[t % half]),
            ]

        after = own[k - 2 : k - 1] if k >= 2 else ()
        recvs = sector_exchange(pack(find, cap, *tables, [density], piece, after))
        kept, sent = drift(find, place, tables, weights, [density], recvs, [part, part], piece)
        swapped = lax.ppermute(sent, "inner", swap)
        own.append(kept)
        got.append(swapped)
        if k < halo_chunks:
            own_halo.append(lax.ppermute(kept, "inner", own_pairs))
            got_halo.append(lax.ppermute(swapped, "inner", got_pairs))

    energies = energy_rate.shape[0]
    frame = 2 * block + 2 * PASSES
    energy_pad = jnp.pad(energy_rate[: energies - 1], ((PASSES, PASSES + 1), (0, 0)))
    pitch_pad = jnp.pad(pitch_rate[:, : pitches - 1], ((PASSES, PASSES), (0, 1)))
    first_energy = group * 2 * block
    a = across_lanes(lax.dynamic_slice_in_dim(energy_pad, first_energy, frame, 0), side)
    b = across_lanes(lax.dynamic_slice_in_dim(pitch_pad, first_energy, frame, 0), side)
    bin_ends = jnp.cumsum(bin_cells[0])
    cells = flip * (half * side) + jnp.arange(half * side, dtype=jnp.int32)
    bin_of = jnp.sum((bin_ends[None, :] <= cells[:, None]).astype(jnp.int32), axis=1)
    bins = jnp.arange(bin_ends.shape[0], dtype=jnp.int32)
    level = jnp.sum(jnp.where(bin_of[:, None] == bins[None, :], wave_level[0][None, :], 0.0), axis=1)
    rate = jnp.broadcast_to(level.reshape(half, 1, side), (half, 8, side))

    kept, sends = diffuse(rate, a, b, own, got, own_halo, got_halo)

    outs, backs = [], []
    for k in range(CHUNKS):
        send = sends[k]
        if backs:
            send, backs[-1] = lax.optimization_barrier((send, backs[-1]))
        backs.append(lax.ppermute(send, "inner", swap))
    for k in range(CHUNKS):
        back = backs[k]

        def find(mine, theirs, k=k):
            here = side_here()
            return lambda t: [
                ((t // half) == here, lambda: mine.at[t % half, pl.ds(step * k, step)]),
                ((t // half) != here, lambda: theirs.at[t % half]),
            ]

        def place(result, k=k):
            return lambda t: [(t >= 0, lambda: result.at[pl.ds(step * k, step), :, at_lanes(t)])]

        recvs = sector_exchange(pack(find, cap, *tables, [kept, back], piece))
        whole = [jax.ShapeDtypeStruct(density.shape, F32)]
        carried = outs[-1] if outs else None
        outs += drift(find, place, tables, weights, [kept, back], recvs, whole, piece, carried)
    return outs[-1]


def slots(tiles, sectors):
    return max(2, (3 * tiles + 2 * sectors - 1) // (2 * sectors))


def order_within(sources):
    tile_count = sources.shape[1]
    same = sources[:, :, None] == sources[:, None, :]
    earlier = jnp.arange(tile_count)[None, :] < jnp.arange(tile_count)[:, None]
    return jnp.sum((same & earlier[None]).astype(jnp.int32), axis=2)


def drift_step(density, source_sector, source_tile, matrix_id, cubic_weights):
    sectors = lax.axis_size("sector")
    sector_here = lax.axis_index("sector")
    energies, pitches, cell_count = density.shape
    tile_len = cubic_weights.shape[1]
    tile_count = cell_count // tile_len
    slot_count = max(2, (3 * tile_count + 2 * sectors - 1) // (2 * sectors))
    sources = source_sector[0]
    picked_tiles = source_tile[0]
    matrix_ids = matrix_id[0]
    tile_ranks = order_within(sources)
    slot_rank = jnp.arange(slot_count, dtype=jnp.int32)
    matched = (sources[:, None, :] == sector_here) & (
        tile_ranks[:, None, :] == slot_rank[None, :, None]
    )
    chosen = jnp.sum(jnp.where(matched, picked_tiles[:, None, :], 0), axis=2).reshape(-1)
    filled = jnp.any(matched, axis=2).reshape(-1).astype(jnp.float32)
    blocks = density.reshape(energies, pitches, tile_count, tile_len)
    outgoing = jnp.take(blocks, chosen, axis=2) * filled[None, None, :, None]
    incoming = lax.all_to_all(outgoing, "sector", split_axis=2, concat_axis=2, tiled=True)
    own_sources = sources[sector_here]
    own_ranks = tile_ranks[sector_here]
    own_ids = matrix_ids[sector_here]
    where_from = own_sources * slot_count + own_ranks
    departing = jnp.take(incoming, where_from, axis=2)
    matrices = jnp.take(cubic_weights, own_ids, axis=0)
    drifted = jnp.einsum("eptj,tij->epti", departing, matrices, precision=lax.Precision.HIGHEST)
    return drifted.reshape(energies, pitches, cell_count)


def one_pass(field, rate_cell, energy_rate, pitch_rate):
    flux_e = energy_rate[:-1, :, None] * (field[1:] - field[:-1])
    flux_p = pitch_rate[:, :-1, None] * (field[:, 1:] - field[:, :-1])
    change_e = jnp.pad(flux_e, ((0, 1), (0, 0), (0, 0))) - jnp.pad(flux_e, ((1, 0), (0, 0), (0, 0)))
    change_p = jnp.pad(flux_p, ((0, 0), (0, 1), (0, 0))) - jnp.pad(flux_p, ((0, 0), (1, 0), (0, 0)))
    return field + rate_cell[None, None, :] * (change_e + change_p)


def shards(
    density,
    source_sector,
    source_tile,
    matrix_id,
    cubic_weights,
    bin_cells,
    wave_level,
    energy_rate,
    pitch_rate,
):
    first = drift_step(density, source_sector, source_tile, matrix_id, cubic_weights)
    inner_count = lax.axis_size("inner")
    inner_here = lax.axis_index("inner")
    cell_count = first.shape[2]
    lengths = bin_cells[0]
    per_device = cell_count // inner_count
    owner_cells = jnp.full((inner_count,), per_device, jnp.int32)
    owner_ends = jnp.cumsum(owner_cells)
    owner_starts = owner_ends - owner_cells
    offsets = jnp.arange(per_device, dtype=jnp.int32)
    cell_index = owner_starts[:, None] + offsets[None, :]
    valid = (offsets[None, :] < owner_cells[:, None]).reshape(-1).astype(jnp.float32)
    clipped = jnp.minimum(cell_index, cell_count - 1).reshape(-1)
    packed = jnp.take(first, clipped, axis=2) * valid[None, None, :]
    cellwise = lax.all_to_all(packed, "inner", split_axis=2, concat_axis=0, tiled=True)
    bin_ends = jnp.cumsum(lengths)
    global_cells = owner_starts[inner_here] + offsets
    is_live = (offsets < owner_cells[inner_here]).astype(jnp.float32)
    bin_of = jnp.sum((bin_ends[None, :] <= global_cells[:, None]).astype(jnp.int32), axis=1)
    onehot = bin_of[:, None] == jnp.arange(inner_count, dtype=jnp.int32)[None, :]
    cell_level = jnp.sum(jnp.where(onehot, wave_level[0][None, :], 0.0), axis=1) * is_live

    def loop_body(step, current):
        return one_pass(current, cell_level, energy_rate, pitch_rate)

    diffused = lax.fori_loop(0, PASSES, loop_body, cellwise)
    returned = lax.all_to_all(diffused, "inner", split_axis=0, concat_axis=2, tiled=True)
    every_cell = jnp.arange(cell_count, dtype=jnp.int32)
    owner_index = jnp.sum((owner_ends[None, :] <= every_cell[:, None]).astype(jnp.int32), axis=1)
    offset = every_cell - owner_starts[owner_index]
    position = owner_index * per_device + offset
    restored = jnp.take(returned, position, axis=2)
    return drift_step(restored, source_sector, source_tile, matrix_id, cubic_weights)


def pairs_fit(mesh, energies, pitches, cells, side):
    sectors, inner = mesh.shape["sector"], mesh.shape["inner"]
    block = energies // inner
    tiles = cells // sectors // side
    return (
        sectors & (sectors - 1) == 0
        and inner % 2 == 0
        and tiles % 2 == 0
        and pitches % 16 == 0
        and side % 128 == 0
        and block >= PASSES
        and block % CHUNKS == 0
        and PASSES % (block // CHUNKS) == 0
    )


def solution(mesh):
    specs = (
        P("inner", None, "sector"),
        P("inner", None, None),
        P("inner", None, None),
        P("inner", None, None),
        P(),
        P("sector", None),
        P("sector", None),
        P(),
        P(),
    )

    def whole(*arrays):
        energies, pitches, cells = arrays[0].shape
        fits = pairs_fit(mesh, energies, pitches, cells, arrays[4].shape[1])
        return jax.shard_map(
            paired_shards if fits else shards,
            mesh=mesh,
            in_specs=specs,
            out_specs=P("inner", None, "sector"),
            check_vma=False,
        )(*arrays)

    return whole
```

```python
import functools

import jax
import jax.numpy as jnp
from jax import lax
from jax.experimental import pallas as pl
from jax.experimental.pallas import tpu as pltpu
from jax.sharding import PartitionSpec as P

PASSES = 12
VMEM_LIMIT = 63 * 1024 * 1024
ANY = pl.BlockSpec(memory_space=pltpu.HBM)
SMEM = pl.BlockSpec(memory_space=pltpu.SMEM)
VMEM = pl.BlockSpec(memory_space=pltpu.VMEM)
F32 = jnp.float32
BF16 = jnp.bfloat16


def params():
    return pltpu.CompilerParams(vmem_limit_bytes=VMEM_LIMIT)


def cost():
    return pl.CostEstimate(flops=0, bytes_accessed=1024, transcendentals=0)


def weights_kernel(mid_ref, w_ref, out_ref, raw, sems):
    tiles, side = raw.shape[0], raw.shape[1]
    me = lax.axis_index("sector")

    def copy(t):
        return pltpu.make_async_copy(w_ref.at[mid_ref[0, me, t]], raw.at[t], sems.at[t])

    @pl.loop(0, tiles)
    def _(t):
        copy(t).start()

    @pl.loop(0, tiles)
    def _(t):
        copy(t).wait()
        turned = jnp.transpose(raw[t])
        high = turned.astype(BF16)
        low = (turned - high.astype(F32)).astype(BF16)
        out_ref[t, :side, :side] = high
        out_ref[t, side:, :side] = high
        out_ref[t, :side, side:] = low
        out_ref[t, side:, side:] = jnp.zeros((side, side), BF16)


def split_weights(matrix_id, cubic_weights):
    tiles, side = matrix_id.shape[2], cubic_weights.shape[1]
    return pl.pallas_call(
        weights_kernel,
        out_shape=jax.ShapeDtypeStruct((tiles, 2 * side, 2 * side), BF16),
        in_specs=[SMEM, ANY],
        out_specs=VMEM,
        scratch_shapes=[
            pltpu.VMEM((tiles, side, side), F32),
            pltpu.SemaphoreType.DMA((tiles,)),
        ],
        compiler_params=params(),
        cost_estimate=cost(),
        name="split_weights",
    )(matrix_id, cubic_weights)


def pack_kernel(find, n_arrays, offsets, sec_ref, til_ref, *refs):
    tiles, n = sec_ref.shape[2], len(offsets)
    sends, room, in_sems, out_sems = refs[-n - 3 : -3], *refs[-3:]
    pieces = find(*refs[:n_arrays])
    me = lax.axis_index("sector")
    counts = []
    for i, d in enumerate(offsets):
        dest = me ^ d

        def body(t, count, i=i, dest=dest):
            hit = sec_ref[0, dest, t] == me

            @pl.when(hit)
            def _():
                for guard, piece in pieces(til_ref[0, dest, t]):

                    @pl.when(guard)
                    def _():
                        pltpu.make_async_copy(piece(), room.at[i, count], in_sems.at[i, count]).start()

            return count + hit.astype(jnp.int32)

        counts.append(lax.fori_loop(0, tiles, body, jnp.int32(0)))
    for i in range(n):

        @pl.loop(0, counts[i])
        def _(slot, i=i):
            here = room.at[i, slot]
            pltpu.make_async_copy(here, here, in_sems.at[i, slot]).wait()
            pltpu.make_async_copy(here, sends[i].at[slot], out_sems.at[i, slot]).start()

    for i in range(n):

        @pl.loop(0, counts[i])
        def _(slot, i=i):
            here = room.at[i, slot]
            pltpu.make_async_copy(here, sends[i].at[slot], out_sems.at[i, slot]).wait()


def pack(find, offsets, cap, tables, arrays, piece, after=()):
    n = len(offsets)
    send = jax.ShapeDtypeStruct((cap,) + piece, F32)
    return pl.pallas_call(
        functools.partial(pack_kernel, find, len(arrays), tuple(offsets)),
        out_shape=[send] * n,
        in_specs=[SMEM, SMEM] + [ANY] * (len(arrays) + len(after)),
        out_specs=[ANY] * n,
        scratch_shapes=[
            pltpu.VMEM((n, cap) + piece, F32),
            pltpu.SemaphoreType.DMA((n, cap)),
            pltpu.SemaphoreType.DMA((n, cap)),
        ],
        compiler_params=params(),
        cost_estimate=cost(),
        name="pack_tiles",
    )(*tables, *arrays, *after)


def sector_exchange(sends, offsets):
    sectors = lax.axis_size("sector")
    return [
        lax.ppermute(send, "sector", [(s, s ^ d) for s in range(sectors)])
        for d, send in zip(offsets, sends)
    ]


def in_turn(later, earlier):
    both = lax.optimization_barrier((*later, *earlier))
    return list(both[: len(later)]), list(both[len(later) :])


def drift_kernel(find, place, receive, n_local, n_extra, sec_ref, til_ref, w_ref, *refs):
    sectors, tiles = sec_ref.shape[1], sec_ref.shape[2]
    local, recvs = refs[:n_local], refs[n_local : n_local + sectors - 1]
    outs = refs[n_local + sectors - 1 + n_extra : -5]
    token, taken, made, in_sems, out_sems = refs[-5:]
    pieces = find(*local)
    put = place(*outs)
    me = lax.axis_index("sector")
    rows, side = taken.shape[1] * taken.shape[2], taken.shape[3]
    token[...] = jnp.zeros(token.shape, F32)

    def fetch(t, counts):
        d = sec_ref[0, me, t] ^ me

        @pl.when(d == 0)
        def _():
            for guard, piece in pieces(til_ref[0, me, t]):

                @pl.when(guard)
                def _():
                    pltpu.make_async_copy(piece(), taken.at[t], in_sems.at[t]).start()

        for other in range(1, sectors):

            @pl.when(d == other)
            def _(other=other):
                came = receive(recvs[other - 1], other, counts[other - 1])
                pltpu.make_async_copy(came, taken.at[t], in_sems.at[t]).start()

        return tuple(c + (d == i + 1).astype(jnp.int32) for i, c in enumerate(counts))

    lax.fori_loop(0, tiles, fetch, (jnp.int32(0),) * (sectors - 1))

    @pl.loop(0, tiles)
    def _(t):
        pltpu.make_async_copy(taken.at[t], taken.at[t], in_sems.at[t]).wait()
        value = taken[t].reshape(rows, side)
        high = value.astype(BF16)
        low = (value - high.astype(F32)).astype(BF16)
        both = jnp.dot(jnp.concatenate([high, low], axis=1), w_ref[t], preferred_element_type=F32)
        made[t] = (both[:, :side] + both[:, side:]).reshape(taken.shape[1:])
        for guard, there in put(t):

            @pl.when(guard)
            def _():
                pltpu.make_async_copy(made.at[t], there(), out_sems.at[t]).start()

    @pl.loop(0, tiles)
    def _(t):
        pltpu.make_async_copy(made.at[t], made.at[t], out_sems.at[t]).wait()


def drift(find, place, receive, tables, weights, local, recvs, outs, piece, carried=()):
    sectors, tiles = tables[0].shape[1], tables[0].shape[2]
    n_local = len(local)
    ins = [*tables, weights, *local, *recvs, *carried]
    return pl.pallas_call(
        functools.partial(drift_kernel, find, place, receive, n_local, len(carried)),
        out_shape=[*outs, jax.ShapeDtypeStruct((8, 128), F32)],
        in_specs=[SMEM, SMEM, VMEM] + [ANY] * (len(ins) - 3),
        out_specs=[ANY] * len(outs) + [VMEM],
        scratch_shapes=[
            pltpu.VMEM((tiles,) + piece, F32),
            pltpu.VMEM((tiles,) + piece, F32),
            pltpu.SemaphoreType.DMA((tiles,)),
            pltpu.SemaphoreType.DMA((tiles,)),
        ],
        input_output_aliases={len(ins) - 1: 0} if carried else {},
        compiler_params=params(),
        cost_estimate=cost(),
        name="drift_chunk",
    )(*ins)


def diffusion_kernel(n_own, n_halo, n_send, rate_ref, a_ref, b_ref, *refs):
    n_in = 2 * n_own + 2 * n_halo
    ins, keep, sends = refs[:n_in], refs[n_in], refs[n_in + 1 : n_in + 1 + n_send]
    field, work, ra_ref, rb_ref, done, in_sems, out_sems = refs[n_in + 1 + n_send :]
    tiles, block = keep.shape[0], keep.shape[1]
    frame, pitches, side = work.shape
    halo = (frame - 2 * block) // 2
    vregs = pitches // 8
    flip = lax.axis_index("inner") % 2
    places, start = [], 0
    for i in range(n_own):
        step = ins[i].shape[1]
        places.append((i, step, halo + start))
        places.append((n_own + i, step, halo + 2 * block - start - step))
        if i < n_halo:
            places.append((2 * n_own + i, step, halo + 2 * block + start))
            places.append((2 * n_own + n_halo + i, step, halo - start - step))
        start += step

    def fetch(g, slot):
        copies = []
        for i, step, place in places:
            at = jnp.where(flip == 0, place, frame - place - step)
            copies.append(
                pltpu.make_async_copy(
                    ins[i].at[g], field.at[slot, pl.ds(at, step)], in_sems.at[slot, i]
                )
            )
        return copies

    def store(g, slot):
        copies = [
            pltpu.make_async_copy(
                done.at[slot, pl.ds(flip * block, block)], keep.at[g], out_sems.at[slot, n_send]
            )
        ]
        first = (1 - flip) * block
        for k in range(n_send):
            step = sends[k].shape[1]
            copies.append(
                pltpu.make_async_copy(
                    done.at[slot, pl.ds(first, step)], sends[k].at[g], out_sems.at[slot, k]
                )
            )
            first = first + step
        return copies

    for copy in fetch(0, 0):
        copy.start()

    @pl.loop(0, tiles)
    def _(g):
        slot = g % 2

        @pl.when(g + 1 < tiles)
        def _():
            for copy in fetch(g + 1, 1 - slot):
                copy.start()

        for copy in fetch(g, slot):
            copy.wait()

        @pl.when(g >= 2)
        def _():
            for copy in store(g - 2, slot):
                copy.wait()

        rate = rate_ref[g]

        def rows_of(ref, e):
            return [ref[e, 8 * v : 8 * v + 8, :] for v in range(vregs)]

        def write_work(e, rows):
            for v in range(vregs):
                work[e, 8 * v : 8 * v + 8, :] = rows[v]

        def read_work(e):
            return rows_of(work, e)

        def read_field(e):
            return [field[slot, e, pl.ds(v, 8, stride=vregs), :] for v in range(vregs)]

        def write_done(e, rows):
            for v in range(vregs):
                done[slot, e - halo, pl.ds(v, 8, stride=vregs), :] = rows[v]

        def scaled(e):
            ra = [rate * x for x in rows_of(a_ref, e)]
            rb = [rate * x for x in rows_of(b_ref, e)]
            for v in range(vregs):
                ra_ref[e, 8 * v : 8 * v + 8, :] = ra[v]
                rb_ref[e, 8 * v : 8 * v + 8, :] = rb[v]
            return ra, rb

        def ready(e):
            return rows_of(ra_ref, e), rows_of(rb_ref, e)

        def sweep(first, count, read, write, rates, wide):
            def energy(e, here, below):
                after = read(e + 1)
                ra, rb = rates(e)
                above = [ra[v] * (after[v] - here[v]) for v in range(vregs)]
                nearby = here[1:] + [pltpu.roll(here[0], 7, 0)]
                pitch = [rb[v] * (nearby[v] - here[v]) for v in range(vregs)]
                before = [pltpu.roll(pitch[-1], 1, 0)] + pitch[:-1]
                write(
                    e,
                    [
                        here[v] + ((above[v] - below[v]) + (pitch[v] - before[v]))
                        for v in range(vregs)
                    ],
                )
                return after, above

            def several(e, carry, n):
                here, below = list(carry[:vregs]), list(carry[vregs:])
                for i in range(n):
                    here, below = energy(e + i, here, below)
                return (*here, *below)

            edge = read(first - 1)
            here = read(first)
            ra = rates(first - 1)[0]
            below = [ra[v] * (here[v] - edge[v]) for v in range(vregs)]
            carry = lax.fori_loop(
                0,
                count // wide,
                lambda i, carry: several(first + wide * i, carry, wide),
                (*here, *below),
            )
            for left in range(2, wide, 2):

                @pl.when(count % wide == left)
                def _(left=left):
                    several(first + count - left, carry, left)

        sweep(1, frame - 2, read_field, write_work, scaled, 2)

        @pl.loop(1, PASSES - 1)
        def _(n):
            sweep(n + 1, frame - 2 - 2 * n, read_work, write_work, ready, 4)

        sweep(PASSES, frame - 2 * PASSES, read_work, write_done, ready, 4)

        for copy in store(g, slot):
            copy.start()

    for g in range(max(0, tiles - 2), tiles):
        for copy in store(g, g % 2):
            copy.wait()


def diffuse(rate, a, b, own, got, own_halo, got_halo, steps):
    tiles, _, pitches, side = own[0].shape
    frame = a.shape[0]
    block = sum(steps)
    ins = [*own, *got, *own_halo, *got_halo]
    out = pl.pallas_call(
        functools.partial(diffusion_kernel, len(own), len(own_halo), len(steps)),
        out_shape=[
            jax.ShapeDtypeStruct((tiles, step, pitches, side), F32) for step in (block, *steps)
        ],
        in_specs=[VMEM] * 3 + [ANY] * len(ins),
        out_specs=[ANY] * (1 + len(steps)),
        scratch_shapes=[
            pltpu.VMEM((2, frame, pitches, side), F32),
            pltpu.VMEM((frame, pitches, side), F32),
            pltpu.VMEM((frame, pitches, side), F32),
            pltpu.VMEM((frame, pitches, side), F32),
            pltpu.VMEM((2, 2 * block, pitches, side), F32),
            pltpu.SemaphoreType.DMA((2, len(ins))),
            pltpu.SemaphoreType.DMA((2, len(steps) + 1)),
        ],
        compiler_params=params(),
        cost_estimate=cost(),
        name="diffuse_tiles",
    )(rate, a, b, *ins)
    return out[0], out[1:]


def across_lanes(window, side):
    frame, pitches = window.shape
    turned = window.reshape(frame, 8, pitches // 8).transpose(0, 2, 1).reshape(frame, pitches)
    return jnp.broadcast_to(turned[:, :, None], (frame, pitches, side))


def paired_shards(
    density,
    source_sector,
    source_tile,
    matrix_id,
    cubic_weights,
    bin_cells,
    wave_level,
    energy_rate,
    pitch_rate,
):
    sectors, inner = lax.axis_size("sector"), lax.axis_size("inner")
    inner_here = lax.axis_index("inner")
    flip, group = inner_here % 2, inner_here // 2
    block, pitches, cell_count = density.shape
    side = cubic_weights.shape[1]
    tiles = cell_count // side
    half = tiles // 2
    quarter = block // 4
    halo_chunks = PASSES // quarter
    first_steps = (quarter,) * 4
    last_steps = (quarter // 2, quarter - quarter // 4, quarter, quarter, quarter - quarter // 4)
    cap = slots(tiles, sectors)
    tables = (source_sector, source_tile)
    near, far = [1], list(range(2, sectors))

    weights = split_weights(matrix_id, cubic_weights)

    def at_lanes(t):
        return pl.ds(pl.multiple_of(t * side, side), side)

    def side_here():
        return lax.axis_index("inner") % 2

    swap = [(i, i ^ 1) for i in range(inner)]
    own_pairs, got_pairs = [], []
    for i in range(inner):
        for pairs, shift in ((own_pairs, -2 if i % 2 == 0 else 2), (got_pairs, 2 if i % 2 == 0 else -2)):
            if 0 <= i + shift < inner:
                pairs.append((i, i + shift))

    own, got, own_halo, got_halo = [], [], [], []
    packed = []
    start = 0
    for k, step in enumerate(first_steps):

        def first_of(start=start, step=step):
            here = side_here()
            return here * (block - start - step) + (1 - here) * start

        def find(field, first_of=first_of, step=step):
            first = first_of()
            return lambda t: [(t >= 0, lambda: field.at[pl.ds(first, step), :, at_lanes(t)])]

        def find_all(field):
            return lambda t: [(t >= 0, lambda: field.at[:, :, at_lanes(t)])]

        def receive(came, other, slot, first_of=first_of, step=step):
            return came.at[slot, pl.ds(first_of(), step)] if other == 1 else came.at[slot]

        def place(kept, sent):
            here = side_here()
            mine = lambda t: (t // half) == here
            return lambda t: [
                (mine(t), lambda: kept.at[t % half]),
                (jnp.logical_not(mine(t)), lambda: sent.at[t % half]),
            ]

        packed.append((start, step, find, receive, place))
        start += step

    def pack_first(k, after):
        start, step, find, _, _ = packed[k]
        return pack(find, far, cap, tables, [density], (step, pitches, side), after)

    sends = pack_first(0, ())
    recvs = sector_exchange(sends, far)
    beside = pack(find_all, near, cap, tables, [density], (block, pitches, side), (sends[0],))
    beside = sector_exchange(beside, near)
    token = sends[0]
    crossing = []
    for k, (start, step, find, receive, place) in enumerate(packed):
        if k + 1 < len(packed):
            later = pack_first(k + 1, (token,))
            later, recvs = in_turn(later, recvs)
            coming = sector_exchange(later, far)
        if k >= 2:
            recvs, _ = in_turn(recvs, crossing[k - 2])
        part = jax.ShapeDtypeStruct((half, step, pitches, side), F32)
        piece = (step, pitches, side)
        kept, sent, token = drift(
            find, place, receive, tables, weights, [density], beside + recvs, [part, part], piece
        )
        recvs = coming
        own.append(kept)
        got.append(lax.ppermute(sent, "inner", swap))
        crossing.append(got[-1:])
        if k < halo_chunks:
            own_halo.append(lax.ppermute(kept, "inner", own_pairs))
            crossing[-1] += own_halo[-1:]
        if 0 < k <= halo_chunks:
            got_halo.append(lax.ppermute(got[k - 1], "inner", got_pairs))
            crossing[-1] += got_halo[-1:]

    energies = energy_rate.shape[0]
    frame = 2 * block + 2 * PASSES
    energy_pad = jnp.pad(energy_rate[: energies - 1], ((PASSES, PASSES + 1), (0, 0)))
    pitch_pad = jnp.pad(pitch_rate[:, : pitches - 1], ((PASSES, PASSES), (0, 1)))
    first_energy = group * 2 * block
    a = across_lanes(lax.dynamic_slice_in_dim(energy_pad, first_energy, frame, 0), side)
    b = across_lanes(lax.dynamic_slice_in_dim(pitch_pad, first_energy, frame, 0), side)
    bin_ends = jnp.cumsum(bin_cells[0])
    cells = flip * (half * side) + jnp.arange(half * side, dtype=jnp.int32)
    bin_of = jnp.sum((bin_ends[None, :] <= cells[:, None]).astype(jnp.int32), axis=1)
    bins = jnp.arange(bin_ends.shape[0], dtype=jnp.int32)
    level = jnp.sum(jnp.where(bin_of[:, None] == bins[None, :], wave_level[0][None, :], 0.0), axis=1)
    rate = jnp.broadcast_to(level.reshape(half, 1, side), (half, 8, side))

    kept, sends = diffuse(rate, a, b, own, got, own_halo, got_halo, last_steps)

    returns, ready, out, start = sends, [], (), 0
    for k, step in enumerate(last_steps):

        def find(mine, theirs, start=start, step=step):
            here = side_here()
            return lambda t: [
                ((t // half) == here, lambda: mine.at[t % half, pl.ds(start, step)]),
                ((t // half) != here, lambda: theirs.at[t % half]),
            ]

        def place(result, start=start, step=step):
            return lambda t: [(t >= 0, lambda: result.at[pl.ds(start, step), :, at_lanes(t)])]

        ready.append((find, place, (step, pitches, side)))
        start += step

    def receive_slot(came, other, slot):
        return came.at[slot]

    def pack_last(k, after):
        find, _, piece = ready[k]
        sends = pack(find, near + far, cap, tables, [kept, backs[k]], piece, after)
        return sends[:1], sends[1:]

    whole = [jax.ShapeDtypeStruct(density.shape, F32)]
    backs = [lax.ppermute(returns[0], "inner", swap)]
    (last,), _ = in_turn([returns[1]], [backs[0]])
    backs.append(lax.ppermute(last, "inner", swap))
    sends, far_sends = pack_last(0, ())
    recvs = sector_exchange(far_sends, far)
    beside = sector_exchange(sends, near)
    token = kept
    for k, (find, place, piece) in enumerate(ready):
        if k + 1 < len(ready):
            sends, far_sends = pack_last(k + 1, (token,))
            far_sends, recvs = in_turn(far_sends, recvs)
            coming = sector_exchange(far_sends, far), sector_exchange(sends, near)
        if k + 2 < len(ready):
            (last,), _ = in_turn([returns[k + 2]], [backs[k + 1], *recvs])
            backs.append(lax.ppermute(last, "inner", swap))
        *out, token = drift(
            find, place, receive_slot, tables, weights, [kept, backs[k]], beside + recvs, whole, piece, out
        )
        recvs, beside = coming
    return out[0]


def slots(tiles, sectors):
    return max(2, (3 * tiles + 2 * sectors - 1) // (2 * sectors))


def order_within(sources):
    tile_count = sources.shape[1]
    same = sources[:, :, None] == sources[:, None, :]
    earlier = jnp.arange(tile_count)[None, :] < jnp.arange(tile_count)[:, None]
    return jnp.sum((same & earlier[None]).astype(jnp.int32), axis=2)


def drift_step(density, source_sector, source_tile, matrix_id, cubic_weights):
    sectors = lax.axis_size("sector")
    sector_here = lax.axis_index("sector")
    energies, pitches, cell_count = density.shape
    tile_len = cubic_weights.shape[1]
    tile_count = cell_count // tile_len
    slot_count = max(2, (3 * tile_count + 2 * sectors - 1) // (2 * sectors))
    sources = source_sector[0]
    picked_tiles = source_tile[0]
    matrix_ids = matrix_id[0]
    tile_ranks = order_within(sources)
    slot_rank = jnp.arange(slot_count, dtype=jnp.int32)
    matched = (sources[:, None, :] == sector_here) & (
        tile_ranks[:, None, :] == slot_rank[None, :, None]
    )
    chosen = jnp.sum(jnp.where(matched, picked_tiles[:, None, :], 0), axis=2).reshape(-1)
    filled = jnp.any(matched, axis=2).reshape(-1).astype(jnp.float32)
    blocks = density.reshape(energies, pitches, tile_count, tile_len)
    outgoing = jnp.take(blocks, chosen, axis=2) * filled[None, None, :, None]
    incoming = lax.all_to_all(outgoing, "sector", split_axis=2, concat_axis=2, tiled=True)
    own_sources = sources[sector_here]
    own_ranks = tile_ranks[sector_here]
    own_ids = matrix_ids[sector_here]
    where_from = own_sources * slot_count + own_ranks
    departing = jnp.take(incoming, where_from, axis=2)
    matrices = jnp.take(cubic_weights, own_ids, axis=0)
    drifted = jnp.einsum("eptj,tij->epti", departing, matrices, precision=lax.Precision.HIGHEST)
    return drifted.reshape(energies, pitches, cell_count)


def one_pass(field, rate_cell, energy_rate, pitch_rate):
    flux_e = energy_rate[:-1, :, None] * (field[1:] - field[:-1])
    flux_p = pitch_rate[:, :-1, None] * (field[:, 1:] - field[:, :-1])
    change_e = jnp.pad(flux_e, ((0, 1), (0, 0), (0, 0))) - jnp.pad(flux_e, ((1, 0), (0, 0), (0, 0)))
    change_p = jnp.pad(flux_p, ((0, 0), (0, 1), (0, 0))) - jnp.pad(flux_p, ((0, 0), (1, 0), (0, 0)))
    return field + rate_cell[None, None, :] * (change_e + change_p)


def shards(
    density,
    source_sector,
    source_tile,
    matrix_id,
    cubic_weights,
    bin_cells,
    wave_level,
    energy_rate,
    pitch_rate,
):
    first = drift_step(density, source_sector, source_tile, matrix_id, cubic_weights)
    inner_count = lax.axis_size("inner")
    inner_here = lax.axis_index("inner")
    cell_count = first.shape[2]
    lengths = bin_cells[0]
    per_device = cell_count // inner_count
    owner_cells = jnp.full((inner_count,), per_device, jnp.int32)
    owner_ends = jnp.cumsum(owner_cells)
    owner_starts = owner_ends - owner_cells
    offsets = jnp.arange(per_device, dtype=jnp.int32)
    cell_index = owner_starts[:, None] + offsets[None, :]
    valid = (offsets[None, :] < owner_cells[:, None]).reshape(-1).astype(jnp.float32)
    clipped = jnp.minimum(cell_index, cell_count - 1).reshape(-1)
    packed = jnp.take(first, clipped, axis=2) * valid[None, None, :]
    cellwise = lax.all_to_all(packed, "inner", split_axis=2, concat_axis=0, tiled=True)
    bin_ends = jnp.cumsum(lengths)
    global_cells = owner_starts[inner_here] + offsets
    is_live = (offsets < owner_cells[inner_here]).astype(jnp.float32)
    bin_of = jnp.sum((bin_ends[None, :] <= global_cells[:, None]).astype(jnp.int32), axis=1)
    onehot = bin_of[:, None] == jnp.arange(inner_count, dtype=jnp.int32)[None, :]
    cell_level = jnp.sum(jnp.where(onehot, wave_level[0][None, :], 0.0), axis=1) * is_live

    def loop_body(step, current):
        return one_pass(current, cell_level, energy_rate, pitch_rate)

    diffused = lax.fori_loop(0, PASSES, loop_body, cellwise)
    returned = lax.all_to_all(diffused, "inner", split_axis=0, concat_axis=2, tiled=True)
    every_cell = jnp.arange(cell_count, dtype=jnp.int32)
    owner_index = jnp.sum((owner_ends[None, :] <= every_cell[:, None]).astype(jnp.int32), axis=1)
    offset = every_cell - owner_starts[owner_index]
    position = owner_index * per_device + offset
    restored = jnp.take(returned, position, axis=2)
    return drift_step(restored, source_sector, source_tile, matrix_id, cubic_weights)


def pairs_fit(mesh, energies, pitches, cells, side):
    sectors, inner = mesh.shape["sector"], mesh.shape["inner"]
    block = energies // inner
    tiles = cells // sectors // side
    return (
        sectors & (sectors - 1) == 0
        and inner % 2 == 0
        and tiles % 2 == 0
        and pitches % 16 == 0
        and side % 128 == 0
        and block % 16 == 0
        and 4 * PASSES == 3 * block
    )


def solution(mesh):
    specs = (
        P("inner", None, "sector"),
        P("inner", None, None),
        P("inner", None, None),
        P("inner", None, None),
        P(),
        P("sector", None),
        P("sector", None),
        P(),
        P(),
    )

    def whole(*arrays):
        energies, pitches, cells = arrays[0].shape
        fits = pairs_fit(mesh, energies, pitches, cells, arrays[4].shape[1])
        return jax.shard_map(
            paired_shards if fits else shards,
            mesh=mesh,
            in_specs=specs,
            out_specs=P("inner", None, "sector"),
            check_vma=False,
        )(*arrays)

    return whole
```

```python
import functools

import jax
import jax.numpy as jnp
from jax import lax
from jax.experimental import pallas as pl
from jax.experimental.pallas import tpu as pltpu
from jax.sharding import PartitionSpec as P

PASSES = 12
VMEM_LIMIT = 64 * 1024 * 1024 - 128 * 1024
ANY = pl.BlockSpec(memory_space=pltpu.HBM)
SMEM = pl.BlockSpec(memory_space=pltpu.SMEM)
VMEM = pl.BlockSpec(memory_space=pltpu.VMEM)
F32 = jnp.float32
BF16 = jnp.bfloat16


def params():
    return pltpu.CompilerParams(vmem_limit_bytes=VMEM_LIMIT)


def cost():
    return pl.CostEstimate(flops=0, bytes_accessed=1024, transcendentals=0)


def weights_kernel(mid_ref, w_ref, out_ref, raw, sems):
    tiles, side = raw.shape[0], raw.shape[1]
    me = lax.axis_index("sector")

    def copy(t):
        return pltpu.make_async_copy(w_ref.at[mid_ref[0, me, t]], raw.at[t], sems.at[t])

    @pl.loop(0, tiles)
    def _(t):
        copy(t).start()

    @pl.loop(0, tiles)
    def _(t):
        copy(t).wait()
        turned = jnp.transpose(raw[t])
        high = turned.astype(BF16)
        low = (turned - high.astype(F32)).astype(BF16)
        out_ref[t, :side, :side] = high
        out_ref[t, side:, :side] = high
        out_ref[t, :side, side:] = low
        out_ref[t, side:, side:] = jnp.zeros((side, side), BF16)


def split_weights(matrix_id, cubic_weights):
    tiles, side = matrix_id.shape[2], cubic_weights.shape[1]
    return pl.pallas_call(
        weights_kernel,
        out_shape=jax.ShapeDtypeStruct((tiles, 2 * side, 2 * side), BF16),
        in_specs=[SMEM, ANY],
        out_specs=VMEM,
        scratch_shapes=[
            pltpu.VMEM((tiles, side, side), F32),
            pltpu.SemaphoreType.DMA((tiles,)),
        ],
        compiler_params=params(),
        cost_estimate=cost(),
        name="split_weights",
    )(matrix_id, cubic_weights)


def pack_kernel(offsets, finds, n_arrays, sec_ref, til_ref, *refs):
    tiles, n = sec_ref.shape[2], len(offsets)
    sends, rooms = refs[-2 * n - 2 : -n - 2], refs[-n - 2 : -2]
    in_sems, out_sems = refs[-2:]
    me = lax.axis_index("sector")
    counts = []
    for i, d in enumerate(offsets):
        dest = me ^ d
        pieces = finds[i](*refs[:n_arrays])

        def body(t, count, i=i, dest=dest, pieces=pieces):
            hit = sec_ref[0, dest, t] == me

            @pl.when(hit)
            def _():
                for guard, piece in pieces(til_ref[0, dest, t]):

                    @pl.when(guard)
                    def _():
                        pltpu.make_async_copy(piece(), rooms[i].at[count], in_sems.at[i, count]).start()

            return count + hit.astype(jnp.int32)

        counts.append(lax.fori_loop(0, tiles, body, jnp.int32(0)))
    for i in range(n):

        @pl.loop(0, counts[i])
        def _(slot, i=i):
            here = rooms[i].at[slot]
            pltpu.make_async_copy(here, here, in_sems.at[i, slot]).wait()
            pltpu.make_async_copy(here, sends[i].at[slot], out_sems.at[i, slot]).start()

    for i in range(n):

        @pl.loop(0, counts[i])
        def _(slot, i=i):
            pltpu.make_async_copy(rooms[i].at[slot], sends[i].at[slot], out_sems.at[i, slot]).wait()


def pack(groups, cap, tables, arrays, after=()):
    n = len(groups)
    offsets, finds, shapes = zip(*groups)
    return pl.pallas_call(
        functools.partial(pack_kernel, offsets, finds, len(arrays)),
        out_shape=[jax.ShapeDtypeStruct((cap,) + shape, F32) for shape in shapes],
        in_specs=[SMEM, SMEM] + [ANY] * (len(arrays) + len(after)),
        out_specs=[ANY] * n,
        scratch_shapes=[
            *[pltpu.VMEM((cap,) + shape, F32) for shape in shapes],
            pltpu.SemaphoreType.DMA((n, cap)),
            pltpu.SemaphoreType.DMA((n, cap)),
        ],
        compiler_params=params(),
        cost_estimate=cost(),
        name="pack_tiles",
    )(*tables, *arrays, *after)


def sector_exchange(sends, offsets):
    sectors = lax.axis_size("sector")
    return [
        lax.ppermute(send, "sector", [(s, s ^ d) for s in range(sectors)])
        for d, send in zip(offsets, sends)
    ]


def in_turn(later, earlier):
    both = lax.optimization_barrier((*later, *earlier))
    return list(both[: len(later)]), list(both[len(later) :])


def drift_kernel(find, place, receive, n_local, n_extra, sec_ref, til_ref, w_ref, *refs):
    sectors, tiles = sec_ref.shape[1], sec_ref.shape[2]
    local, recvs = refs[:n_local], refs[n_local : n_local + sectors - 1]
    outs = refs[n_local + sectors - 1 + n_extra : -5]
    token, taken, made, in_sems, out_sems = refs[-5:]
    pieces = find(*local)
    put = place(*outs)
    me = lax.axis_index("sector")
    rows, side = taken.shape[1] * taken.shape[2], taken.shape[3]
    token[...] = jnp.zeros(token.shape, F32)

    def fetch(t, counts):
        d = sec_ref[0, me, t] ^ me

        @pl.when(d == 0)
        def _():
            for guard, piece in pieces(til_ref[0, me, t]):

                @pl.when(guard)
                def _():
                    pltpu.make_async_copy(piece(), taken.at[t], in_sems.at[t]).start()

        for other in range(1, sectors):

            @pl.when(d == other)
            def _(other=other):
                came = receive(recvs[other - 1], other, counts[other - 1])
                pltpu.make_async_copy(came, taken.at[t], in_sems.at[t]).start()

        return tuple(c + (d == i + 1).astype(jnp.int32) for i, c in enumerate(counts))

    lax.fori_loop(0, tiles, fetch, (jnp.int32(0),) * (sectors - 1))

    @pl.loop(0, tiles)
    def _(t):
        pltpu.make_async_copy(taken.at[t], taken.at[t], in_sems.at[t]).wait()
        value = taken[t].reshape(rows, side)
        high = value.astype(BF16)
        low = (value - high.astype(F32)).astype(BF16)
        both = jnp.dot(jnp.concatenate([high, low], axis=1), w_ref[t], preferred_element_type=F32)
        made[t] = (both[:, :side] + both[:, side:]).reshape(taken.shape[1:])
        for guard, there in put(t):

            @pl.when(guard)
            def _():
                pltpu.make_async_copy(made.at[t], there(), out_sems.at[t]).start()

    @pl.loop(0, tiles)
    def _(t):
        pltpu.make_async_copy(made.at[t], made.at[t], out_sems.at[t]).wait()


def drift(find, place, receive, tables, weights, local, recvs, outs, piece, after=(), carried=()):
    sectors, tiles = tables[0].shape[1], tables[0].shape[2]
    n_local = len(local)
    ins = [*tables, weights, *local, *recvs, *after, *carried]
    n_extra = len(after) + len(carried)
    return pl.pallas_call(
        functools.partial(drift_kernel, find, place, receive, n_local, n_extra),
        out_shape=[*outs, jax.ShapeDtypeStruct((8, 128), F32)],
        in_specs=[SMEM, SMEM, VMEM] + [ANY] * (len(ins) - 3),
        out_specs=[ANY] * len(outs) + [VMEM],
        scratch_shapes=[
            pltpu.VMEM((tiles,) + piece, F32),
            pltpu.VMEM((tiles,) + piece, F32),
            pltpu.SemaphoreType.DMA((tiles,)),
            pltpu.SemaphoreType.DMA((tiles,)),
        ],
        input_output_aliases={len(ins) - 1: 0} if carried else {},
        compiler_params=params(),
        cost_estimate=cost(),
        name="drift_chunk",
    )(*ins)


def diffusion_kernel(n_own, n_halo, n_send, rate_ref, a_ref, b_ref, *refs):
    n_in = 2 * n_own + 2 * n_halo
    ins, keep, sends = refs[:n_in], refs[n_in], refs[n_in + 1 : n_in + 1 + n_send]
    field, work, ra_ref, rb_ref, done, in_sems, out_sems = refs[n_in + 1 + n_send :]
    tiles, block = keep.shape[0], keep.shape[1]
    frame, pitches, side = work.shape
    halo = (frame - 2 * block) // 2
    vregs = pitches // 8
    flip = lax.axis_index("inner") % 2
    places, start = [], 0
    for i in range(n_own):
        step = ins[i].shape[1]
        places.append((i, step, halo + start))
        places.append((n_own + i, step, halo + 2 * block - start - step))
        if i < n_halo:
            places.append((2 * n_own + i, step, halo + 2 * block + start))
            places.append((2 * n_own + n_halo + i, step, halo - start - step))
        start += step

    def fetch(g, slot):
        copies = []
        for i, step, place in places:
            at = jnp.where(flip == 0, place, frame - place - step)
            copies.append(
                pltpu.make_async_copy(
                    ins[i].at[g], field.at[slot, pl.ds(at, step)], in_sems.at[slot, i]
                )
            )
        return copies

    def store(g, slot):
        copies = [
            pltpu.make_async_copy(
                done.at[slot, pl.ds(flip * block, block)], keep.at[g], out_sems.at[slot, n_send]
            )
        ]
        first = (1 - flip) * block
        for k in range(n_send):
            step = sends[k].shape[1]
            copies.append(
                pltpu.make_async_copy(
                    done.at[slot, pl.ds(first, step)], sends[k].at[g], out_sems.at[slot, k]
                )
            )
            first = first + step
        return copies

    for copy in fetch(0, 0):
        copy.start()

    @pl.loop(0, tiles)
    def _(g):
        slot = g % 2

        @pl.when(g + 1 < tiles)
        def _():
            for copy in fetch(g + 1, 1 - slot):
                copy.start()

        for copy in fetch(g, slot):
            copy.wait()

        @pl.when(g >= 2)
        def _():
            for copy in store(g - 2, slot):
                copy.wait()

        rate = rate_ref[g]

        def rows_of(ref, e):
            return [ref[e, 8 * v : 8 * v + 8, :] for v in range(vregs)]

        def write_work(e, rows):
            for v in range(vregs):
                work[e, 8 * v : 8 * v + 8, :] = rows[v]

        def read_work(e):
            return rows_of(work, e)

        def read_field(e):
            return [field[slot, e, pl.ds(v, 8, stride=vregs), :] for v in range(vregs)]

        def write_done(e, rows):
            for v in range(vregs):
                done[slot, e - halo, pl.ds(v, 8, stride=vregs), :] = rows[v]

        def scaled(e):
            ra = [rate * x for x in rows_of(a_ref, e)]
            rb = [rate * x for x in rows_of(b_ref, e)]
            for v in range(vregs):
                ra_ref[e, 8 * v : 8 * v + 8, :] = ra[v]
                rb_ref[e, 8 * v : 8 * v + 8, :] = rb[v]
            return ra, rb

        def ready(e):
            return rows_of(ra_ref, e), rows_of(rb_ref, e)

        def sweep(first, count, read, write, rates, wide):
            def energy(e, here, below):
                after = read(e + 1)
                ra, rb = rates(e)
                above = [ra[v] * (after[v] - here[v]) for v in range(vregs)]
                nearby = here[1:] + [pltpu.roll(here[0], 7, 0)]
                pitch = [rb[v] * (nearby[v] - here[v]) for v in range(vregs)]
                before = [pltpu.roll(pitch[-1], 1, 0)] + pitch[:-1]
                write(
                    e,
                    [
                        here[v] + ((above[v] - below[v]) + (pitch[v] - before[v]))
                        for v in range(vregs)
                    ],
                )
                return after, above

            def several(e, carry, n):
                here, below = list(carry[:vregs]), list(carry[vregs:])
                for i in range(n):
                    here, below = energy(e + i, here, below)
                return (*here, *below)

            edge = read(first - 1)
            here = read(first)
            ra = rates(first - 1)[0]
            below = [ra[v] * (here[v] - edge[v]) for v in range(vregs)]
            carry = lax.fori_loop(
                0,
                count // wide,
                lambda i, carry: several(first + wide * i, carry, wide),
                (*here, *below),
            )
            for left in range(2, wide, 2):

                @pl.when(count % wide == left)
                def _(left=left):
                    several(first + count - left, carry, left)

        sweep(1, frame - 2, read_field, write_work, scaled, 2)

        @pl.loop(1, PASSES - 1)
        def _(n):
            sweep(n + 1, frame - 2 - 2 * n, read_work, write_work, ready, 4)

        sweep(PASSES, frame - 2 * PASSES, read_work, write_done, ready, 4)

        for copy in store(g, slot):
            copy.start()

    for g in range(max(0, tiles - 2), tiles):
        for copy in store(g, g % 2):
            copy.wait()


def diffuse(rate, a, b, own, got, own_halo, got_halo, steps):
    tiles, _, pitches, side = own[0].shape
    frame = a.shape[0]
    block = sum(steps)
    ins = [*own, *got, *own_halo, *got_halo]
    out = pl.pallas_call(
        functools.partial(diffusion_kernel, len(own), len(own_halo), len(steps)),
        out_shape=[
            jax.ShapeDtypeStruct((tiles, step, pitches, side), F32) for step in (block, *steps)
        ],
        in_specs=[VMEM] * 3 + [ANY] * len(ins),
        out_specs=[ANY] * (1 + len(steps)),
        scratch_shapes=[
            pltpu.VMEM((2, frame, pitches, side), F32),
            pltpu.VMEM((frame, pitches, side), F32),
            pltpu.VMEM((frame, pitches, side), F32),
            pltpu.VMEM((frame, pitches, side), F32),
            pltpu.VMEM((2, 2 * block, pitches, side), F32),
            pltpu.SemaphoreType.DMA((2, len(ins))),
            pltpu.SemaphoreType.DMA((2, len(steps) + 1)),
        ],
        compiler_params=params(),
        cost_estimate=cost(),
        name="diffuse_tiles",
    )(rate, a, b, *ins)
    return out[0], out[1:]


def across_lanes(window, side):
    frame, pitches = window.shape
    turned = window.reshape(frame, 8, pitches // 8).transpose(0, 2, 1).reshape(frame, pitches)
    return jnp.broadcast_to(turned[:, :, None], (frame, pitches, side))


def paired_shards(
    density,
    source_sector,
    source_tile,
    matrix_id,
    cubic_weights,
    bin_cells,
    wave_level,
    energy_rate,
    pitch_rate,
):
    sectors, inner = lax.axis_size("sector"), lax.axis_size("inner")
    inner_here = lax.axis_index("inner")
    flip, group = inner_here % 2, inner_here // 2
    block, pitches, cell_count = density.shape
    side = cubic_weights.shape[1]
    tiles = cell_count // side
    half = tiles // 2
    quarter = block // 4
    halo_chunks = PASSES // quarter
    first_steps = (quarter, quarter, quarter, quarter // 2, quarter - quarter // 2)
    last_steps = (quarter // 2, quarter, quarter, quarter - quarter // 4, block - 3 * quarter - quarter // 2 + quarter // 4)
    cap = slots(tiles, sectors)
    tables = (source_sector, source_tile)
    near, far = [1], list(range(2, sectors))

    weights = split_weights(matrix_id, cubic_weights)

    energies = energy_rate.shape[0]
    frame = 2 * block + 2 * PASSES
    energy_pad = jnp.pad(energy_rate[: energies - 1], ((PASSES, PASSES + 1), (0, 0)))
    pitch_pad = jnp.pad(pitch_rate[:, : pitches - 1], ((PASSES, PASSES), (0, 1)))
    first_energy = group * 2 * block
    a = across_lanes(lax.dynamic_slice_in_dim(energy_pad, first_energy, frame, 0), side)
    b = across_lanes(lax.dynamic_slice_in_dim(pitch_pad, first_energy, frame, 0), side)
    bin_ends = jnp.cumsum(bin_cells[0])
    cells = flip * (half * side) + jnp.arange(half * side, dtype=jnp.int32)
    bin_of = jnp.sum((bin_ends[None, :] <= cells[:, None]).astype(jnp.int32), axis=1)
    bins = jnp.arange(bin_ends.shape[0], dtype=jnp.int32)
    level = jnp.sum(jnp.where(bin_of[:, None] == bins[None, :], wave_level[0][None, :], 0.0), axis=1)
    rate = jnp.broadcast_to(level.reshape(half, 1, side), (half, 8, side))

    def at_lanes(t):
        return pl.ds(pl.multiple_of(t * side, side), side)

    def side_here():
        return lax.axis_index("inner") % 2

    swap = [(i, i ^ 1) for i in range(inner)]
    own_pairs, got_pairs = [], []
    for i in range(inner):
        for pairs, shift in ((own_pairs, -2 if i % 2 == 0 else 2), (got_pairs, 2 if i % 2 == 0 else -2)):
            if 0 <= i + shift < inner:
                pairs.append((i, i + shift))

    own, got, own_halo, got_halo = [], [], [], []
    packed = []
    start = 0
    for k, step in enumerate(first_steps):

        def first_of(start=start, step=step):
            here = side_here()
            return here * (block - start - step) + (1 - here) * start

        def find(field, first_of=first_of, step=step):
            first = first_of()
            return lambda t: [(t >= 0, lambda: field.at[pl.ds(first, step), :, at_lanes(t)])]

        def find_all(field):
            return lambda t: [(t >= 0, lambda: field.at[:, :, at_lanes(t)])]

        def receive(came, other, slot, first_of=first_of, step=step):
            return came.at[slot, pl.ds(first_of(), step)] if other == 1 else came.at[slot]

        def place(kept, sent):
            here = side_here()
            mine = lambda t: (t // half) == here
            return lambda t: [
                (mine(t), lambda: kept.at[t % half]),
                (jnp.logical_not(mine(t)), lambda: sent.at[t % half]),
            ]

        packed.append((start, step, find, receive, place))
        start += step

    def pack_first(k, after):
        start, step, find, _, _ = packed[k]
        groups = [(d, find, (step, pitches, side)) for d in far]
        if k == 0:
            groups += [(d, find_all, (block, pitches, side)) for d in near]
        return pack(groups, cap, tables, [density], after)

    sends = pack_first(0, ())
    recvs = sector_exchange(sends[:-1], far)
    beside = sector_exchange(sends[-1:], near)
    token = sends[0]
    crossing = []
    for k, (start, step, find, receive, place) in enumerate(packed):
        if k + 1 < len(packed):
            later = pack_first(k + 1, (token,))
            later, recvs = in_turn(later, recvs)
            coming = sector_exchange(later, far)
        if k == 1:
            recvs, (rate, a, b) = in_turn(recvs, [rate, a, b])
        after = ()
        if k > 0:
            after = [token, *(crossing[k - 2] if k == 2 else ()), *got_halo[: k - 2][-1:]]
        part = jax.ShapeDtypeStruct((half, step, pitches, side), F32)
        piece = (step, pitches, side)
        kept, sent, token = drift(
            find, place, receive, tables, weights, [density], beside + recvs, [part, part], piece, after
        )
        recvs = coming
        own.append(kept)
        got.append(lax.ppermute(sent, "inner", swap))
        crossing.append(got[-1:])
        if k < halo_chunks:
            own_halo.append(lax.ppermute(kept, "inner", own_pairs))
            crossing[-1] += own_halo[-1:]
        if 0 < k <= halo_chunks:
            got_halo.append(lax.ppermute(got[k - 1], "inner", got_pairs))
            crossing[-1] += got_halo[-1:]

    kept, sends = diffuse(rate, a, b, own, got, own_halo, got_halo, last_steps)

    returns, ready, out, start = sends, [], (), 0
    for k, step in enumerate(last_steps):

        def find(mine, theirs, start=start, step=step):
            here = side_here()
            return lambda t: [
                ((t // half) == here, lambda: mine.at[t % half, pl.ds(start, step)]),
                ((t // half) != here, lambda: theirs.at[t % half]),
            ]

        def place(result, start=start, step=step):
            return lambda t: [(t >= 0, lambda: result.at[pl.ds(start, step), :, at_lanes(t)])]

        ready.append((find, place, (step, pitches, side)))
        start += step

    def receive_slot(came, other, slot):
        return came.at[slot]

    def pack_last(k, after):
        find, _, piece = ready[k]
        sends = pack([(d, find, piece) for d in near + far], cap, tables, [kept, backs[k]], after)
        return sends[:1], sends[1:]

    whole = [jax.ShapeDtypeStruct(density.shape, F32)]
    backs = [lax.ppermute(returns[0], "inner", swap)]
    (last,), (backs[0],) = in_turn([returns[1]], [backs[0]])
    backs.append(lax.ppermute(last, "inner", swap))
    sends, far_sends = pack_last(0, ())
    recvs = sector_exchange(far_sends, far)
    beside = sector_exchange(sends, near)
    token = kept
    for k, (find, place, piece) in enumerate(ready):
        if k + 1 < len(ready):
            sends, far_sends = pack_last(k + 1, (token,))
            far_sends, recvs = in_turn(far_sends, recvs)
            coming = sector_exchange(far_sends, far), sector_exchange(sends, near)
        if k + 2 < len(ready):
            (last,), (backs[k + 1], *recvs) = in_turn([returns[k + 2]], [backs[k + 1], *recvs])
            backs.append(lax.ppermute(last, "inner", swap))
        *out, token = drift(
            find, place, receive_slot, tables, weights, [kept, backs[k]], beside + recvs, whole, piece, (), out
        )
        recvs, beside = coming
    return out[0]


def slots(tiles, sectors):
    return max(2, (3 * tiles + 2 * sectors - 1) // (2 * sectors))


def order_within(sources):
    tile_count = sources.shape[1]
    same = sources[:, :, None] == sources[:, None, :]
    earlier = jnp.arange(tile_count)[None, :] < jnp.arange(tile_count)[:, None]
    return jnp.sum((same & earlier[None]).astype(jnp.int32), axis=2)


def drift_step(density, source_sector, source_tile, matrix_id, cubic_weights):
    sectors = lax.axis_size("sector")
    sector_here = lax.axis_index("sector")
    energies, pitches, cell_count = density.shape
    tile_len = cubic_weights.shape[1]
    tile_count = cell_count // tile_len
    slot_count = max(2, (3 * tile_count + 2 * sectors - 1) // (2 * sectors))
    sources = source_sector[0]
    picked_tiles = source_tile[0]
    matrix_ids = matrix_id[0]
    tile_ranks = order_within(sources)
    slot_rank = jnp.arange(slot_count, dtype=jnp.int32)
    matched = (sources[:, None, :] == sector_here) & (
        tile_ranks[:, None, :] == slot_rank[None, :, None]
    )
    chosen = jnp.sum(jnp.where(matched, picked_tiles[:, None, :], 0), axis=2).reshape(-1)
    filled = jnp.any(matched, axis=2).reshape(-1).astype(jnp.float32)
    blocks = density.reshape(energies, pitches, tile_count, tile_len)
    outgoing = jnp.take(blocks, chosen, axis=2) * filled[None, None, :, None]
    incoming = lax.all_to_all(outgoing, "sector", split_axis=2, concat_axis=2, tiled=True)
    own_sources = sources[sector_here]
    own_ranks = tile_ranks[sector_here]
    own_ids = matrix_ids[sector_here]
    where_from = own_sources * slot_count + own_ranks
    departing = jnp.take(incoming, where_from, axis=2)
    matrices = jnp.take(cubic_weights, own_ids, axis=0)
    drifted = jnp.einsum("eptj,tij->epti", departing, matrices, precision=lax.Precision.HIGHEST)
    return drifted.reshape(energies, pitches, cell_count)


def one_pass(field, rate_cell, energy_rate, pitch_rate):
    flux_e = energy_rate[:-1, :, None] * (field[1:] - field[:-1])
    flux_p = pitch_rate[:, :-1, None] * (field[:, 1:] - field[:, :-1])
    change_e = jnp.pad(flux_e, ((0, 1), (0, 0), (0, 0))) - jnp.pad(flux_e, ((1, 0), (0, 0), (0, 0)))
    change_p = jnp.pad(flux_p, ((0, 0), (0, 1), (0, 0))) - jnp.pad(flux_p, ((0, 0), (1, 0), (0, 0)))
    return field + rate_cell[None, None, :] * (change_e + change_p)


def shards(
    density,
    source_sector,
    source_tile,
    matrix_id,
    cubic_weights,
    bin_cells,
    wave_level,
    energy_rate,
    pitch_rate,
):
    first = drift_step(density, source_sector, source_tile, matrix_id, cubic_weights)
    inner_count = lax.axis_size("inner")
    inner_here = lax.axis_index("inner")
    cell_count = first.shape[2]
    lengths = bin_cells[0]
    per_device = cell_count // inner_count
    owner_cells = jnp.full((inner_count,), per_device, jnp.int32)
    owner_ends = jnp.cumsum(owner_cells)
    owner_starts = owner_ends - owner_cells
    offsets = jnp.arange(per_device, dtype=jnp.int32)
    cell_index = owner_starts[:, None] + offsets[None, :]
    valid = (offsets[None, :] < owner_cells[:, None]).reshape(-1).astype(jnp.float32)
    clipped = jnp.minimum(cell_index, cell_count - 1).reshape(-1)
    packed = jnp.take(first, clipped, axis=2) * valid[None, None, :]
    cellwise = lax.all_to_all(packed, "inner", split_axis=2, concat_axis=0, tiled=True)
    bin_ends = jnp.cumsum(lengths)
    global_cells = owner_starts[inner_here] + offsets
    is_live = (offsets < owner_cells[inner_here]).astype(jnp.float32)
    bin_of = jnp.sum((bin_ends[None, :] <= global_cells[:, None]).astype(jnp.int32), axis=1)
    onehot = bin_of[:, None] == jnp.arange(inner_count, dtype=jnp.int32)[None, :]
    cell_level = jnp.sum(jnp.where(onehot, wave_level[0][None, :], 0.0), axis=1) * is_live

    def loop_body(step, current):
        return one_pass(current, cell_level, energy_rate, pitch_rate)

    diffused = lax.fori_loop(0, PASSES, loop_body, cellwise)
    returned = lax.all_to_all(diffused, "inner", split_axis=0, concat_axis=2, tiled=True)
    every_cell = jnp.arange(cell_count, dtype=jnp.int32)
    owner_index = jnp.sum((owner_ends[None, :] <= every_cell[:, None]).astype(jnp.int32), axis=1)
    offset = every_cell - owner_starts[owner_index]
    position = owner_index * per_device + offset
    restored = jnp.take(returned, position, axis=2)
    return drift_step(restored, source_sector, source_tile, matrix_id, cubic_weights)


def pairs_fit(mesh, energies, pitches, cells, side):
    sectors, inner = mesh.shape["sector"], mesh.shape["inner"]
    block = energies // inner
    tiles = cells // sectors // side
    return (
        sectors & (sectors - 1) == 0
        and inner % 2 == 0
        and tiles % 2 == 0
        and pitches % 16 == 0
        and side % 128 == 0
        and block % 16 == 0
        and 4 * PASSES == 3 * block
    )


def solution(mesh):
    specs = (
        P("inner", None, "sector"),
        P("inner", None, None),
        P("inner", None, None),
        P("inner", None, None),
        P(),
        P("sector", None),
        P("sector", None),
        P(),
        P(),
    )

    def whole(*arrays):
        energies, pitches, cells = arrays[0].shape
        fits = pairs_fit(mesh, energies, pitches, cells, arrays[4].shape[1])
        return jax.shard_map(
            paired_shards if fits else shards,
            mesh=mesh,
            in_specs=specs,
            out_specs=P("inner", None, "sector"),
            check_vma=False,
        )(*arrays)

    return whole
```

```python
import functools

import jax
import jax.numpy as jnp
from jax import lax
from jax.experimental import pallas as pl
from jax.experimental.pallas import tpu as pltpu
from jax.sharding import PartitionSpec as P

PASSES = 12
VMEM_LIMIT = 64 * 1024 * 1024 - 128 * 1024
ANY = pl.BlockSpec(memory_space=pltpu.HBM)
SMEM = pl.BlockSpec(memory_space=pltpu.SMEM)
VMEM = pl.BlockSpec(memory_space=pltpu.VMEM)
F32 = jnp.float32
BF16 = jnp.bfloat16


def params():
    return pltpu.CompilerParams(vmem_limit_bytes=VMEM_LIMIT)


def cost():
    return pl.CostEstimate(flops=0, bytes_accessed=1024, transcendentals=0)


def weights_kernel(mid_ref, w_ref, out_ref, raw, sems):
    tiles, side = raw.shape[0], raw.shape[1]
    me = lax.axis_index("sector")

    def copy(t):
        return pltpu.make_async_copy(w_ref.at[mid_ref[0, me, t]], raw.at[t], sems.at[t])

    @pl.loop(0, tiles)
    def _(t):
        copy(t).start()

    @pl.loop(0, tiles)
    def _(t):
        copy(t).wait()
        turned = jnp.transpose(raw[t])
        high = turned.astype(BF16)
        low = (turned - high.astype(F32)).astype(BF16)
        out_ref[t, :side, :side] = high
        out_ref[t, side:, :side] = high
        out_ref[t, :side, side:] = low
        out_ref[t, side:, side:] = jnp.zeros((side, side), BF16)


def split_weights(matrix_id, cubic_weights):
    tiles, side = matrix_id.shape[2], cubic_weights.shape[1]
    return pl.pallas_call(
        weights_kernel,
        out_shape=jax.ShapeDtypeStruct((tiles, 2 * side, 2 * side), BF16),
        in_specs=[SMEM, ANY],
        out_specs=VMEM,
        scratch_shapes=[
            pltpu.VMEM((tiles, side, side), F32),
            pltpu.SemaphoreType.DMA((tiles,)),
        ],
        compiler_params=params(),
        cost_estimate=cost(),
        name="split_weights",
    )(matrix_id, cubic_weights)


def pack_kernel(find, n_arrays, sec_ref, til_ref, *refs):
    sectors, tiles = sec_ref.shape[1], sec_ref.shape[2]
    send, room, in_sems, out_sems = refs[-4:]
    pieces = find(*refs[:n_arrays])
    me = lax.axis_index("sector")
    counts = []
    for dest in range(sectors):

        def body(t, count, dest=dest):
            hit = jnp.logical_and(sec_ref[0, dest, t] == me, me != dest)

            @pl.when(hit)
            def _():
                for guard, piece in pieces(til_ref[0, dest, t]):

                    @pl.when(guard)
                    def _():
                        pltpu.make_async_copy(
                            piece(), room.at[dest, count], in_sems.at[dest, count]
                        ).start()

            return count + hit.astype(jnp.int32)

        counts.append(lax.fori_loop(0, tiles, body, jnp.int32(0)))
    for dest in range(sectors):

        @pl.loop(0, counts[dest])
        def _(slot, dest=dest):
            here, there = room.at[dest, slot], send.at[dest, slot]
            pltpu.make_async_copy(here, here, in_sems.at[dest, slot]).wait()
            pltpu.make_async_copy(here, there, out_sems.at[dest, slot]).start()

    for dest in range(sectors):

        @pl.loop(0, counts[dest])
        def _(slot, dest=dest):
            here, there = room.at[dest, slot], send.at[dest, slot]
            pltpu.make_async_copy(here, there, out_sems.at[dest, slot]).wait()


def pack(find, cap, tables, arrays, piece, after=()):
    sectors = tables[0].shape[1]
    return pl.pallas_call(
        functools.partial(pack_kernel, find, len(arrays)),
        out_shape=jax.ShapeDtypeStruct((sectors, cap) + piece, F32),
        in_specs=[SMEM, SMEM] + [ANY] * (len(arrays) + len(after)),
        out_specs=ANY,
        scratch_shapes=[
            pltpu.VMEM((sectors, cap) + piece, F32),
            pltpu.SemaphoreType.DMA((sectors, cap)),
            pltpu.SemaphoreType.DMA((sectors, cap)),
        ],
        compiler_params=params(),
        cost_estimate=cost(),
        name="pack_tiles",
    )(*tables, *arrays, *after)


def sector_exchange(send):
    return lax.all_to_all(send, "sector", split_axis=0, concat_axis=0, tiled=True)


def in_turn(later, earlier):
    both = lax.optimization_barrier((*later, *earlier))
    return list(both[: len(later)]), list(both[len(later) :])


def drift_kernel(find, place, n_local, n_extra, sec_ref, til_ref, w_ref, *refs):
    sectors, tiles = sec_ref.shape[1], sec_ref.shape[2]
    local, came = refs[:n_local], refs[n_local]
    outs = refs[n_local + 1 + n_extra : -5]
    token, taken, made, in_sems, out_sems = refs[-5:]
    pieces = find(*local)
    put = place(*outs)
    me = lax.axis_index("sector")
    rows, side = taken.shape[1] * taken.shape[2], taken.shape[3]
    token[...] = jnp.zeros(token.shape, F32)

    def fetch(t, counts):
        source = sec_ref[0, me, t]

        @pl.when(source == me)
        def _():
            for guard, piece in pieces(til_ref[0, me, t]):

                @pl.when(guard)
                def _():
                    pltpu.make_async_copy(piece(), taken.at[t], in_sems.at[t]).start()

        slot = jnp.int32(0)
        for s in range(sectors):
            slot = jnp.where(source == s, counts[s], slot)

        @pl.when(source != me)
        def _():
            pltpu.make_async_copy(came.at[source, slot], taken.at[t], in_sems.at[t]).start()

        return tuple(c + (source == s).astype(jnp.int32) for s, c in enumerate(counts))

    lax.fori_loop(0, tiles, fetch, (jnp.int32(0),) * sectors)

    @pl.loop(0, tiles)
    def _(t):
        pltpu.make_async_copy(taken.at[t], taken.at[t], in_sems.at[t]).wait()
        value = taken[t].reshape(rows, side)
        high = value.astype(BF16)
        low = (value - high.astype(F32)).astype(BF16)
        both = jnp.dot(jnp.concatenate([high, low], axis=1), w_ref[t], preferred_element_type=F32)
        made[t] = (both[:, :side] + both[:, side:]).reshape(taken.shape[1:])
        for guard, there in put(t):

            @pl.when(guard)
            def _():
                pltpu.make_async_copy(made.at[t], there(), out_sems.at[t]).start()

    @pl.loop(0, tiles)
    def _(t):
        pltpu.make_async_copy(made.at[t], made.at[t], out_sems.at[t]).wait()


def drift(find, place, tables, weights, local, came, outs, piece, after=(), carried=()):
    tiles = tables[0].shape[2]
    n_local = len(local)
    ins = [*tables, weights, *local, came, *after, *carried]
    n_extra = len(after) + len(carried)
    return pl.pallas_call(
        functools.partial(drift_kernel, find, place, n_local, n_extra),
        out_shape=[*outs, jax.ShapeDtypeStruct((8, 128), F32)],
        in_specs=[SMEM, SMEM, VMEM] + [ANY] * (len(ins) - 3),
        out_specs=[ANY] * len(outs) + [VMEM],
        scratch_shapes=[
            pltpu.VMEM((tiles,) + piece, F32),
            pltpu.VMEM((tiles,) + piece, F32),
            pltpu.SemaphoreType.DMA((tiles,)),
            pltpu.SemaphoreType.DMA((tiles,)),
        ],
        input_output_aliases={len(ins) - 1: 0} if carried else {},
        compiler_params=params(),
        cost_estimate=cost(),
        name="drift_chunk",
    )(*ins)


def diffusion_kernel(n_own, n_halo, n_send, rate_ref, a_ref, b_ref, *refs):
    n_in = 2 * n_own + 2 * n_halo
    ins, keep, sends = refs[:n_in], refs[n_in], refs[n_in + 1 : n_in + 1 + n_send]
    field, work, ra_ref, rb_ref, done, in_sems, out_sems = refs[n_in + 1 + n_send :]
    tiles, block = keep.shape[0], keep.shape[1]
    frame, pitches, side = work.shape
    halo = (frame - 2 * block) // 2
    vregs = pitches // 8
    flip = lax.axis_index("inner") % 2
    places, start = [], 0
    for i in range(n_own):
        step = ins[i].shape[1]
        places.append((i, step, halo + start))
        places.append((n_own + i, step, halo + 2 * block - start - step))
        if i < n_halo:
            places.append((2 * n_own + i, step, halo + 2 * block + start))
            places.append((2 * n_own + n_halo + i, step, halo - start - step))
        start += step

    def fetch(g, slot):
        copies = []
        for i, step, place in places:
            at = jnp.where(flip == 0, place, frame - place - step)
            copies.append(
                pltpu.make_async_copy(
                    ins[i].at[g], field.at[slot, pl.ds(at, step)], in_sems.at[slot, i]
                )
            )
        return copies

    def store(g, slot):
        copies = [
            pltpu.make_async_copy(
                done.at[slot, pl.ds(flip * block, block)], keep.at[g], out_sems.at[slot, n_send]
            )
        ]
        first = (1 - flip) * block
        for k in range(n_send):
            step = sends[k].shape[1]
            copies.append(
                pltpu.make_async_copy(
                    done.at[slot, pl.ds(first, step)], sends[k].at[g], out_sems.at[slot, k]
                )
            )
            first = first + step
        return copies

    for copy in fetch(0, 0):
        copy.start()

    @pl.loop(0, tiles)
    def _(g):
        slot = g % 2

        @pl.when(g + 1 < tiles)
        def _():
            for copy in fetch(g + 1, 1 - slot):
                copy.start()

        for copy in fetch(g, slot):
            copy.wait()

        @pl.when(g >= 2)
        def _():
            for copy in store(g - 2, slot):
                copy.wait()

        rate = rate_ref[g]

        def rows_of(ref, e):
            return [ref[e, 8 * v : 8 * v + 8, :] for v in range(vregs)]

        def write_work(e, rows):
            for v in range(vregs):
                work[e, 8 * v : 8 * v + 8, :] = rows[v]

        def read_work(e):
            return rows_of(work, e)

        def read_field(e):
            return [field[slot, e, pl.ds(v, 8, stride=vregs), :] for v in range(vregs)]

        def write_done(e, rows):
            for v in range(vregs):
                done[slot, e - halo, pl.ds(v, 8, stride=vregs), :] = rows[v]

        def scaled(e):
            ra = [rate * x for x in rows_of(a_ref, e)]
            rb = [rate * x for x in rows_of(b_ref, e)]
            for v in range(vregs):
                ra_ref[e, 8 * v : 8 * v + 8, :] = ra[v]
                rb_ref[e, 8 * v : 8 * v + 8, :] = rb[v]
            return ra, rb

        def ready(e):
            return rows_of(ra_ref, e), rows_of(rb_ref, e)

        def sweep(first, count, read, write, rates, wide):
            def energy(e, here, below):
                after = read(e + 1)
                ra, rb = rates(e)
                above = [ra[v] * (after[v] - here[v]) for v in range(vregs)]
                nearby = here[1:] + [pltpu.roll(here[0], 7, 0)]
                pitch = [rb[v] * (nearby[v] - here[v]) for v in range(vregs)]
                before = [pltpu.roll(pitch[-1], 1, 0)] + pitch[:-1]
                write(
                    e,
                    [
                        here[v] + ((above[v] - below[v]) + (pitch[v] - before[v]))
                        for v in range(vregs)
                    ],
                )
                return after, above

            def several(e, carry, n):
                here, below = list(carry[:vregs]), list(carry[vregs:])
                for i in range(n):
                    here, below = energy(e + i, here, below)
                return (*here, *below)

            edge = read(first - 1)
            here = read(first)
            ra = rates(first - 1)[0]
            below = [ra[v] * (here[v] - edge[v]) for v in range(vregs)]
            carry = lax.fori_loop(
                0,
                count // wide,
                lambda i, carry: several(first + wide * i, carry, wide),
                (*here, *below),
            )
            for left in range(2, wide, 2):

                @pl.when(count % wide == left)
                def _(left=left):
                    several(first + count - left, carry, left)

        sweep(1, frame - 2, read_field, write_work, scaled, 2)

        @pl.loop(1, PASSES - 1)
        def _(n):
            sweep(n + 1, frame - 2 - 2 * n, read_work, write_work, ready, 4)

        sweep(PASSES, frame - 2 * PASSES, read_work, write_done, ready, 4)

        for copy in store(g, slot):
            copy.start()

    for g in range(max(0, tiles - 2), tiles):
        for copy in store(g, g % 2):
            copy.wait()


def diffuse(rate, a, b, own, got, own_halo, got_halo, steps):
    tiles, _, pitches, side = own[0].shape
    frame = a.shape[0]
    block = sum(steps)
    ins = [*own, *got, *own_halo, *got_halo]
    out = pl.pallas_call(
        functools.partial(diffusion_kernel, len(own), len(own_halo), len(steps)),
        out_shape=[
            jax.ShapeDtypeStruct((tiles, step, pitches, side), F32) for step in (block, *steps)
        ],
        in_specs=[VMEM] * 3 + [ANY] * len(ins),
        out_specs=[ANY] * (1 + len(steps)),
        scratch_shapes=[
            pltpu.VMEM((2, frame, pitches, side), F32),
            pltpu.VMEM((frame, pitches, side), F32),
            pltpu.VMEM((frame, pitches, side), F32),
            pltpu.VMEM((frame, pitches, side), F32),
            pltpu.VMEM((2, 2 * block, pitches, side), F32),
            pltpu.SemaphoreType.DMA((2, len(ins))),
            pltpu.SemaphoreType.DMA((2, len(steps) + 1)),
        ],
        compiler_params=params(),
        cost_estimate=cost(),
        name="diffuse_tiles",
    )(rate, a, b, *ins)
    return out[0], out[1:]


def across_lanes(window, side):
    frame, pitches = window.shape
    turned = window.reshape(frame, 8, pitches // 8).transpose(0, 2, 1).reshape(frame, pitches)
    return jnp.broadcast_to(turned[:, :, None], (frame, pitches, side))


def paired_shards(
    density,
    source_sector,
    source_tile,
    matrix_id,
    cubic_weights,
    bin_cells,
    wave_level,
    energy_rate,
    pitch_rate,
):
    sectors, inner = lax.axis_size("sector"), lax.axis_size("inner")
    inner_here = lax.axis_index("inner")
    flip, group = inner_here % 2, inner_here // 2
    block, pitches, cell_count = density.shape
    side = cubic_weights.shape[1]
    tiles = cell_count // side
    half = tiles // 2
    quarter = block // 4
    halo_chunks = PASSES // quarter
    first_steps = (quarter, quarter, quarter, quarter // 2, quarter - quarter // 2)
    last_steps = (quarter // 2, quarter, quarter, quarter - quarter // 4, block - 3 * quarter - quarter // 2 + quarter // 4)
    cap = slots(tiles, sectors)
    tables = (source_sector, source_tile)

    weights = split_weights(matrix_id, cubic_weights)

    energies = energy_rate.shape[0]
    frame = 2 * block + 2 * PASSES
    energy_pad = jnp.pad(energy_rate[: energies - 1], ((PASSES, PASSES + 1), (0, 0)))
    pitch_pad = jnp.pad(pitch_rate[:, : pitches - 1], ((PASSES, PASSES), (0, 1)))
    first_energy = group * 2 * block
    a = across_lanes(lax.dynamic_slice_in_dim(energy_pad, first_energy, frame, 0), side)
    b = across_lanes(lax.dynamic_slice_in_dim(pitch_pad, first_energy, frame, 0), side)
    bin_ends = jnp.cumsum(bin_cells[0])
    cells = flip * (half * side) + jnp.arange(half * side, dtype=jnp.int32)
    bin_of = jnp.sum((bin_ends[None, :] <= cells[:, None]).astype(jnp.int32), axis=1)
    bins = jnp.arange(bin_ends.shape[0], dtype=jnp.int32)
    level = jnp.sum(jnp.where(bin_of[:, None] == bins[None, :], wave_level[0][None, :], 0.0), axis=1)
    rate = jnp.broadcast_to(level.reshape(half, 1, side), (half, 8, side))

    def at_lanes(t):
        return pl.ds(pl.multiple_of(t * side, side), side)

    def side_here():
        return lax.axis_index("inner") % 2

    swap = [(i, i ^ 1) for i in range(inner)]
    own_pairs, got_pairs = [], []
    for i in range(inner):
        for pairs, shift in ((own_pairs, -2 if i % 2 == 0 else 2), (got_pairs, 2 if i % 2 == 0 else -2)):
            if 0 <= i + shift < inner:
                pairs.append((i, i + shift))

    own, got, own_halo, got_halo = [], [], [], []
    packed = []
    start = 0
    for k, step in enumerate(first_steps):

        def first_of(start=start, step=step):
            here = side_here()
            return here * (block - start - step) + (1 - here) * start

        def find(field, first_of=first_of, step=step):
            first = first_of()
            return lambda t: [(t >= 0, lambda: field.at[pl.ds(first, step), :, at_lanes(t)])]

        def place(kept, sent):
            here = side_here()
            mine = lambda t: (t // half) == here
            return lambda t: [
                (mine(t), lambda: kept.at[t % half]),
                (jnp.logical_not(mine(t)), lambda: sent.at[t % half]),
            ]

        packed.append((start, step, find, place))
        start += step

    def pack_first(k, after):
        _, step, find, _ = packed[k]
        return pack(find, cap, tables, [density], (step, pitches, side), after)

    send = pack_first(0, ())
    came = sector_exchange(send)
    token = send
    crossing = []
    for k, (start, step, find, place) in enumerate(packed):
        if k + 1 < len(packed):
            later = pack_first(k + 1, (token,))
            (later,), (came,) = in_turn([later], [came])
            coming = sector_exchange(later)
        if k == 1:
            (came,), (rate, a, b) = in_turn([came], [rate, a, b])
        after = ()
        if k > 0:
            after = [token, *(crossing[k - 2] if k == 2 else ()), *got_halo[: k - 2][-1:]]
        part = jax.ShapeDtypeStruct((half, step, pitches, side), F32)
        piece = (step, pitches, side)
        kept, sent, token = drift(
            find, place, tables, weights, [density], came, [part, part], piece, after
        )
        came = coming
        own.append(kept)
        got.append(lax.ppermute(sent, "inner", swap))
        crossing.append(got[-1:])
        if k < halo_chunks:
            own_halo.append(lax.ppermute(kept, "inner", own_pairs))
            crossing[-1] += own_halo[-1:]
        if 0 < k <= halo_chunks:
            got_halo.append(lax.ppermute(got[k - 1], "inner", got_pairs))
            crossing[-1] += got_halo[-1:]

    kept, sends = diffuse(rate, a, b, own, got, own_halo, got_halo, last_steps)

    returns, ready, out, start = sends, [], (), 0
    for k, step in enumerate(last_steps):

        def find(mine, theirs, start=start, step=step):
            here = side_here()
            return lambda t: [
                ((t // half) == here, lambda: mine.at[t % half, pl.ds(start, step)]),
                ((t // half) != here, lambda: theirs.at[t % half]),
            ]

        def place(result, start=start, step=step):
            return lambda t: [(t >= 0, lambda: result.at[pl.ds(start, step), :, at_lanes(t)])]

        ready.append((find, place, (step, pitches, side)))
        start += step

    def pack_last(k, after):
        find, _, piece = ready[k]
        return pack(find, cap, tables, [kept, backs[k]], piece, after)

    whole = [jax.ShapeDtypeStruct(density.shape, F32)]
    backs = [lax.ppermute(returns[0], "inner", swap)]
    (last,), (backs[0],) = in_turn([returns[1]], [backs[0]])
    backs.append(lax.ppermute(last, "inner", swap))
    came = sector_exchange(pack_last(0, ()))
    token = kept
    for k, (find, place, piece) in enumerate(ready):
        if k + 1 < len(ready):
            send = pack_last(k + 1, (token,))
            (send,), (came,) = in_turn([send], [came])
            coming = sector_exchange(send)
        if k + 2 < len(ready):
            (last,), (backs[k + 1],) = in_turn([returns[k + 2]], [backs[k + 1]])
            backs.append(lax.ppermute(last, "inner", swap))
        *out, token = drift(
            find, place, tables, weights, [kept, backs[k]], came, whole, piece, (), out
        )
        came = coming
    return out[0]


def slots(tiles, sectors):
    return max(2, (3 * tiles + 2 * sectors - 1) // (2 * sectors))


def order_within(sources):
    tile_count = sources.shape[1]
    same = sources[:, :, None] == sources[:, None, :]
    earlier = jnp.arange(tile_count)[None, :] < jnp.arange(tile_count)[:, None]
    return jnp.sum((same & earlier[None]).astype(jnp.int32), axis=2)


def drift_step(density, source_sector, source_tile, matrix_id, cubic_weights):
    sectors = lax.axis_size("sector")
    sector_here = lax.axis_index("sector")
    energies, pitches, cell_count = density.shape
    tile_len = cubic_weights.shape[1]
    tile_count = cell_count // tile_len
    slot_count = max(2, (3 * tile_count + 2 * sectors - 1) // (2 * sectors))
    sources = source_sector[0]
    picked_tiles = source_tile[0]
    matrix_ids = matrix_id[0]
    tile_ranks = order_within(sources)
    slot_rank = jnp.arange(slot_count, dtype=jnp.int32)
    matched = (sources[:, None, :] == sector_here) & (
        tile_ranks[:, None, :] == slot_rank[None, :, None]
    )
    chosen = jnp.sum(jnp.where(matched, picked_tiles[:, None, :], 0), axis=2).reshape(-1)
    filled = jnp.any(matched, axis=2).reshape(-1).astype(jnp.float32)
    blocks = density.reshape(energies, pitches, tile_count, tile_len)
    outgoing = jnp.take(blocks, chosen, axis=2) * filled[None, None, :, None]
    incoming = lax.all_to_all(outgoing, "sector", split_axis=2, concat_axis=2, tiled=True)
    own_sources = sources[sector_here]
    own_ranks = tile_ranks[sector_here]
    own_ids = matrix_ids[sector_here]
    where_from = own_sources * slot_count + own_ranks
    departing = jnp.take(incoming, where_from, axis=2)
    matrices = jnp.take(cubic_weights, own_ids, axis=0)
    drifted = jnp.einsum("eptj,tij->epti", departing, matrices, precision=lax.Precision.HIGHEST)
    return drifted.reshape(energies, pitches, cell_count)


def one_pass(field, rate_cell, energy_rate, pitch_rate):
    flux_e = energy_rate[:-1, :, None] * (field[1:] - field[:-1])
    flux_p = pitch_rate[:, :-1, None] * (field[:, 1:] - field[:, :-1])
    change_e = jnp.pad(flux_e, ((0, 1), (0, 0), (0, 0))) - jnp.pad(flux_e, ((1, 0), (0, 0), (0, 0)))
    change_p = jnp.pad(flux_p, ((0, 0), (0, 1), (0, 0))) - jnp.pad(flux_p, ((0, 0), (1, 0), (0, 0)))
    return field + rate_cell[None, None, :] * (change_e + change_p)


def shards(
    density,
    source_sector,
    source_tile,
    matrix_id,
    cubic_weights,
    bin_cells,
    wave_level,
    energy_rate,
    pitch_rate,
):
    first = drift_step(density, source_sector, source_tile, matrix_id, cubic_weights)
    inner_count = lax.axis_size("inner")
    inner_here = lax.axis_index("inner")
    cell_count = first.shape[2]
    lengths = bin_cells[0]
    per_device = cell_count // inner_count
    owner_cells = jnp.full((inner_count,), per_device, jnp.int32)
    owner_ends = jnp.cumsum(owner_cells)
    owner_starts = owner_ends - owner_cells
    offsets = jnp.arange(per_device, dtype=jnp.int32)
    cell_index = owner_starts[:, None] + offsets[None, :]
    valid = (offsets[None, :] < owner_cells[:, None]).reshape(-1).astype(jnp.float32)
    clipped = jnp.minimum(cell_index, cell_count - 1).reshape(-1)
    packed = jnp.take(first, clipped, axis=2) * valid[None, None, :]
    cellwise = lax.all_to_all(packed, "inner", split_axis=2, concat_axis=0, tiled=True)
    bin_ends = jnp.cumsum(lengths)
    global_cells = owner_starts[inner_here] + offsets
    is_live = (offsets < owner_cells[inner_here]).astype(jnp.float32)
    bin_of = jnp.sum((bin_ends[None, :] <= global_cells[:, None]).astype(jnp.int32), axis=1)
    onehot = bin_of[:, None] == jnp.arange(inner_count, dtype=jnp.int32)[None, :]
    cell_level = jnp.sum(jnp.where(onehot, wave_level[0][None, :], 0.0), axis=1) * is_live

    def loop_body(step, current):
        return one_pass(current, cell_level, energy_rate, pitch_rate)

    diffused = lax.fori_loop(0, PASSES, loop_body, cellwise)
    returned = lax.all_to_all(diffused, "inner", split_axis=0, concat_axis=2, tiled=True)
    every_cell = jnp.arange(cell_count, dtype=jnp.int32)
    owner_index = jnp.sum((owner_ends[None, :] <= every_cell[:, None]).astype(jnp.int32), axis=1)
    offset = every_cell - owner_starts[owner_index]
    position = owner_index * per_device + offset
    restored = jnp.take(returned, position, axis=2)
    return drift_step(restored, source_sector, source_tile, matrix_id, cubic_weights)


def pairs_fit(mesh, energies, pitches, cells, side):
    sectors, inner = mesh.shape["sector"], mesh.shape["inner"]
    block = energies // inner
    tiles = cells // sectors // side
    return (
        sectors & (sectors - 1) == 0
        and inner % 2 == 0
        and tiles % 2 == 0
        and pitches % 16 == 0
        and side % 128 == 0
        and block % 16 == 0
        and 4 * PASSES == 3 * block
    )


def solution(mesh):
    specs = (
        P("inner", None, "sector"),
        P("inner", None, None),
        P("inner", None, None),
        P("inner", None, None),
        P(),
        P("sector", None),
        P("sector", None),
        P(),
        P(),
    )

    def whole(*arrays):
        energies, pitches, cells = arrays[0].shape
        fits = pairs_fit(mesh, energies, pitches, cells, arrays[4].shape[1])
        return jax.shard_map(
            paired_shards if fits else shards,
            mesh=mesh,
            in_specs=specs,
            out_specs=P("inner", None, "sector"),
            check_vma=False,
        )(*arrays)

    return whole
```

```python
import functools

import jax
import jax.numpy as jnp
from jax import lax
from jax.experimental import pallas as pl
from jax.experimental.pallas import tpu as pltpu
from jax.sharding import PartitionSpec as P

PASSES = 12
VMEM_LIMIT = 64 * 1024 * 1024 - 128 * 1024
ANY = pl.BlockSpec(memory_space=pltpu.HBM)
SMEM = pl.BlockSpec(memory_space=pltpu.SMEM)
VMEM = pl.BlockSpec(memory_space=pltpu.VMEM)
F32 = jnp.float32
BF16 = jnp.bfloat16


def params():
    return pltpu.CompilerParams(vmem_limit_bytes=VMEM_LIMIT)


def cost():
    return pl.CostEstimate(flops=0, bytes_accessed=1024, transcendentals=0)


def weights_kernel(mid_ref, w_ref, out_ref, raw, sems):
    tiles, side = raw.shape[0], raw.shape[1]
    me = lax.axis_index("sector")

    def copy(t):
        return pltpu.make_async_copy(w_ref.at[mid_ref[0, me, t]], raw.at[t], sems.at[t])

    @pl.loop(0, tiles)
    def _(t):
        copy(t).start()

    @pl.loop(0, tiles)
    def _(t):
        copy(t).wait()
        turned = jnp.transpose(raw[t])
        high = turned.astype(BF16)
        low = (turned - high.astype(F32)).astype(BF16)
        out_ref[t, :side, :side] = high
        out_ref[t, side:, :side] = high
        out_ref[t, :side, side:] = low
        out_ref[t, side:, side:] = jnp.zeros((side, side), BF16)


def split_weights(matrix_id, cubic_weights):
    tiles, side = matrix_id.shape[2], cubic_weights.shape[1]
    return pl.pallas_call(
        weights_kernel,
        out_shape=jax.ShapeDtypeStruct((tiles, 2 * side, 2 * side), BF16),
        in_specs=[SMEM, ANY],
        out_specs=VMEM,
        scratch_shapes=[
            pltpu.VMEM((tiles, side, side), F32),
            pltpu.SemaphoreType.DMA((tiles,)),
        ],
        compiler_params=params(),
        cost_estimate=cost(),
        name="split_weights",
    )(matrix_id, cubic_weights)


def pack_kernel(offsets, finds, n_arrays, sec_ref, til_ref, *refs):
    tiles, n = sec_ref.shape[2], len(offsets)
    sends, rooms = refs[-2 * n - 2 : -n - 2], refs[-n - 2 : -2]
    in_sems, out_sems = refs[-2:]
    me = lax.axis_index("sector")
    counts = []
    for i, d in enumerate(offsets):
        dest = me ^ d
        pieces = finds[i](*refs[:n_arrays])

        def body(t, count, i=i, dest=dest, pieces=pieces):
            hit = sec_ref[0, dest, t] == me

            @pl.when(hit)
            def _():
                for guard, piece in pieces(til_ref[0, dest, t]):

                    @pl.when(guard)
                    def _():
                        pltpu.make_async_copy(piece(), rooms[i].at[count], in_sems.at[i, count]).start()

            return count + hit.astype(jnp.int32)

        counts.append(lax.fori_loop(0, tiles, body, jnp.int32(0)))
    for i in range(n):

        @pl.loop(0, counts[i])
        def _(slot, i=i):
            here = rooms[i].at[slot]
            pltpu.make_async_copy(here, here, in_sems.at[i, slot]).wait()
            pltpu.make_async_copy(here, sends[i].at[slot], out_sems.at[i, slot]).start()

    for i in range(n):

        @pl.loop(0, counts[i])
        def _(slot, i=i):
            pltpu.make_async_copy(rooms[i].at[slot], sends[i].at[slot], out_sems.at[i, slot]).wait()


def pack(groups, cap, tables, arrays, after=()):
    n = len(groups)
    offsets, finds, shapes = zip(*groups)
    return pl.pallas_call(
        functools.partial(pack_kernel, offsets, finds, len(arrays)),
        out_shape=[jax.ShapeDtypeStruct((cap,) + shape, F32) for shape in shapes],
        in_specs=[SMEM, SMEM] + [ANY] * (len(arrays) + len(after)),
        out_specs=[ANY] * n,
        scratch_shapes=[
            *[pltpu.VMEM((cap,) + shape, F32) for shape in shapes],
            pltpu.SemaphoreType.DMA((n, cap)),
            pltpu.SemaphoreType.DMA((n, cap)),
        ],
        compiler_params=params(),
        cost_estimate=cost(),
        name="pack_tiles",
    )(*tables, *arrays, *after)


def sector_exchange(sends, offsets):
    sectors = lax.axis_size("sector")
    return [
        lax.ppermute(send, "sector", [(s, s ^ d) for s in range(sectors)])
        for d, send in zip(offsets, sends)
    ]


def queue(came, sends, offsets):
    sends = list(sends)
    for i, send in enumerate(sends):
        (sends[i],), (came[-1][i],) = in_turn([send], [came[-1][i]])
    came.append(sector_exchange(sends, offsets))


def in_turn(later, earlier):
    both = lax.optimization_barrier((*later, *earlier))
    return list(both[: len(later)]), list(both[len(later) :])


def drift_kernel(find, place, receive, n_local, n_extra, sec_ref, til_ref, w_ref, *refs):
    sectors, tiles = sec_ref.shape[1], sec_ref.shape[2]
    local, recvs = refs[:n_local], refs[n_local : n_local + sectors - 1]
    outs = refs[n_local + sectors - 1 + n_extra : -5]
    token, taken, made, in_sems, out_sems = refs[-5:]
    pieces = find(*local)
    put = place(*outs)
    me = lax.axis_index("sector")
    rows, side = taken.shape[1] * taken.shape[2], taken.shape[3]
    token[...] = jnp.zeros(token.shape, F32)

    def fetch(t, counts):
        d = sec_ref[0, me, t] ^ me

        @pl.when(d == 0)
        def _():
            for guard, piece in pieces(til_ref[0, me, t]):

                @pl.when(guard)
                def _():
                    pltpu.make_async_copy(piece(), taken.at[t], in_sems.at[t]).start()

        for other in range(1, sectors):

            @pl.when(d == other)
            def _(other=other):
                came = receive(recvs[other - 1], other, counts[other - 1])
                pltpu.make_async_copy(came, taken.at[t], in_sems.at[t]).start()

        return tuple(c + (d == i + 1).astype(jnp.int32) for i, c in enumerate(counts))

    lax.fori_loop(0, tiles, fetch, (jnp.int32(0),) * (sectors - 1))

    @pl.loop(0, tiles)
    def _(t):
        pltpu.make_async_copy(taken.at[t], taken.at[t], in_sems.at[t]).wait()
        value = taken[t].reshape(rows, side)
        high = value.astype(BF16)
        low = (value - high.astype(F32)).astype(BF16)
        both = jnp.dot(jnp.concatenate([high, low], axis=1), w_ref[t], preferred_element_type=F32)
        made[t] = (both[:, :side] + both[:, side:]).reshape(taken.shape[1:])
        for guard, there in put(t):

            @pl.when(guard)
            def _():
                pltpu.make_async_copy(made.at[t], there(), out_sems.at[t]).start()

    @pl.loop(0, tiles)
    def _(t):
        pltpu.make_async_copy(made.at[t], made.at[t], out_sems.at[t]).wait()


def drift(find, place, receive, tables, weights, local, recvs, outs, piece, after=(), carried=()):
    sectors, tiles = tables[0].shape[1], tables[0].shape[2]
    n_local = len(local)
    ins = [*tables, weights, *local, *recvs, *after, *carried]
    n_extra = len(after) + len(carried)
    return pl.pallas_call(
        functools.partial(drift_kernel, find, place, receive, n_local, n_extra),
        out_shape=[*outs, jax.ShapeDtypeStruct((8, 128), F32)],
        in_specs=[SMEM, SMEM, VMEM] + [ANY] * (len(ins) - 3),
        out_specs=[ANY] * len(outs) + [VMEM],
        scratch_shapes=[
            pltpu.VMEM((tiles,) + piece, F32),
            pltpu.VMEM((tiles,) + piece, F32),
            pltpu.SemaphoreType.DMA((tiles,)),
            pltpu.SemaphoreType.DMA((tiles,)),
        ],
        input_output_aliases={len(ins) - 1: 0} if carried else {},
        compiler_params=params(),
        cost_estimate=cost(),
        name="drift_chunk",
    )(*ins)


def diffusion_kernel(n_own, n_halo, n_send, rate_ref, a_ref, b_ref, *refs):
    n_in = 2 * n_own + 2 * n_halo
    ins, keep, sends = refs[:n_in], refs[n_in], refs[n_in + 1 : n_in + 1 + n_send]
    field, work, ra_ref, rb_ref, done, in_sems, out_sems = refs[n_in + 1 + n_send :]
    tiles, block = keep.shape[0], keep.shape[1]
    frame, pitches, side = work.shape
    halo = (frame - 2 * block) // 2
    vregs = pitches // 8
    flip = lax.axis_index("inner") % 2
    places, start = [], 0
    for i in range(n_own):
        step = ins[i].shape[1]
        places.append((i, step, halo + start))
        places.append((n_own + i, step, halo + 2 * block - start - step))
        if i < n_halo:
            places.append((2 * n_own + i, step, halo + 2 * block + start))
            places.append((2 * n_own + n_halo + i, step, halo - start - step))
        start += step

    def fetch(g, slot):
        copies = []
        for i, step, place in places:
            at = jnp.where(flip == 0, place, frame - place - step)
            copies.append(
                pltpu.make_async_copy(
                    ins[i].at[g], field.at[slot, pl.ds(at, step)], in_sems.at[slot, i]
                )
            )
        return copies

    def store(g, slot):
        copies = [
            pltpu.make_async_copy(
                done.at[slot, pl.ds(flip * block, block)], keep.at[g], out_sems.at[slot, n_send]
            )
        ]
        first = (1 - flip) * block
        for k in range(n_send):
            step = sends[k].shape[1]
            copies.append(
                pltpu.make_async_copy(
                    done.at[slot, pl.ds(first, step)], sends[k].at[g], out_sems.at[slot, k]
                )
            )
            first = first + step
        return copies

    for copy in fetch(0, 0):
        copy.start()

    @pl.loop(0, tiles)
    def _(g):
        slot = g % 2

        @pl.when(g + 1 < tiles)
        def _():
            for copy in fetch(g + 1, 1 - slot):
                copy.start()

        for copy in fetch(g, slot):
            copy.wait()

        @pl.when(g >= 2)
        def _():
            for copy in store(g - 2, slot):
                copy.wait()

        rate = rate_ref[g]

        def rows_of(ref, e):
            return [ref[e, 8 * v : 8 * v + 8, :] for v in range(vregs)]

        def write_work(e, rows):
            for v in range(vregs):
                work[e, 8 * v : 8 * v + 8, :] = rows[v]

        def read_work(e):
            return rows_of(work, e)

        def read_field(e):
            return [field[slot, e, pl.ds(v, 8, stride=vregs), :] for v in range(vregs)]

        def write_done(e, rows):
            for v in range(vregs):
                done[slot, e - halo, pl.ds(v, 8, stride=vregs), :] = rows[v]

        def scaled(e):
            ra = [rate * x for x in rows_of(a_ref, e)]
            rb = [rate * x for x in rows_of(b_ref, e)]
            for v in range(vregs):
                ra_ref[e, 8 * v : 8 * v + 8, :] = ra[v]
                rb_ref[e, 8 * v : 8 * v + 8, :] = rb[v]
            return ra, rb

        def ready(e):
            return rows_of(ra_ref, e), rows_of(rb_ref, e)

        def sweep(first, count, read, write, rates, wide):
            def energy(e, here, below):
                after = read(e + 1)
                ra, rb = rates(e)
                above = [ra[v] * (after[v] - here[v]) for v in range(vregs)]
                nearby = here[1:] + [pltpu.roll(here[0], 7, 0)]
                pitch = [rb[v] * (nearby[v] - here[v]) for v in range(vregs)]
                before = [pltpu.roll(pitch[-1], 1, 0)] + pitch[:-1]
                write(
                    e,
                    [
                        here[v] + ((above[v] - below[v]) + (pitch[v] - before[v]))
                        for v in range(vregs)
                    ],
                )
                return after, above

            def several(e, carry, n):
                here, below = list(carry[:vregs]), list(carry[vregs:])
                for i in range(n):
                    here, below = energy(e + i, here, below)
                return (*here, *below)

            edge = read(first - 1)
            here = read(first)
            ra = rates(first - 1)[0]
            below = [ra[v] * (here[v] - edge[v]) for v in range(vregs)]
            carry = lax.fori_loop(
                0,
                count // wide,
                lambda i, carry: several(first + wide * i, carry, wide),
                (*here, *below),
            )
            for left in range(2, wide, 2):

                @pl.when(count % wide == left)
                def _(left=left):
                    several(first + count - left, carry, left)

        sweep(1, frame - 2, read_field, write_work, scaled, 2)

        @pl.loop(1, PASSES - 1)
        def _(n):
            sweep(n + 1, frame - 2 - 2 * n, read_work, write_work, ready, 4)

        sweep(PASSES, frame - 2 * PASSES, read_work, write_done, ready, 4)

        for copy in store(g, slot):
            copy.start()

    for g in range(max(0, tiles - 2), tiles):
        for copy in store(g, g % 2):
            copy.wait()


def diffuse(rate, a, b, own, got, own_halo, got_halo, steps):
    tiles, _, pitches, side = own[0].shape
    frame = a.shape[0]
    block = sum(steps)
    ins = [*own, *got, *own_halo, *got_halo]
    out = pl.pallas_call(
        functools.partial(diffusion_kernel, len(own), len(own_halo), len(steps)),
        out_shape=[
            jax.ShapeDtypeStruct((tiles, step, pitches, side), F32) for step in (block, *steps)
        ],
        in_specs=[VMEM] * 3 + [ANY] * len(ins),
        out_specs=[ANY] * (1 + len(steps)),
        scratch_shapes=[
            pltpu.VMEM((2, frame, pitches, side), F32),
            pltpu.VMEM((frame, pitches, side), F32),
            pltpu.VMEM((frame, pitches, side), F32),
            pltpu.VMEM((frame, pitches, side), F32),
            pltpu.VMEM((2, 2 * block, pitches, side), F32),
            pltpu.SemaphoreType.DMA((2, len(ins))),
            pltpu.SemaphoreType.DMA((2, len(steps) + 1)),
        ],
        compiler_params=params(),
        cost_estimate=cost(),
        name="diffuse_tiles",
    )(rate, a, b, *ins)
    return out[0], out[1:]


def across_lanes(window, side):
    frame, pitches = window.shape
    turned = window.reshape(frame, 8, pitches // 8).transpose(0, 2, 1).reshape(frame, pitches)
    return jnp.broadcast_to(turned[:, :, None], (frame, pitches, side))


def paired_shards(
    density,
    source_sector,
    source_tile,
    matrix_id,
    cubic_weights,
    bin_cells,
    wave_level,
    energy_rate,
    pitch_rate,
):
    sectors, inner = lax.axis_size("sector"), lax.axis_size("inner")
    inner_here = lax.axis_index("inner")
    flip, group = inner_here % 2, inner_here // 2
    block, pitches, cell_count = density.shape
    side = cubic_weights.shape[1]
    tiles = cell_count // side
    half = tiles // 2
    quarter = block // 4
    halo_chunks = PASSES // quarter
    first_steps = (quarter, quarter, quarter, quarter // 2, quarter - quarter // 2)
    last_steps = (quarter // 2, quarter, quarter, quarter - quarter // 4, block - 3 * quarter - quarter // 2 + quarter // 4)
    cap = slots(tiles, sectors)
    tables = (source_sector, source_tile)
    near, far = [1], list(range(2, sectors))

    weights = split_weights(matrix_id, cubic_weights)

    energies = energy_rate.shape[0]
    frame = 2 * block + 2 * PASSES
    energy_pad = jnp.pad(energy_rate[: energies - 1], ((PASSES, PASSES + 1), (0, 0)))
    pitch_pad = jnp.pad(pitch_rate[:, : pitches - 1], ((PASSES, PASSES), (0, 1)))
    first_energy = group * 2 * block
    a = across_lanes(lax.dynamic_slice_in_dim(energy_pad, first_energy, frame, 0), side)
    b = across_lanes(lax.dynamic_slice_in_dim(pitch_pad, first_energy, frame, 0), side)
    bin_ends = jnp.cumsum(bin_cells[0])
    cells = flip * (half * side) + jnp.arange(half * side, dtype=jnp.int32)
    bin_of = jnp.sum((bin_ends[None, :] <= cells[:, None]).astype(jnp.int32), axis=1)
    bins = jnp.arange(bin_ends.shape[0], dtype=jnp.int32)
    level = jnp.sum(jnp.where(bin_of[:, None] == bins[None, :], wave_level[0][None, :], 0.0), axis=1)
    rate = jnp.broadcast_to(level.reshape(half, 1, side), (half, 8, side))

    def at_lanes(t):
        return pl.ds(pl.multiple_of(t * side, side), side)

    def side_here():
        return lax.axis_index("inner") % 2

    swap = [(i, i ^ 1) for i in range(inner)]
    own_pairs, got_pairs = [], []
    for i in range(inner):
        for pairs, shift in ((own_pairs, -2 if i % 2 == 0 else 2), (got_pairs, 2 if i % 2 == 0 else -2)):
            if 0 <= i + shift < inner:
                pairs.append((i, i + shift))

    own, got, own_halo, got_halo = [], [], [], []
    packed = []
    start = 0
    for k, step in enumerate(first_steps):

        def first_of(start=start, step=step):
            here = side_here()
            return here * (block - start - step) + (1 - here) * start

        def find(field, first_of=first_of, step=step):
            first = first_of()
            return lambda t: [(t >= 0, lambda: field.at[pl.ds(first, step), :, at_lanes(t)])]

        def find_all(field):
            return lambda t: [(t >= 0, lambda: field.at[:, :, at_lanes(t)])]

        def receive(came, other, slot, first_of=first_of, step=step):
            return came.at[slot, pl.ds(first_of(), step)] if other == 1 else came.at[slot]

        def place(kept, sent):
            here = side_here()
            mine = lambda t: (t // half) == here
            return lambda t: [
                (mine(t), lambda: kept.at[t % half]),
                (jnp.logical_not(mine(t)), lambda: sent.at[t % half]),
            ]

        packed.append((start, step, find, receive, place))
        start += step

    def pack_first(k, after):
        start, step, find, _, _ = packed[k]
        groups = [(d, find, (step, pitches, side)) for d in far]
        if k == 0:
            groups += [(d, find_all, (block, pitches, side)) for d in near]
        return pack(groups, cap, tables, [density], after)

    sends = pack_first(0, ())
    beside = sector_exchange(sends[-1:], near)
    came = [sector_exchange(sends[:-1], far)]
    after_pack, token = sends[0], None
    for k, (start, step, find, receive, place) in enumerate(packed):
        if k + 1 < len(packed):
            queue(came, pack_first(k + 1, (after_pack,)), far)
            after_pack = came[k][0]
        if k == 1:
            came[k], (rate, a, b) = in_turn(came[k], [rate, a, b])
        part = jax.ShapeDtypeStruct((half, step, pitches, side), F32)
        piece = (step, pitches, side)
        after = () if token is None else (token,)
        kept, sent, token = drift(
            find, place, receive, tables, weights, [density], beside + came[k], [part, part], piece, after
        )
        own.append(kept)
        if k + 1 < len(packed):
            (sent, kept), (came[k + 1][0],) = in_turn([sent, kept], [came[k + 1][0]])
        if k > 0:
            (sent,), (got[k - 1],) = in_turn([sent], [got[k - 1]])
        got.append(lax.ppermute(sent, "inner", swap))
        if 0 < k <= halo_chunks:
            forward = got[k - 1]
            if k > 1:
                (forward,), (got_halo[k - 2],) = in_turn([forward], [got_halo[k - 2]])
            got_halo.append(lax.ppermute(forward, "inner", got_pairs))
        if k < halo_chunks:
            if k > 0:
                (kept,), (own_halo[k - 1],) = in_turn([kept], [own_halo[k - 1]])
            own_halo.append(lax.ppermute(kept, "inner", own_pairs))

    kept, sends = diffuse(rate, a, b, own, got, own_halo, got_halo, last_steps)

    returns, ready, out, start = sends, [], (), 0
    for k, step in enumerate(last_steps):

        def find(mine, theirs, start=start, step=step):
            here = side_here()
            return lambda t: [
                ((t // half) == here, lambda: mine.at[t % half, pl.ds(start, step)]),
                ((t // half) != here, lambda: theirs.at[t % half]),
            ]

        def place(result, start=start, step=step):
            return lambda t: [(t >= 0, lambda: result.at[pl.ds(start, step), :, at_lanes(t)])]

        ready.append((find, place, (step, pitches, side)))
        start += step

    def receive_slot(came, other, slot):
        return came.at[slot]

    def pack_last(k, after):
        find, _, piece = ready[k]
        sends = pack([(d, find, piece) for d in near + far], cap, tables, [kept, backs[k]], after)
        return sends[:1], sends[1:]

    whole = [jax.ShapeDtypeStruct(density.shape, F32)]
    backs = [lax.ppermute(returns[0], "inner", swap)]
    (last,), (backs[0],) = in_turn([returns[1]], [backs[0]])
    backs.append(lax.ppermute(last, "inner", swap))
    sends, far_sends = pack_last(0, ())
    came = [sector_exchange(far_sends, far)]
    beside = sector_exchange(sends, near)
    token = None
    for k, (find, place, piece) in enumerate(ready):
        after = [] if token is None else [token]
        if k + 1 < len(ready):
            sends, far_sends = pack_last(k + 1, after)
            queue(came, far_sends, far)
            beside_next = sector_exchange(sends, near)
        if k + 2 < len(ready):
            (last,), (backs[k + 1], *came[k]) = in_turn([returns[k + 2]], [backs[k + 1], *came[k]])
            backs.append(lax.ppermute(last, "inner", swap))
        *out, token = drift(
            find, place, receive_slot, tables, weights, [kept, backs[k]], beside + came[k], whole, piece, after, out
        )
        beside = beside_next
    return out[0]


def slots(tiles, sectors):
    return max(2, (3 * tiles + 2 * sectors - 1) // (2 * sectors))


def order_within(sources):
    tile_count = sources.shape[1]
    same = sources[:, :, None] == sources[:, None, :]
    earlier = jnp.arange(tile_count)[None, :] < jnp.arange(tile_count)[:, None]
    return jnp.sum((same & earlier[None]).astype(jnp.int32), axis=2)


def drift_step(density, source_sector, source_tile, matrix_id, cubic_weights):
    sectors = lax.axis_size("sector")
    sector_here = lax.axis_index("sector")
    energies, pitches, cell_count = density.shape
    tile_len = cubic_weights.shape[1]
    tile_count = cell_count // tile_len
    slot_count = max(2, (3 * tile_count + 2 * sectors - 1) // (2 * sectors))
    sources = source_sector[0]
    picked_tiles = source_tile[0]
    matrix_ids = matrix_id[0]
    tile_ranks = order_within(sources)
    slot_rank = jnp.arange(slot_count, dtype=jnp.int32)
    matched = (sources[:, None, :] == sector_here) & (
        tile_ranks[:, None, :] == slot_rank[None, :, None]
    )
    chosen = jnp.sum(jnp.where(matched, picked_tiles[:, None, :], 0), axis=2).reshape(-1)
    filled = jnp.any(matched, axis=2).reshape(-1).astype(jnp.float32)
    blocks = density.reshape(energies, pitches, tile_count, tile_len)
    outgoing = jnp.take(blocks, chosen, axis=2) * filled[None, None, :, None]
    incoming = lax.all_to_all(outgoing, "sector", split_axis=2, concat_axis=2, tiled=True)
    own_sources = sources[sector_here]
    own_ranks = tile_ranks[sector_here]
    own_ids = matrix_ids[sector_here]
    where_from = own_sources * slot_count + own_ranks
    departing = jnp.take(incoming, where_from, axis=2)
    matrices = jnp.take(cubic_weights, own_ids, axis=0)
    drifted = jnp.einsum("eptj,tij->epti", departing, matrices, precision=lax.Precision.HIGHEST)
    return drifted.reshape(energies, pitches, cell_count)


def one_pass(field, rate_cell, energy_rate, pitch_rate):
    flux_e = energy_rate[:-1, :, None] * (field[1:] - field[:-1])
    flux_p = pitch_rate[:, :-1, None] * (field[:, 1:] - field[:, :-1])
    change_e = jnp.pad(flux_e, ((0, 1), (0, 0), (0, 0))) - jnp.pad(flux_e, ((1, 0), (0, 0), (0, 0)))
    change_p = jnp.pad(flux_p, ((0, 0), (0, 1), (0, 0))) - jnp.pad(flux_p, ((0, 0), (1, 0), (0, 0)))
    return field + rate_cell[None, None, :] * (change_e + change_p)


def shards(
    density,
    source_sector,
    source_tile,
    matrix_id,
    cubic_weights,
    bin_cells,
    wave_level,
    energy_rate,
    pitch_rate,
):
    first = drift_step(density, source_sector, source_tile, matrix_id, cubic_weights)
    inner_count = lax.axis_size("inner")
    inner_here = lax.axis_index("inner")
    cell_count = first.shape[2]
    lengths = bin_cells[0]
    per_device = cell_count // inner_count
    owner_cells = jnp.full((inner_count,), per_device, jnp.int32)
    owner_ends = jnp.cumsum(owner_cells)
    owner_starts = owner_ends - owner_cells
    offsets = jnp.arange(per_device, dtype=jnp.int32)
    cell_index = owner_starts[:, None] + offsets[None, :]
    valid = (offsets[None, :] < owner_cells[:, None]).reshape(-1).astype(jnp.float32)
    clipped = jnp.minimum(cell_index, cell_count - 1).reshape(-1)
    packed = jnp.take(first, clipped, axis=2) * valid[None, None, :]
    cellwise = lax.all_to_all(packed, "inner", split_axis=2, concat_axis=0, tiled=True)
    bin_ends = jnp.cumsum(lengths)
    global_cells = owner_starts[inner_here] + offsets
    is_live = (offsets < owner_cells[inner_here]).astype(jnp.float32)
    bin_of = jnp.sum((bin_ends[None, :] <= global_cells[:, None]).astype(jnp.int32), axis=1)
    onehot = bin_of[:, None] == jnp.arange(inner_count, dtype=jnp.int32)[None, :]
    cell_level = jnp.sum(jnp.where(onehot, wave_level[0][None, :], 0.0), axis=1) * is_live

    def loop_body(step, current):
        return one_pass(current, cell_level, energy_rate, pitch_rate)

    diffused = lax.fori_loop(0, PASSES, loop_body, cellwise)
    returned = lax.all_to_all(diffused, "inner", split_axis=0, concat_axis=2, tiled=True)
    every_cell = jnp.arange(cell_count, dtype=jnp.int32)
    owner_index = jnp.sum((owner_ends[None, :] <= every_cell[:, None]).astype(jnp.int32), axis=1)
    offset = every_cell - owner_starts[owner_index]
    position = owner_index * per_device + offset
    restored = jnp.take(returned, position, axis=2)
    return drift_step(restored, source_sector, source_tile, matrix_id, cubic_weights)


def pairs_fit(mesh, energies, pitches, cells, side):
    sectors, inner = mesh.shape["sector"], mesh.shape["inner"]
    block = energies // inner
    tiles = cells // sectors // side
    return (
        sectors & (sectors - 1) == 0
        and inner % 2 == 0
        and tiles % 2 == 0
        and pitches % 16 == 0
        and side % 128 == 0
        and block % 16 == 0
        and 4 * PASSES == 3 * block
    )


def solution(mesh):
    specs = (
        P("inner", None, "sector"),
        P("inner", None, None),
        P("inner", None, None),
        P("inner", None, None),
        P(),
        P("sector", None),
        P("sector", None),
        P(),
        P(),
    )

    def whole(*arrays):
        energies, pitches, cells = arrays[0].shape
        fits = pairs_fit(mesh, energies, pitches, cells, arrays[4].shape[1])
        return jax.shard_map(
            paired_shards if fits else shards,
            mesh=mesh,
            in_specs=specs,
            out_specs=P("inner", None, "sector"),
            check_vma=False,
        )(*arrays)

    return whole
```

```python
import functools

import jax
import jax.numpy as jnp
from jax import lax
from jax.experimental import pallas as pl
from jax.experimental.pallas import tpu as pltpu
from jax.sharding import PartitionSpec as P

PASSES = 12
VMEM_LIMIT = 64 * 1024 * 1024 - 128 * 1024
ANY = pl.BlockSpec(memory_space=pltpu.HBM)
SMEM = pl.BlockSpec(memory_space=pltpu.SMEM)
VMEM = pl.BlockSpec(memory_space=pltpu.VMEM)
F32 = jnp.float32
BF16 = jnp.bfloat16


def params():
    return pltpu.CompilerParams(vmem_limit_bytes=VMEM_LIMIT)


def cost():
    return pl.CostEstimate(flops=0, bytes_accessed=1024, transcendentals=0)


def weights_kernel(mid_ref, w_ref, out_ref, raw, sems):
    tiles, side = raw.shape[0], raw.shape[1]
    me = lax.axis_index("sector")

    def copy(t):
        return pltpu.make_async_copy(w_ref.at[mid_ref[0, me, t]], raw.at[t], sems.at[t])

    @pl.loop(0, tiles)
    def _(t):
        copy(t).start()

    @pl.loop(0, tiles)
    def _(t):
        copy(t).wait()
        turned = jnp.transpose(raw[t])
        high = turned.astype(BF16)
        low = (turned - high.astype(F32)).astype(BF16)
        out_ref[t, :side, :side] = high
        out_ref[t, side:, :side] = high
        out_ref[t, :side, side:] = low
        out_ref[t, side:, side:] = jnp.zeros((side, side), BF16)


def split_weights(matrix_id, cubic_weights):
    tiles, side = matrix_id.shape[2], cubic_weights.shape[1]
    return pl.pallas_call(
        weights_kernel,
        out_shape=jax.ShapeDtypeStruct((tiles, 2 * side, 2 * side), BF16),
        in_specs=[SMEM, ANY],
        out_specs=VMEM,
        scratch_shapes=[
            pltpu.VMEM((tiles, side, side), F32),
            pltpu.SemaphoreType.DMA((tiles,)),
        ],
        compiler_params=params(),
        cost_estimate=cost(),
        name="split_weights",
    )(matrix_id, cubic_weights)


def pack_kernel(offsets, finds, n_far, n_arrays, sec_ref, til_ref, *refs):
    tiles, n = sec_ref.shape[2], len(offsets)
    near = n - n_far
    sends, rooms = refs[-n - 2 - (near + (n_far > 0)) : -n - 2], refs[-n - 2 : -2]
    if n_far:
        sends = [sends[0].at[i] for i in range(n_far)] + list(sends[1:])
    in_sems, out_sems = refs[-2:]
    me = lax.axis_index("sector")
    counts = []
    for i, d in enumerate(offsets):
        dest = me ^ d
        pieces = finds[i](*refs[:n_arrays])

        def body(t, count, i=i, dest=dest, pieces=pieces):
            hit = sec_ref[0, dest, t] == me

            @pl.when(hit)
            def _():
                for guard, piece in pieces(til_ref[0, dest, t]):

                    @pl.when(guard)
                    def _():
                        pltpu.make_async_copy(piece(), rooms[i].at[count], in_sems.at[i, count]).start()

            return count + hit.astype(jnp.int32)

        counts.append(lax.fori_loop(0, tiles, body, jnp.int32(0)))
    for i in range(n):

        @pl.loop(0, counts[i])
        def _(slot, i=i):
            here = rooms[i].at[slot]
            pltpu.make_async_copy(here, here, in_sems.at[i, slot]).wait()
            pltpu.make_async_copy(here, sends[i].at[slot], out_sems.at[i, slot]).start()

    for i in range(n):

        @pl.loop(0, counts[i])
        def _(slot, i=i):
            pltpu.make_async_copy(rooms[i].at[slot], sends[i].at[slot], out_sems.at[i, slot]).wait()


def pack(groups, cap, tables, arrays, after=()):
    n = len(groups)
    offsets, finds, shapes = zip(*groups)
    n_far = sum(d > 1 for d in offsets)
    outs = [(n_far, cap) + shapes[0]] * (n_far > 0) + [(cap,) + shape for shape in shapes[n_far:]]
    return pl.pallas_call(
        functools.partial(pack_kernel, offsets, finds, n_far, len(arrays)),
        out_shape=[jax.ShapeDtypeStruct(out, F32) for out in outs],
        in_specs=[SMEM, SMEM] + [ANY] * (len(arrays) + len(after)),
        out_specs=[ANY] * len(outs),
        scratch_shapes=[
            *[pltpu.VMEM((cap,) + shape, F32) for shape in shapes],
            pltpu.SemaphoreType.DMA((n, cap)),
            pltpu.SemaphoreType.DMA((n, cap)),
        ],
        compiler_params=params(),
        cost_estimate=cost(),
        name="pack_tiles",
    )(*tables, *arrays, *after)


def sector_exchange(sends, offsets):
    sectors = lax.axis_size("sector")
    return [
        lax.ppermute(send, "sector", [(s, s ^ d) for s in range(sectors)])
        for d, send in zip(offsets, sends)
    ]


def far_queue(came, send):
    if len(came) > 1:
        (send,), (came[-2][0],) = in_turn([send], [came[-2][0]])
    sectors = lax.axis_size("sector")
    whole = lax.ppermute(send, "sector", [(s, s ^ 2) for s in range(sectors)])
    came.append([whole, lax.ppermute(whole[1], "sector", [(s, s ^ 1) for s in range(sectors)])])


def in_turn(later, earlier):
    both = lax.optimization_barrier((*later, *earlier))
    return list(both[: len(later)]), list(both[len(later) :])


def drift_kernel(find, place, receive, n_local, n_extra, sec_ref, til_ref, w_ref, *refs):
    sectors, tiles = sec_ref.shape[1], sec_ref.shape[2]
    local, recvs = refs[:n_local], refs[n_local : n_local + sectors - 1]
    outs = refs[n_local + sectors - 1 + n_extra : -5]
    token, taken, made, in_sems, out_sems = refs[-5:]
    pieces = find(*local)
    put = place(*outs)
    me = lax.axis_index("sector")
    rows, side = taken.shape[1] * taken.shape[2], taken.shape[3]
    token[...] = jnp.zeros(token.shape, F32)

    def fetch(t, counts):
        d = sec_ref[0, me, t] ^ me

        @pl.when(d == 0)
        def _():
            for guard, piece in pieces(til_ref[0, me, t]):

                @pl.when(guard)
                def _():
                    pltpu.make_async_copy(piece(), taken.at[t], in_sems.at[t]).start()

        for other in range(1, sectors):

            @pl.when(d == other)
            def _(other=other):
                came = receive(recvs[other - 1], other, counts[other - 1])
                pltpu.make_async_copy(came, taken.at[t], in_sems.at[t]).start()

        return tuple(c + (d == i + 1).astype(jnp.int32) for i, c in enumerate(counts))

    lax.fori_loop(0, tiles, fetch, (jnp.int32(0),) * (sectors - 1))

    @pl.loop(0, tiles, unroll=4)
    def _(t):
        pltpu.make_async_copy(taken.at[t], taken.at[t], in_sems.at[t]).wait()
        value = taken[t].reshape(rows, side)
        high = value.astype(BF16)
        low = (value - high.astype(F32)).astype(BF16)
        both = jnp.dot(jnp.concatenate([high, low], axis=1), w_ref[t], preferred_element_type=F32)
        made[t] = (both[:, :side] + both[:, side:]).reshape(taken.shape[1:])
        for guard, there in put(t):

            @pl.when(guard)
            def _():
                pltpu.make_async_copy(made.at[t], there(), out_sems.at[t]).start()

    @pl.loop(0, tiles)
    def _(t):
        pltpu.make_async_copy(made.at[t], made.at[t], out_sems.at[t]).wait()


def drift(find, place, receive, tables, weights, local, recvs, outs, piece, after=(), carried=()):
    sectors, tiles = tables[0].shape[1], tables[0].shape[2]
    n_local = len(local)
    ins = [*tables, weights, *local, *recvs, *after, *carried]
    n_extra = len(after) + len(carried)
    return pl.pallas_call(
        functools.partial(drift_kernel, find, place, receive, n_local, n_extra),
        out_shape=[*outs, jax.ShapeDtypeStruct((8, 128), F32)],
        in_specs=[SMEM, SMEM, VMEM] + [ANY] * (len(ins) - 3),
        out_specs=[ANY] * len(outs) + [VMEM],
        scratch_shapes=[
            pltpu.VMEM((tiles,) + piece, F32),
            pltpu.VMEM((tiles,) + piece, F32),
            pltpu.SemaphoreType.DMA((tiles,)),
            pltpu.SemaphoreType.DMA((tiles,)),
        ],
        input_output_aliases={len(ins) - 1: 0} if carried else {},
        compiler_params=params(),
        cost_estimate=cost(),
        name="drift_chunk",
    )(*ins)


def diffusion_kernel(n_own, n_halo, n_send, rate_ref, a_ref, b_ref, *refs):
    n_in = 2 * n_own + 2 * n_halo
    ins, keep, sends = refs[:n_in], refs[n_in], refs[n_in + 1 : n_in + 1 + n_send]
    field, work, ra_ref, rb_ref, done, in_sems, out_sems = refs[n_in + 1 + n_send :]
    tiles, block = keep.shape[0], keep.shape[1]
    frame, pitches, side = work.shape
    halo = (frame - 2 * block) // 2
    vregs = pitches // 8
    flip = lax.axis_index("inner") % 2
    places, start = [], 0
    for i in range(n_own):
        step = ins[i].shape[1]
        places.append((i, step, halo + start))
        places.append((n_own + i, step, halo + 2 * block - start - step))
        if i < n_halo:
            places.append((2 * n_own + i, step, halo + 2 * block + start))
            places.append((2 * n_own + n_halo + i, step, halo - start - step))
        start += step

    def fetch(g, slot):
        copies = []
        for i, step, place in places:
            at = jnp.where(flip == 0, place, frame - place - step)
            copies.append(
                pltpu.make_async_copy(
                    ins[i].at[g], field.at[slot, pl.ds(at, step)], in_sems.at[slot, i]
                )
            )
        return copies

    def store(g, slot):
        copies = [
            pltpu.make_async_copy(
                done.at[slot, pl.ds(flip * block, block)], keep.at[g], out_sems.at[slot, n_send]
            )
        ]
        first = (1 - flip) * block
        for k in range(n_send):
            step = sends[k].shape[1]
            copies.append(
                pltpu.make_async_copy(
                    done.at[slot, pl.ds(first, step)], sends[k].at[g], out_sems.at[slot, k]
                )
            )
            first = first + step
        return copies

    for copy in fetch(0, 0):
        copy.start()

    @pl.loop(0, tiles)
    def _(g):
        slot = g % 2

        @pl.when(g + 1 < tiles)
        def _():
            for copy in fetch(g + 1, 1 - slot):
                copy.start()

        for copy in fetch(g, slot):
            copy.wait()

        @pl.when(g >= 2)
        def _():
            for copy in store(g - 2, slot):
                copy.wait()

        rate = rate_ref[g]

        def rows_of(ref, e):
            return [ref[e, 8 * v : 8 * v + 8, :] for v in range(vregs)]

        def write_work(e, rows):
            for v in range(vregs):
                work[e, 8 * v : 8 * v + 8, :] = rows[v]

        def read_work(e):
            return rows_of(work, e)

        def read_field(e):
            return [field[slot, e, pl.ds(v, 8, stride=vregs), :] for v in range(vregs)]

        def write_done(e, rows):
            for v in range(vregs):
                done[slot, e - halo, pl.ds(v, 8, stride=vregs), :] = rows[v]

        def scaled(e):
            ra = [rate * x for x in rows_of(a_ref, e)]
            rb = [rate * x for x in rows_of(b_ref, e)]
            for v in range(vregs):
                ra_ref[e, 8 * v : 8 * v + 8, :] = ra[v]
                rb_ref[e, 8 * v : 8 * v + 8, :] = rb[v]
            return ra, rb

        def ready(e):
            return rows_of(ra_ref, e), rows_of(rb_ref, e)

        def sweep(first, count, read, write, rates, wide):
            def energy(e, here, below):
                after = read(e + 1)
                ra, rb = rates(e)
                above = [ra[v] * (after[v] - here[v]) for v in range(vregs)]
                nearby = here[1:] + [pltpu.roll(here[0], 7, 0)]
                pitch = [rb[v] * (nearby[v] - here[v]) for v in range(vregs)]
                before = [pltpu.roll(pitch[-1], 1, 0)] + pitch[:-1]
                write(
                    e,
                    [
                        here[v] + ((above[v] - below[v]) + (pitch[v] - before[v]))
                        for v in range(vregs)
                    ],
                )
                return after, above

            def several(e, carry, n):
                here, below = list(carry[:vregs]), list(carry[vregs:])
                for i in range(n):
                    here, below = energy(e + i, here, below)
                return (*here, *below)

            edge = read(first - 1)
            here = read(first)
            ra = rates(first - 1)[0]
            below = [ra[v] * (here[v] - edge[v]) for v in range(vregs)]
            carry = lax.fori_loop(
                0,
                count // wide,
                lambda i, carry: several(first + wide * i, carry, wide),
                (*here, *below),
            )
            for left in range(2, wide, 2):

                @pl.when(count % wide == left)
                def _(left=left):
                    several(first + count - left, carry, left)

        sweep(1, frame - 2, read_field, write_work, scaled, 2)

        @pl.loop(1, PASSES - 1)
        def _(n):
            sweep(n + 1, frame - 2 - 2 * n, read_work, write_work, ready, 4)

        sweep(PASSES, frame - 2 * PASSES, read_work, write_done, ready, 4)

        for copy in store(g, slot):
            copy.start()

    for g in range(max(0, tiles - 2), tiles):
        for copy in store(g, g % 2):
            copy.wait()


def diffuse(rate, a, b, own, got, own_halo, got_halo, steps):
    tiles, _, pitches, side = own[0].shape
    frame = a.shape[0]
    block = sum(steps)
    ins = [*own, *got, *own_halo, *got_halo]
    out = pl.pallas_call(
        functools.partial(diffusion_kernel, len(own), len(own_halo), len(steps)),
        out_shape=[
            jax.ShapeDtypeStruct((tiles, step, pitches, side), F32) for step in (block, *steps)
        ],
        in_specs=[VMEM] * 3 + [ANY] * len(ins),
        out_specs=[ANY] * (1 + len(steps)),
        scratch_shapes=[
            pltpu.VMEM((2, frame, pitches, side), F32),
            pltpu.VMEM((frame, pitches, side), F32),
            pltpu.VMEM((frame, pitches, side), F32),
            pltpu.VMEM((frame, pitches, side), F32),
            pltpu.VMEM((2, 2 * block, pitches, side), F32),
            pltpu.SemaphoreType.DMA((2, len(ins))),
            pltpu.SemaphoreType.DMA((2, len(steps) + 1)),
        ],
        compiler_params=params(),
        cost_estimate=cost(),
        name="diffuse_tiles",
    )(rate, a, b, *ins)
    return out[0], out[1:]


def across_lanes(window, side):
    frame, pitches = window.shape
    turned = window.reshape(frame, 8, pitches // 8).transpose(0, 2, 1).reshape(frame, pitches)
    return jnp.broadcast_to(turned[:, :, None], (frame, pitches, side))


def paired_shards(
    density,
    source_sector,
    source_tile,
    matrix_id,
    cubic_weights,
    bin_cells,
    wave_level,
    energy_rate,
    pitch_rate,
):
    sectors, inner = lax.axis_size("sector"), lax.axis_size("inner")
    inner_here = lax.axis_index("inner")
    flip, group = inner_here % 2, inner_here // 2
    block, pitches, cell_count = density.shape
    side = cubic_weights.shape[1]
    tiles = cell_count // side
    half = tiles // 2
    quarter = block // 4
    first_steps = (quarter, quarter, quarter, quarter // 2, quarter - quarter // 2)
    halo_chunks = PASSES // quarter
    less = quarter - quarter // 4
    last_steps = (less, quarter, block - quarter - 2 * less, less)
    cap = slots(tiles, sectors)
    tables = (source_sector, source_tile)
    near, far = [1], list(range(2, sectors))

    weights = split_weights(matrix_id, cubic_weights)

    energies = energy_rate.shape[0]
    frame = 2 * block + 2 * PASSES
    energy_pad = jnp.pad(energy_rate[: energies - 1], ((PASSES, PASSES + 1), (0, 0)))
    pitch_pad = jnp.pad(pitch_rate[:, : pitches - 1], ((PASSES, PASSES), (0, 1)))
    first_energy = group * 2 * block
    a = across_lanes(lax.dynamic_slice_in_dim(energy_pad, first_energy, frame, 0), side)
    b = across_lanes(lax.dynamic_slice_in_dim(pitch_pad, first_energy, frame, 0), side)
    bin_ends = jnp.cumsum(bin_cells[0])
    cells = flip * (half * side) + jnp.arange(half * side, dtype=jnp.int32)
    bin_of = jnp.sum((bin_ends[None, :] <= cells[:, None]).astype(jnp.int32), axis=1)
    bins = jnp.arange(bin_ends.shape[0], dtype=jnp.int32)
    level = jnp.sum(jnp.where(bin_of[:, None] == bins[None, :], wave_level[0][None, :], 0.0), axis=1)
    rate = jnp.broadcast_to(level.reshape(half, 1, side), (half, 8, side))

    def at_lanes(t):
        return pl.ds(pl.multiple_of(t * side, side), side)

    def side_here():
        return lax.axis_index("inner") % 2

    swap = [(i, i ^ 1) for i in range(inner)]
    own_pairs, got_pairs = [], []
    for i in range(inner):
        for pairs, shift in ((own_pairs, -2 if i % 2 == 0 else 2), (got_pairs, 2 if i % 2 == 0 else -2)):
            if 0 <= i + shift < inner:
                pairs.append((i, i + shift))

    own, got, own_halo, got_halo = [], [], [], []
    packed = []
    start = 0
    for k, step in enumerate(first_steps):

        def first_of(start=start, step=step):
            here = side_here()
            return here * (block - start - step) + (1 - here) * start

        def find(field, first_of=first_of, step=step):
            first = first_of()
            return lambda t: [(t >= 0, lambda: field.at[pl.ds(first, step), :, at_lanes(t)])]

        def find_all(field):
            return lambda t: [(t >= 0, lambda: field.at[:, :, at_lanes(t)])]

        def receive(came, other, slot, first_of=first_of, step=step):
            if other == 2:
                return came.at[0, slot]
            return came.at[slot, pl.ds(first_of(), step)] if other == 1 else came.at[slot]

        def place(kept, sent):
            here = side_here()
            mine = lambda t: (t // half) == here
            return lambda t: [
                (mine(t), lambda: kept.at[t % half]),
                (jnp.logical_not(mine(t)), lambda: sent.at[t % half]),
            ]

        packed.append((start, step, find, receive, place))
        start += step

    def pack_first(k, after):
        start, step, find, _, _ = packed[k]
        groups = [(d, find, (step, pitches, side)) for d in far]
        if k == 0:
            groups += [(d, find_all, (block, pitches, side)) for d in near]
        return pack(groups, cap, tables, [density], after)

    sends = pack_first(0, ())
    beside = sector_exchange(sends[-1:], near)
    came = []
    far_queue(came, sends[0])
    token, tokens = None, []
    for k, (start, step, find, receive, place) in enumerate(packed):
        if k + 1 < len(packed):
            before = tokens[k - 1] if k else sends[0]
            far_queue(came, pack_first(k + 1, (before,))[0])
        if k == 1:
            came[k], (rate, a, b) = in_turn(came[k], [rate, a, b])
        part = jax.ShapeDtypeStruct((half, step, pitches, side), F32)
        piece = (step, pitches, side)
        after = [] if token is None else [token]
        kept, sent, token = drift(
            find, place, receive, tables, weights, [density], beside + came[k], [part, part], piece, after
        )
        tokens.append(token)
        own.append(kept)
        if k > 0:
            (sent,), (got[k - 1],) = in_turn([sent], [got[k - 1]])
        got.append(lax.ppermute(sent, "inner", swap))
        if 0 < k <= halo_chunks:
            forward = got[k - 1]
            if k > 1:
                (forward,), (got_halo[k - 2],) = in_turn([forward], [got_halo[k - 2]])
            got_halo.append(lax.ppermute(forward, "inner", got_pairs))
        if k < halo_chunks:
            if k > 0:
                (kept,), (own_halo[k - 1],) = in_turn([kept], [own_halo[k - 1]])
            own_halo.append(lax.ppermute(kept, "inner", own_pairs))

    kept, sends = diffuse(rate, a, b, own, got, own_halo, got_halo, last_steps)

    returns, ready, out, start = sends, [], (), 0
    for k, step in enumerate(last_steps):

        def find(mine, theirs, start=start, step=step):
            here = side_here()
            return lambda t: [
                ((t // half) == here, lambda: mine.at[t % half, pl.ds(start, step)]),
                ((t // half) != here, lambda: theirs.at[t % half]),
            ]

        def place(result, start=start, step=step):
            return lambda t: [(t >= 0, lambda: result.at[pl.ds(start, step), :, at_lanes(t)])]

        ready.append((find, place, (step, pitches, side)))
        start += step

    def receive_slot(came, other, slot):
        return came.at[0, slot] if other == 2 else came.at[slot]

    def pack_last(k, after):
        find, _, piece = ready[k]
        sends = pack([(d, find, piece) for d in far + near], cap, tables, [kept, backs[k]], after)
        return sends[1:], sends[0]

    whole = [jax.ShapeDtypeStruct(density.shape, F32)]
    backs = [lax.ppermute(returns[0], "inner", swap)]
    (last,), (backs[0],) = in_turn([returns[1]], [backs[0]])
    backs.append(lax.ppermute(last, "inner", swap))
    sends, far_sends = pack_last(0, ())
    came = []
    far_queue(came, far_sends)
    beside = sector_exchange(sends, near)
    token = None
    for k, (find, place, piece) in enumerate(ready):
        after = [] if token is None else [token]
        if k + 1 < len(ready):
            sends, far_sends = pack_last(k + 1, after)
            far_queue(came, far_sends)
            beside_next = sector_exchange(sends, near)
        if k + 2 < len(ready):
            (last,), (backs[k + 1], came[k][0]) = in_turn([returns[k + 2]], [backs[k + 1], came[k][0]])
            backs.append(lax.ppermute(last, "inner", swap))
        *out, token = drift(
            find, place, receive_slot, tables, weights, [kept, backs[k]], beside + came[k], whole, piece, after, out
        )
        beside = beside_next
    return out[0]


def slots(tiles, sectors):
    return max(2, (3 * tiles + 2 * sectors - 1) // (2 * sectors))


def order_within(sources):
    tile_count = sources.shape[1]
    same = sources[:, :, None] == sources[:, None, :]
    earlier = jnp.arange(tile_count)[None, :] < jnp.arange(tile_count)[:, None]
    return jnp.sum((same & earlier[None]).astype(jnp.int32), axis=2)


def drift_step(density, source_sector, source_tile, matrix_id, cubic_weights):
    sectors = lax.axis_size("sector")
    sector_here = lax.axis_index("sector")
    energies, pitches, cell_count = density.shape
    tile_len = cubic_weights.shape[1]
    tile_count = cell_count // tile_len
    slot_count = max(2, (3 * tile_count + 2 * sectors - 1) // (2 * sectors))
    sources = source_sector[0]
    picked_tiles = source_tile[0]
    matrix_ids = matrix_id[0]
    tile_ranks = order_within(sources)
    slot_rank = jnp.arange(slot_count, dtype=jnp.int32)
    matched = (sources[:, None, :] == sector_here) & (
        tile_ranks[:, None, :] == slot_rank[None, :, None]
    )
    chosen = jnp.sum(jnp.where(matched, picked_tiles[:, None, :], 0), axis=2).reshape(-1)
    filled = jnp.any(matched, axis=2).reshape(-1).astype(jnp.float32)
    blocks = density.reshape(energies, pitches, tile_count, tile_len)
    outgoing = jnp.take(blocks, chosen, axis=2) * filled[None, None, :, None]
    incoming = lax.all_to_all(outgoing, "sector", split_axis=2, concat_axis=2, tiled=True)
    own_sources = sources[sector_here]
    own_ranks = tile_ranks[sector_here]
    own_ids = matrix_ids[sector_here]
    where_from = own_sources * slot_count + own_ranks
    departing = jnp.take(incoming, where_from, axis=2)
    matrices = jnp.take(cubic_weights, own_ids, axis=0)
    drifted = jnp.einsum("eptj,tij->epti", departing, matrices, precision=lax.Precision.HIGHEST)
    return drifted.reshape(energies, pitches, cell_count)


def one_pass(field, rate_cell, energy_rate, pitch_rate):
    flux_e = energy_rate[:-1, :, None] * (field[1:] - field[:-1])
    flux_p = pitch_rate[:, :-1, None] * (field[:, 1:] - field[:, :-1])
    change_e = jnp.pad(flux_e, ((0, 1), (0, 0), (0, 0))) - jnp.pad(flux_e, ((1, 0), (0, 0), (0, 0)))
    change_p = jnp.pad(flux_p, ((0, 0), (0, 1), (0, 0))) - jnp.pad(flux_p, ((0, 0), (1, 0), (0, 0)))
    return field + rate_cell[None, None, :] * (change_e + change_p)


def shards(
    density,
    source_sector,
    source_tile,
    matrix_id,
    cubic_weights,
    bin_cells,
    wave_level,
    energy_rate,
    pitch_rate,
):
    first = drift_step(density, source_sector, source_tile, matrix_id, cubic_weights)
    inner_count = lax.axis_size("inner")
    inner_here = lax.axis_index("inner")
    cell_count = first.shape[2]
    lengths = bin_cells[0]
    per_device = cell_count // inner_count
    owner_cells = jnp.full((inner_count,), per_device, jnp.int32)
    owner_ends = jnp.cumsum(owner_cells)
    owner_starts = owner_ends - owner_cells
    offsets = jnp.arange(per_device, dtype=jnp.int32)
    cell_index = owner_starts[:, None] + offsets[None, :]
    valid = (offsets[None, :] < owner_cells[:, None]).reshape(-1).astype(jnp.float32)
    clipped = jnp.minimum(cell_index, cell_count - 1).reshape(-1)
    packed = jnp.take(first, clipped, axis=2) * valid[None, None, :]
    cellwise = lax.all_to_all(packed, "inner", split_axis=2, concat_axis=0, tiled=True)
    bin_ends = jnp.cumsum(lengths)
    global_cells = owner_starts[inner_here] + offsets
    is_live = (offsets < owner_cells[inner_here]).astype(jnp.float32)
    bin_of = jnp.sum((bin_ends[None, :] <= global_cells[:, None]).astype(jnp.int32), axis=1)
    onehot = bin_of[:, None] == jnp.arange(inner_count, dtype=jnp.int32)[None, :]
    cell_level = jnp.sum(jnp.where(onehot, wave_level[0][None, :], 0.0), axis=1) * is_live

    def loop_body(step, current):
        return one_pass(current, cell_level, energy_rate, pitch_rate)

    diffused = lax.fori_loop(0, PASSES, loop_body, cellwise)
    returned = lax.all_to_all(diffused, "inner", split_axis=0, concat_axis=2, tiled=True)
    every_cell = jnp.arange(cell_count, dtype=jnp.int32)
    owner_index = jnp.sum((owner_ends[None, :] <= every_cell[:, None]).astype(jnp.int32), axis=1)
    offset = every_cell - owner_starts[owner_index]
    position = owner_index * per_device + offset
    restored = jnp.take(returned, position, axis=2)
    return drift_step(restored, source_sector, source_tile, matrix_id, cubic_weights)


def pairs_fit(mesh, energies, pitches, cells, side):
    sectors, inner = mesh.shape["sector"], mesh.shape["inner"]
    block = energies // inner
    tiles = cells // sectors // side
    return (
        sectors == 4
        and inner % 2 == 0
        and tiles % 4 == 0
        and pitches % 16 == 0
        and side % 128 == 0
        and block % 16 == 0
        and 4 * PASSES == 3 * block
    )


def solution(mesh):
    specs = (
        P("inner", None, "sector"),
        P("inner", None, None),
        P("inner", None, None),
        P("inner", None, None),
        P(),
        P("sector", None),
        P("sector", None),
        P(),
        P(),
    )

    def whole(*arrays):
        energies, pitches, cells = arrays[0].shape
        fits = pairs_fit(mesh, energies, pitches, cells, arrays[4].shape[1])
        return jax.shard_map(
            paired_shards if fits else shards,
            mesh=mesh,
            in_specs=specs,
            out_specs=P("inner", None, "sector"),
            check_vma=False,
        )(*arrays)

    return whole
```

```python
import functools

import jax
import jax.numpy as jnp
from jax import lax
from jax.experimental import pallas as pl
from jax.experimental.pallas import tpu as pltpu
from jax.sharding import PartitionSpec as P

PASSES = 12
VMEM_LIMIT = 64 * 1024 * 1024 - 128 * 1024
ANY = pl.BlockSpec(memory_space=pltpu.HBM)
SMEM = pl.BlockSpec(memory_space=pltpu.SMEM)
VMEM = pl.BlockSpec(memory_space=pltpu.VMEM)
F32 = jnp.float32
BF16 = jnp.bfloat16


def params():
    return pltpu.CompilerParams(vmem_limit_bytes=VMEM_LIMIT)


def cost():
    return pl.CostEstimate(flops=0, bytes_accessed=1024, transcendentals=0)


def weights_kernel(mid_ref, w_ref, out_ref, raw, sems):
    tiles, side = raw.shape[0], raw.shape[1]
    me = lax.axis_index("sector")

    def copy(t):
        return pltpu.make_async_copy(w_ref.at[mid_ref[0, me, t]], raw.at[t], sems.at[t])

    @pl.loop(0, tiles)
    def _(t):
        copy(t).start()

    @pl.loop(0, tiles)
    def _(t):
        copy(t).wait()
        turned = jnp.transpose(raw[t])
        high = turned.astype(BF16)
        low = (turned - high.astype(F32)).astype(BF16)
        out_ref[t, :side, :side] = high
        out_ref[t, side:, :side] = high
        out_ref[t, :side, side:] = low
        out_ref[t, side:, side:] = jnp.zeros((side, side), BF16)


def split_weights(matrix_id, cubic_weights):
    tiles, side = matrix_id.shape[2], cubic_weights.shape[1]
    return pl.pallas_call(
        weights_kernel,
        out_shape=jax.ShapeDtypeStruct((tiles, 2 * side, 2 * side), BF16),
        in_specs=[SMEM, ANY],
        out_specs=VMEM,
        scratch_shapes=[
            pltpu.VMEM((tiles, side, side), F32),
            pltpu.SemaphoreType.DMA((tiles,)),
        ],
        compiler_params=params(),
        cost_estimate=cost(),
        name="split_weights",
    )(matrix_id, cubic_weights)


def pack_kernel(offsets, finds, n_far, n_arrays, sec_ref, til_ref, *refs):
    tiles, n = sec_ref.shape[2], len(offsets)
    near = n - n_far
    sends, rooms = refs[-n - 2 - (near + (n_far > 0)) : -n - 2], refs[-n - 2 : -2]
    if n_far:
        sends = [sends[0].at[i] for i in range(n_far)] + list(sends[1:])
    in_sems, out_sems = refs[-2:]
    me = lax.axis_index("sector")
    counts = []
    for i, d in enumerate(offsets):
        dest = me ^ d
        pieces = finds[i](*refs[:n_arrays])

        def body(t, count, i=i, dest=dest, pieces=pieces):
            hit = sec_ref[0, dest, t] == me

            @pl.when(hit)
            def _():
                for guard, piece in pieces(til_ref[0, dest, t]):

                    @pl.when(guard)
                    def _():
                        pltpu.make_async_copy(piece(), rooms[i].at[count], in_sems.at[i, count]).start()

            return count + hit.astype(jnp.int32)

        counts.append(lax.fori_loop(0, tiles, body, jnp.int32(0)))
    for i in range(n):

        @pl.loop(0, counts[i])
        def _(slot, i=i):
            here = rooms[i].at[slot]
            pltpu.make_async_copy(here, here, in_sems.at[i, slot]).wait()
            pltpu.make_async_copy(here, sends[i].at[slot], out_sems.at[i, slot]).start()

    for i in range(n):

        @pl.loop(0, counts[i])
        def _(slot, i=i):
            pltpu.make_async_copy(rooms[i].at[slot], sends[i].at[slot], out_sems.at[i, slot]).wait()


def pack(groups, cap, tables, arrays, after=()):
    n = len(groups)
    offsets, finds, shapes = zip(*groups)
    n_far = sum(d > 1 for d in offsets)
    outs = [(n_far, cap) + shapes[0]] * (n_far > 0) + [(cap,) + shape for shape in shapes[n_far:]]
    return pl.pallas_call(
        functools.partial(pack_kernel, offsets, finds, n_far, len(arrays)),
        out_shape=[jax.ShapeDtypeStruct(out, F32) for out in outs],
        in_specs=[SMEM, SMEM] + [ANY] * (len(arrays) + len(after)),
        out_specs=[ANY] * len(outs),
        scratch_shapes=[
            *[pltpu.VMEM((cap,) + shape, F32) for shape in shapes],
            pltpu.SemaphoreType.DMA((n, cap)),
            pltpu.SemaphoreType.DMA((n, cap)),
        ],
        compiler_params=params(),
        cost_estimate=cost(),
        name="pack_tiles",
    )(*tables, *arrays, *after)


def sector_exchange(sends, offsets):
    sectors = lax.axis_size("sector")
    return [
        lax.ppermute(send, "sector", [(s, s ^ d) for s in range(sectors)])
        for d, send in zip(offsets, sends)
    ]


def far_queue(came, send):
    if len(came) > 1:
        (send,), (came[-2][0],) = in_turn([send], [came[-2][0]])
    sectors = lax.axis_size("sector")
    whole = lax.ppermute(send, "sector", [(s, s ^ 2) for s in range(sectors)])
    came.append([whole, lax.ppermute(whole[1], "sector", [(s, s ^ 1) for s in range(sectors)])])


def in_turn(later, earlier):
    both = lax.optimization_barrier((*later, *earlier))
    return list(both[: len(later)]), list(both[len(later) :])


def drift_kernel(find, place, receive, n_local, n_extra, sec_ref, til_ref, w_ref, *refs):
    sectors, tiles = sec_ref.shape[1], sec_ref.shape[2]
    local, recvs = refs[:n_local], refs[n_local : n_local + sectors - 1]
    outs = refs[n_local + sectors - 1 + n_extra : -5]
    token, taken, made, in_sems, out_sems = refs[-5:]
    pieces = find(*local)
    put = place(*outs)
    me = lax.axis_index("sector")
    rows, side = taken.shape[1] * taken.shape[2], taken.shape[3]
    token[...] = jnp.zeros(token.shape, F32)

    def fetch(t, counts):
        d = sec_ref[0, me, t] ^ me

        @pl.when(d == 0)
        def _():
            for guard, piece in pieces(til_ref[0, me, t]):

                @pl.when(guard)
                def _():
                    pltpu.make_async_copy(piece(), taken.at[t], in_sems.at[t]).start()

        for other in range(1, sectors):

            @pl.when(d == other)
            def _(other=other):
                came = receive(recvs[other - 1], other, counts[other - 1])
                pltpu.make_async_copy(came, taken.at[t], in_sems.at[t]).start()

        return tuple(c + (d == i + 1).astype(jnp.int32) for i, c in enumerate(counts))

    lax.fori_loop(0, tiles, fetch, (jnp.int32(0),) * (sectors - 1))

    @pl.loop(0, tiles, unroll=4)
    def _(t):
        pltpu.make_async_copy(taken.at[t], taken.at[t], in_sems.at[t]).wait()
        value = taken[t].reshape(rows, side)
        high = value.astype(BF16)
        low = (value - high.astype(F32)).astype(BF16)
        both = jnp.dot(jnp.concatenate([high, low], axis=1), w_ref[t], preferred_element_type=F32)
        made[t] = (both[:, :side] + both[:, side:]).reshape(taken.shape[1:])
        for guard, there in put(t):

            @pl.when(guard)
            def _():
                pltpu.make_async_copy(made.at[t], there(), out_sems.at[t]).start()

    @pl.loop(0, tiles)
    def _(t):
        pltpu.make_async_copy(made.at[t], made.at[t], out_sems.at[t]).wait()


def drift(find, place, receive, tables, weights, local, recvs, outs, piece, after=(), carried=()):
    sectors, tiles = tables[0].shape[1], tables[0].shape[2]
    n_local = len(local)
    ins = [*tables, weights, *local, *recvs, *after, *carried]
    n_extra = len(after) + len(carried)
    return pl.pallas_call(
        functools.partial(drift_kernel, find, place, receive, n_local, n_extra),
        out_shape=[*outs, jax.ShapeDtypeStruct((8, 128), F32)],
        in_specs=[SMEM, SMEM, VMEM] + [ANY] * (len(ins) - 3),
        out_specs=[ANY] * len(outs) + [VMEM],
        scratch_shapes=[
            pltpu.VMEM((tiles,) + piece, F32),
            pltpu.VMEM((tiles,) + piece, F32),
            pltpu.SemaphoreType.DMA((tiles,)),
            pltpu.SemaphoreType.DMA((tiles,)),
        ],
        input_output_aliases={len(ins) - 1: 0} if carried else {},
        compiler_params=params(),
        cost_estimate=cost(),
        name="drift_chunk",
    )(*ins)


def diffusion_kernel(n_own, n_halo, n_send, rate_ref, a_ref, b_ref, *refs):
    n_in = 2 * n_own + 2 * n_halo
    ins, keep, sends = refs[:n_in], refs[n_in], refs[n_in + 1 : n_in + 1 + n_send]
    field, work, done, in_sems, out_sems = refs[n_in + 1 + n_send :]
    tiles, block = keep.shape[0], keep.shape[1]
    pair, frame, pitches, side = work.shape
    halo = (frame - 2 * block) // 2
    vregs = pitches // 8
    flip = lax.axis_index("inner") % 2
    places, start = [], 0
    for i in range(n_own):
        step = ins[i].shape[1]
        places.append((i, step, halo + start))
        places.append((n_own + i, step, halo + 2 * block - start - step))
        if i < n_halo:
            places.append((2 * n_own + i, step, halo + 2 * block + start))
            places.append((2 * n_own + n_halo + i, step, halo - start - step))
        start += step

    def fetch(g, slot):
        copies = []
        for i, step, place in places:
            at = jnp.where(flip == 0, place, frame - place - step)
            copies.append(
                pltpu.make_async_copy(
                    ins[i].at[pl.ds(pair * g, pair)],
                    field.at[slot, :, pl.ds(at, step)],
                    in_sems.at[slot, i],
                )
            )
        return copies

    def store(g, slot):
        these = pl.ds(pair * g, pair)
        copies = [
            pltpu.make_async_copy(
                done.at[slot, :, pl.ds(flip * block, block)],
                keep.at[these],
                out_sems.at[slot, n_send],
            )
        ]
        first = (1 - flip) * block
        for k in range(n_send):
            step = sends[k].shape[1]
            copies.append(
                pltpu.make_async_copy(
                    done.at[slot, :, pl.ds(first, step)], sends[k].at[these], out_sems.at[slot, k]
                )
            )
            first = first + step
        return copies

    rounds = tiles // pair
    both = range(pair)
    for copy in fetch(0, 0):
        copy.start()

    @pl.loop(0, rounds)
    def _(g):
        slot = g % 2

        @pl.when(g + 1 < rounds)
        def _():
            for copy in fetch(g + 1, 1 - slot):
                copy.start()

        for copy in fetch(g, slot):
            copy.wait()

        @pl.when(g >= 2)
        def _():
            for copy in store(g - 2, slot):
                copy.wait()

        rate = [rate_ref[pair * g + i] for i in both]

        def read_work(i, e, v):
            return work[i, e, 8 * v : 8 * v + 8, :]

        def write_work(i, e, v, value):
            work[i, e, 8 * v : 8 * v + 8, :] = value

        def read_field(i, e, v):
            return field[slot, i, e, pl.ds(v, 8, stride=vregs), :]

        def write_done(i, e, v, value):
            done[slot, i, e - halo, pl.ds(v, 8, stride=vregs), :] = value

        def sweep(first, count, read, write):
            def energy(e, here, below):
                after = [[None] * vregs for _ in both]
                above = [[None] * vregs for _ in both]
                pitch = [[None] * vregs for _ in both]
                turned = [pltpu.roll(here[i][0], 7, 0) for i in both]
                for v in reversed(range(vregs)):
                    a_rate = a_ref[e, 8 * v : 8 * v + 8, :]
                    b_rate = b_ref[e, 8 * v : 8 * v + 8, :]
                    for i in both:
                        after[i][v] = read(i, e + 1, v)
                        above[i][v] = a_rate * (after[i][v] - here[i][v])
                        nearby = here[i][v + 1] if v + 1 < vregs else turned[i]
                        pitch[i][v] = b_rate * (nearby - here[i][v])
                        if v + 1 < vregs:
                            change = (above[i][v + 1] - below[i][v + 1]) + (pitch[i][v + 1] - pitch[i][v])
                            write(i, e, v + 1, here[i][v + 1] + rate[i] * change)
                for i in both:
                    before = pltpu.roll(pitch[i][-1], 1, 0)
                    change = (above[i][0] - below[i][0]) + (pitch[i][0] - before)
                    write(i, e, 0, here[i][0] + rate[i] * change)
                return after, above

            def two(j, carry):
                rows = [list(carry[vregs * i : vregs * (i + 1)]) for i in range(2 * pair)]
                here, below = rows[:pair], rows[pair:]
                e = first + 2 * j
                here, below = energy(e, here, below)
                here, below = energy(e + 1, here, below)
                return tuple(x for row in here + below for x in row)

            here = [[read(i, first, v) for v in range(vregs)] for i in both]
            below = [
                [
                    a_ref[first - 1, 8 * v : 8 * v + 8, :] * (here[i][v] - read(i, first - 1, v))
                    for v in range(vregs)
                ]
                for i in both
            ]
            lax.fori_loop(0, count // 2, two, tuple(x for row in here + below for x in row))

        sweep(1, frame - 2, read_field, write_work)

        @pl.loop(1, PASSES - 1)
        def _(n):
            sweep(n + 1, frame - 2 - 2 * n, read_work, write_work)

        sweep(PASSES, frame - 2 * PASSES, read_work, write_done)

        for copy in store(g, slot):
            copy.start()

    for g in range(max(0, rounds - 2), rounds):
        for copy in store(g, g % 2):
            copy.wait()


def diffuse(rate, a, b, own, got, own_halo, got_halo, steps):
    tiles, _, pitches, side = own[0].shape
    frame = a.shape[0]
    block = sum(steps)
    ins = [*own, *got, *own_halo, *got_halo]
    out = pl.pallas_call(
        functools.partial(diffusion_kernel, len(own), len(own_halo), len(steps)),
        out_shape=[
            jax.ShapeDtypeStruct((tiles, step, pitches, side), F32) for step in (block, *steps)
        ],
        in_specs=[VMEM] * 3 + [ANY] * len(ins),
        out_specs=[ANY] * (1 + len(steps)),
        scratch_shapes=[
            pltpu.VMEM((2, 2, frame, pitches, side), F32),
            pltpu.VMEM((2, frame, pitches, side), F32),
            pltpu.VMEM((2, 2, 2 * block, pitches, side), F32),
            pltpu.SemaphoreType.DMA((2, len(ins))),
            pltpu.SemaphoreType.DMA((2, len(steps) + 1)),
        ],
        compiler_params=params(),
        cost_estimate=cost(),
        name="diffuse_tiles",
    )(rate, a, b, *ins)
    return out[0], out[1:]


def across_lanes(window, side):
    frame, pitches = window.shape
    turned = window.reshape(frame, 8, pitches // 8).transpose(0, 2, 1).reshape(frame, pitches)
    return jnp.broadcast_to(turned[:, :, None], (frame, pitches, side))


def paired_shards(
    density,
    source_sector,
    source_tile,
    matrix_id,
    cubic_weights,
    bin_cells,
    wave_level,
    energy_rate,
    pitch_rate,
):
    sectors, inner = lax.axis_size("sector"), lax.axis_size("inner")
    inner_here = lax.axis_index("inner")
    flip, group = inner_here % 2, inner_here // 2
    block, pitches, cell_count = density.shape
    side = cubic_weights.shape[1]
    tiles = cell_count // side
    half = tiles // 2
    quarter = block // 4
    first_steps = (quarter, quarter, quarter, quarter // 2, quarter - quarter // 2)
    halo_chunks = PASSES // quarter
    less = quarter - quarter // 4
    last_steps = (less, quarter, block - quarter - 2 * less, less)
    cap = slots(tiles, sectors)
    tables = (source_sector, source_tile)
    near, far = [1], list(range(2, sectors))

    weights = split_weights(matrix_id, cubic_weights)

    energies = energy_rate.shape[0]
    frame = 2 * block + 2 * PASSES
    energy_pad = jnp.pad(energy_rate[: energies - 1], ((PASSES, PASSES + 1), (0, 0)))
    pitch_pad = jnp.pad(pitch_rate[:, : pitches - 1], ((PASSES, PASSES), (0, 1)))
    first_energy = group * 2 * block
    a = across_lanes(lax.dynamic_slice_in_dim(energy_pad, first_energy, frame, 0), side)
    b = across_lanes(lax.dynamic_slice_in_dim(pitch_pad, first_energy, frame, 0), side)
    bin_ends = jnp.cumsum(bin_cells[0])
    cells = flip * (half * side) + jnp.arange(half * side, dtype=jnp.int32)
    bin_of = jnp.sum((bin_ends[None, :] <= cells[:, None]).astype(jnp.int32), axis=1)
    bins = jnp.arange(bin_ends.shape[0], dtype=jnp.int32)
    level = jnp.sum(jnp.where(bin_of[:, None] == bins[None, :], wave_level[0][None, :], 0.0), axis=1)
    rate = jnp.broadcast_to(level.reshape(half, 1, side), (half, 8, side))

    def at_lanes(t):
        return pl.ds(pl.multiple_of(t * side, side), side)

    def side_here():
        return lax.axis_index("inner") % 2

    swap = [(i, i ^ 1) for i in range(inner)]
    own_pairs, got_pairs = [], []
    for i in range(inner):
        for pairs, shift in ((own_pairs, -2 if i % 2 == 0 else 2), (got_pairs, 2 if i % 2 == 0 else -2)):
            if 0 <= i + shift < inner:
                pairs.append((i, i + shift))

    own, got, own_halo, got_halo = [], [], [], []
    packed = []
    start = 0
    for k, step in enumerate(first_steps):

        def first_of(start=start, step=step):
            here = side_here()
            return here * (block - start - step) + (1 - here) * start

        def find(field, first_of=first_of, step=step):
            first = first_of()
            return lambda t: [(t >= 0, lambda: field.at[pl.ds(first, step), :, at_lanes(t)])]

        def find_all(field):
            return lambda t: [(t >= 0, lambda: field.at[:, :, at_lanes(t)])]

        def receive(came, other, slot, first_of=first_of, step=step):
            if other == 2:
                return came.at[0, slot]
            return came.at[slot, pl.ds(first_of(), step)] if other == 1 else came.at[slot]

        def place(kept, sent):
            here = side_here()
            mine = lambda t: (t // half) == here
            return lambda t: [
                (mine(t), lambda: kept.at[t % half]),
                (jnp.logical_not(mine(t)), lambda: sent.at[t % half]),
            ]

        packed.append((start, step, find, receive, place))
        start += step

    def pack_first(k, after):
        start, step, find, _, _ = packed[k]
        groups = [(d, find, (step, pitches, side)) for d in far]
        if k == 0:
            groups += [(d, find_all, (block, pitches, side)) for d in near]
        return pack(groups, cap, tables, [density], after)

    sends = pack_first(0, ())
    beside = sector_exchange(sends[-1:], near)
    came = []
    far_queue(came, sends[0])
    token, tokens = None, []
    for k, (start, step, find, receive, place) in enumerate(packed):
        if k + 1 < len(packed):
            before = tokens[k - 1] if k else sends[0]
            far_queue(came, pack_first(k + 1, (before,))[0])
        if k == 1:
            came[k], (rate, a, b) = in_turn(came[k], [rate, a, b])
        part = jax.ShapeDtypeStruct((half, step, pitches, side), F32)
        piece = (step, pitches, side)
        after = [] if token is None else [token]
        kept, sent, token = drift(
            find, place, receive, tables, weights, [density], beside + came[k], [part, part], piece, after
        )
        tokens.append(token)
        own.append(kept)
        if k > 0:
            (sent,), (got[k - 1],) = in_turn([sent], [got[k - 1]])
        got.append(lax.ppermute(sent, "inner", swap))
        if 0 < k <= halo_chunks:
            forward = got[k - 1]
            if k > 1:
                (forward,), (got_halo[k - 2],) = in_turn([forward], [got_halo[k - 2]])
            got_halo.append(lax.ppermute(forward, "inner", got_pairs))
        if k < halo_chunks:
            if k > 0:
                (kept,), (own_halo[k - 1],) = in_turn([kept], [own_halo[k - 1]])
            own_halo.append(lax.ppermute(kept, "inner", own_pairs))

    kept, sends = diffuse(rate, a, b, own, got, own_halo, got_halo, last_steps)

    returns, ready, out, start = sends, [], (), 0
    for k, step in enumerate(last_steps):

        def find(mine, theirs, start=start, step=step):
            here = side_here()
            return lambda t: [
                ((t // half) == here, lambda: mine.at[t % half, pl.ds(start, step)]),
                ((t // half) != here, lambda: theirs.at[t % half]),
            ]

        def place(result, start=start, step=step):
            return lambda t: [(t >= 0, lambda: result.at[pl.ds(start, step), :, at_lanes(t)])]

        ready.append((find, place, (step, pitches, side)))
        start += step

    def receive_slot(came, other, slot):
        return came.at[0, slot] if other == 2 else came.at[slot]

    def pack_last(k, after):
        find, _, piece = ready[k]
        sends = pack([(d, find, piece) for d in far + near], cap, tables, [kept, backs[k]], after)
        return sends[1:], sends[0]

    whole = [jax.ShapeDtypeStruct(density.shape, F32)]
    backs = [lax.ppermute(returns[0], "inner", swap)]
    (last,), (backs[0],) = in_turn([returns[1]], [backs[0]])
    backs.append(lax.ppermute(last, "inner", swap))
    sends, far_sends = pack_last(0, ())
    came = []
    far_queue(came, far_sends)
    beside = sector_exchange(sends, near)
    token = None
    for k, (find, place, piece) in enumerate(ready):
        after = [] if token is None else [token]
        if k + 1 < len(ready):
            sends, far_sends = pack_last(k + 1, after)
            far_queue(came, far_sends)
            beside_next = sector_exchange(sends, near)
        if k + 2 < len(ready):
            (last,), (backs[k + 1], came[k][0]) = in_turn([returns[k + 2]], [backs[k + 1], came[k][0]])
            backs.append(lax.ppermute(last, "inner", swap))
        *out, token = drift(
            find, place, receive_slot, tables, weights, [kept, backs[k]], beside + came[k], whole, piece, after, out
        )
        beside = beside_next
    return out[0]


def slots(tiles, sectors):
    return max(2, (3 * tiles + 2 * sectors - 1) // (2 * sectors))


def order_within(sources):
    tile_count = sources.shape[1]
    same = sources[:, :, None] == sources[:, None, :]
    earlier = jnp.arange(tile_count)[None, :] < jnp.arange(tile_count)[:, None]
    return jnp.sum((same & earlier[None]).astype(jnp.int32), axis=2)


def drift_step(density, source_sector, source_tile, matrix_id, cubic_weights):
    sectors = lax.axis_size("sector")
    sector_here = lax.axis_index("sector")
    energies, pitches, cell_count = density.shape
    tile_len = cubic_weights.shape[1]
    tile_count = cell_count // tile_len
    slot_count = max(2, (3 * tile_count + 2 * sectors - 1) // (2 * sectors))
    sources = source_sector[0]
    picked_tiles = source_tile[0]
    matrix_ids = matrix_id[0]
    tile_ranks = order_within(sources)
    slot_rank = jnp.arange(slot_count, dtype=jnp.int32)
    matched = (sources[:, None, :] == sector_here) & (
        tile_ranks[:, None, :] == slot_rank[None, :, None]
    )
    chosen = jnp.sum(jnp.where(matched, picked_tiles[:, None, :], 0), axis=2).reshape(-1)
    filled = jnp.any(matched, axis=2).reshape(-1).astype(jnp.float32)
    blocks = density.reshape(energies, pitches, tile_count, tile_len)
    outgoing = jnp.take(blocks, chosen, axis=2) * filled[None, None, :, None]
    incoming = lax.all_to_all(outgoing, "sector", split_axis=2, concat_axis=2, tiled=True)
    own_sources = sources[sector_here]
    own_ranks = tile_ranks[sector_here]
    own_ids = matrix_ids[sector_here]
    where_from = own_sources * slot_count + own_ranks
    departing = jnp.take(incoming, where_from, axis=2)
    matrices = jnp.take(cubic_weights, own_ids, axis=0)
    drifted = jnp.einsum("eptj,tij->epti", departing, matrices, precision=lax.Precision.HIGHEST)
    return drifted.reshape(energies, pitches, cell_count)


def one_pass(field, rate_cell, energy_rate, pitch_rate):
    flux_e = energy_rate[:-1, :, None] * (field[1:] - field[:-1])
    flux_p = pitch_rate[:, :-1, None] * (field[:, 1:] - field[:, :-1])
    change_e = jnp.pad(flux_e, ((0, 1), (0, 0), (0, 0))) - jnp.pad(flux_e, ((1, 0), (0, 0), (0, 0)))
    change_p = jnp.pad(flux_p, ((0, 0), (0, 1), (0, 0))) - jnp.pad(flux_p, ((0, 0), (1, 0), (0, 0)))
    return field + rate_cell[None, None, :] * (change_e + change_p)


def shards(
    density,
    source_sector,
    source_tile,
    matrix_id,
    cubic_weights,
    bin_cells,
    wave_level,
    energy_rate,
    pitch_rate,
):
    first = drift_step(density, source_sector, source_tile, matrix_id, cubic_weights)
    inner_count = lax.axis_size("inner")
    inner_here = lax.axis_index("inner")
    cell_count = first.shape[2]
    lengths = bin_cells[0]
    per_device = cell_count // inner_count
    owner_cells = jnp.full((inner_count,), per_device, jnp.int32)
    owner_ends = jnp.cumsum(owner_cells)
    owner_starts = owner_ends - owner_cells
    offsets = jnp.arange(per_device, dtype=jnp.int32)
    cell_index = owner_starts[:, None] + offsets[None, :]
    valid = (offsets[None, :] < owner_cells[:, None]).reshape(-1).astype(jnp.float32)
    clipped = jnp.minimum(cell_index, cell_count - 1).reshape(-1)
    packed = jnp.take(first, clipped, axis=2) * valid[None, None, :]
    cellwise = lax.all_to_all(packed, "inner", split_axis=2, concat_axis=0, tiled=True)
    bin_ends = jnp.cumsum(lengths)
    global_cells = owner_starts[inner_here] + offsets
    is_live = (offsets < owner_cells[inner_here]).astype(jnp.float32)
    bin_of = jnp.sum((bin_ends[None, :] <= global_cells[:, None]).astype(jnp.int32), axis=1)
    onehot = bin_of[:, None] == jnp.arange(inner_count, dtype=jnp.int32)[None, :]
    cell_level = jnp.sum(jnp.where(onehot, wave_level[0][None, :], 0.0), axis=1) * is_live

    def loop_body(step, current):
        return one_pass(current, cell_level, energy_rate, pitch_rate)

    diffused = lax.fori_loop(0, PASSES, loop_body, cellwise)
    returned = lax.all_to_all(diffused, "inner", split_axis=0, concat_axis=2, tiled=True)
    every_cell = jnp.arange(cell_count, dtype=jnp.int32)
    owner_index = jnp.sum((owner_ends[None, :] <= every_cell[:, None]).astype(jnp.int32), axis=1)
    offset = every_cell - owner_starts[owner_index]
    position = owner_index * per_device + offset
    restored = jnp.take(returned, position, axis=2)
    return drift_step(restored, source_sector, source_tile, matrix_id, cubic_weights)


def pairs_fit(mesh, energies, pitches, cells, side):
    sectors, inner = mesh.shape["sector"], mesh.shape["inner"]
    block = energies // inner
    tiles = cells // sectors // side
    return (
        sectors == 4
        and inner % 2 == 0
        and tiles % 4 == 0
        and pitches % 16 == 0
        and side % 128 == 0
        and block % 16 == 0
        and 4 * PASSES == 3 * block
    )


def solution(mesh):
    specs = (
        P("inner", None, "sector"),
        P("inner", None, None),
        P("inner", None, None),
        P("inner", None, None),
        P(),
        P("sector", None),
        P("sector", None),
        P(),
        P(),
    )

    def whole(*arrays):
        energies, pitches, cells = arrays[0].shape
        fits = pairs_fit(mesh, energies, pitches, cells, arrays[4].shape[1])
        return jax.shard_map(
            paired_shards if fits else shards,
            mesh=mesh,
            in_specs=specs,
            out_specs=P("inner", None, "sector"),
            check_vma=False,
        )(*arrays)

    return whole
```

```python
import functools

import jax
import jax.numpy as jnp
from jax import lax
from jax.experimental import pallas as pl
from jax.experimental.pallas import tpu as pltpu
from jax.sharding import PartitionSpec as P

PASSES = 12
VMEM_LIMIT = 64 * 1024 * 1024 - 128 * 1024
ANY = pl.BlockSpec(memory_space=pltpu.HBM)
SMEM = pl.BlockSpec(memory_space=pltpu.SMEM)
VMEM = pl.BlockSpec(memory_space=pltpu.VMEM)
F32 = jnp.float32
BF16 = jnp.bfloat16


def params():
    return pltpu.CompilerParams(vmem_limit_bytes=VMEM_LIMIT)


def cost():
    return pl.CostEstimate(flops=0, bytes_accessed=1024, transcendentals=0)


def weights_kernel(mid_ref, w_ref, out_ref, raw, sems):
    tiles, side = raw.shape[0], raw.shape[1]
    me = lax.axis_index("sector")

    def copy(t):
        return pltpu.make_async_copy(w_ref.at[mid_ref[0, me, t]], raw.at[t], sems.at[t])

    @pl.loop(0, tiles)
    def _(t):
        copy(t).start()

    @pl.loop(0, tiles)
    def _(t):
        copy(t).wait()
        turned = jnp.transpose(raw[t])
        high = turned.astype(BF16)
        low = (turned - high.astype(F32)).astype(BF16)
        out_ref[t, :side, :side] = high
        out_ref[t, side:, :side] = high
        out_ref[t, :side, side:] = low
        out_ref[t, side:, side:] = jnp.zeros((side, side), BF16)


def split_weights(matrix_id, cubic_weights):
    tiles, side = matrix_id.shape[2], cubic_weights.shape[1]
    return pl.pallas_call(
        weights_kernel,
        out_shape=jax.ShapeDtypeStruct((tiles, 2 * side, 2 * side), BF16),
        in_specs=[SMEM, ANY],
        out_specs=VMEM,
        scratch_shapes=[
            pltpu.VMEM((tiles, side, side), F32),
            pltpu.SemaphoreType.DMA((tiles,)),
        ],
        compiler_params=params(),
        cost_estimate=cost(),
        name="split_weights",
    )(matrix_id, cubic_weights)


def pack_kernel(offsets, finds, n_far, n_arrays, sec_ref, til_ref, *refs):
    tiles, n = sec_ref.shape[2], len(offsets)
    near = n - n_far
    sends, rooms = refs[-n - 2 - (near + (n_far > 0)) : -n - 2], refs[-n - 2 : -2]
    if n_far:
        sends = [sends[0].at[i] for i in range(n_far)] + list(sends[1:])
    in_sems, out_sems = refs[-2:]
    me = lax.axis_index("sector")
    counts = []
    for i, d in enumerate(offsets):
        dest = me ^ d
        pieces = finds[i](*refs[:n_arrays])

        def body(t, count, i=i, dest=dest, pieces=pieces):
            hit = sec_ref[0, dest, t] == me

            @pl.when(hit)
            def _():
                for guard, piece in pieces(til_ref[0, dest, t]):

                    @pl.when(guard)
                    def _():
                        pltpu.make_async_copy(piece(), rooms[i].at[count], in_sems.at[i, count]).start()

            return count + hit.astype(jnp.int32)

        counts.append(lax.fori_loop(0, tiles, body, jnp.int32(0)))
    for i in range(n):

        @pl.loop(0, counts[i])
        def _(slot, i=i):
            here = rooms[i].at[slot]
            pltpu.make_async_copy(here, here, in_sems.at[i, slot]).wait()
            pltpu.make_async_copy(here, sends[i].at[slot], out_sems.at[i, slot]).start()

    for i in range(n):

        @pl.loop(0, counts[i])
        def _(slot, i=i):
            pltpu.make_async_copy(rooms[i].at[slot], sends[i].at[slot], out_sems.at[i, slot]).wait()


def pack(groups, cap, tables, arrays, after=()):
    n = len(groups)
    offsets, finds, shapes = zip(*groups)
    n_far = sum(d > 1 for d in offsets)
    outs = [(n_far, cap) + shapes[0]] * (n_far > 0) + [(cap,) + shape for shape in shapes[n_far:]]
    return pl.pallas_call(
        functools.partial(pack_kernel, offsets, finds, n_far, len(arrays)),
        out_shape=[jax.ShapeDtypeStruct(out, F32) for out in outs],
        in_specs=[SMEM, SMEM] + [ANY] * (len(arrays) + len(after)),
        out_specs=[ANY] * len(outs),
        scratch_shapes=[
            *[pltpu.VMEM((cap,) + shape, F32) for shape in shapes],
            pltpu.SemaphoreType.DMA((n, cap)),
            pltpu.SemaphoreType.DMA((n, cap)),
        ],
        compiler_params=params(),
        cost_estimate=cost(),
        name="pack_tiles",
    )(*tables, *arrays, *after)


def sector_exchange(sends, offsets):
    sectors = lax.axis_size("sector")
    return [
        lax.ppermute(send, "sector", [(s, s ^ d) for s in range(sectors)])
        for d, send in zip(offsets, sends)
    ]


def far_queue(came, send):
    if len(came) > 1:
        (send,), (came[-2][0],) = in_turn([send], [came[-2][0]])
    sectors = lax.axis_size("sector")
    whole = lax.ppermute(send, "sector", [(s, s ^ 2) for s in range(sectors)])
    came.append([whole, lax.ppermute(whole[1], "sector", [(s, s ^ 1) for s in range(sectors)])])


def in_turn(later, earlier):
    both = lax.optimization_barrier((*later, *earlier))
    return list(both[: len(later)]), list(both[len(later) :])


def drift_kernel(find, place, receive, n_local, n_extra, sec_ref, til_ref, w_ref, *refs):
    sectors, tiles = sec_ref.shape[1], sec_ref.shape[2]
    local, recvs = refs[:n_local], refs[n_local : n_local + sectors - 1]
    outs = refs[n_local + sectors - 1 + n_extra : -5]
    token, taken, made, in_sems, out_sems = refs[-5:]
    pieces = find(*local)
    put = place(*outs)
    me = lax.axis_index("sector")
    rows, side = taken.shape[1] * taken.shape[2], taken.shape[3]
    token[...] = jnp.zeros(token.shape, F32)

    def fetch(t, counts):
        d = sec_ref[0, me, t] ^ me

        @pl.when(d == 0)
        def _():
            for guard, piece in pieces(til_ref[0, me, t]):

                @pl.when(guard)
                def _():
                    pltpu.make_async_copy(piece(), taken.at[t], in_sems.at[t]).start()

        for other in range(1, sectors):

            @pl.when(d == other)
            def _(other=other):
                came = receive(recvs[other - 1], other, counts[other - 1])
                pltpu.make_async_copy(came, taken.at[t], in_sems.at[t]).start()

        return tuple(c + (d == i + 1).astype(jnp.int32) for i, c in enumerate(counts))

    lax.fori_loop(0, tiles, fetch, (jnp.int32(0),) * (sectors - 1))

    @pl.loop(0, tiles, unroll=4)
    def _(t):
        pltpu.make_async_copy(taken.at[t], taken.at[t], in_sems.at[t]).wait()
        value = taken[t].reshape(rows, side)
        high = value.astype(BF16)
        low = (value - high.astype(F32)).astype(BF16)
        both = jnp.dot(jnp.concatenate([high, low], axis=1), w_ref[t], preferred_element_type=F32)
        made[t] = (both[:, :side] + both[:, side:]).reshape(taken.shape[1:])
        for guard, there in put(t):

            @pl.when(guard)
            def _():
                pltpu.make_async_copy(made.at[t], there(), out_sems.at[t]).start()

    @pl.loop(0, tiles)
    def _(t):
        pltpu.make_async_copy(made.at[t], made.at[t], out_sems.at[t]).wait()


def drift(find, place, receive, tables, weights, local, recvs, outs, piece, after=(), carried=()):
    sectors, tiles = tables[0].shape[1], tables[0].shape[2]
    n_local = len(local)
    ins = [*tables, weights, *local, *recvs, *after, *carried]
    n_extra = len(after) + len(carried)
    return pl.pallas_call(
        functools.partial(drift_kernel, find, place, receive, n_local, n_extra),
        out_shape=[*outs, jax.ShapeDtypeStruct((8, 128), F32)],
        in_specs=[SMEM, SMEM, VMEM] + [ANY] * (len(ins) - 3),
        out_specs=[ANY] * len(outs) + [VMEM],
        scratch_shapes=[
            pltpu.VMEM((tiles,) + piece, F32),
            pltpu.VMEM((tiles,) + piece, F32),
            pltpu.SemaphoreType.DMA((tiles,)),
            pltpu.SemaphoreType.DMA((tiles,)),
        ],
        input_output_aliases={len(ins) - 1: 0} if carried else {},
        compiler_params=params(),
        cost_estimate=cost(),
        name="drift_chunk",
    )(*ins)


def diffusion_kernel(n_own, n_halo, n_send, first_tile, rate_ref, a_ref, b_ref, *refs):
    n_in = 2 * n_own + 2 * n_halo
    ins, keep, sends = refs[:n_in], refs[n_in], refs[n_in + 1 : n_in + 1 + n_send]
    field, work, ra_ref, rb_ref, done, in_sems, out_sems = refs[n_in + 1 + n_send :]
    tiles, block = keep.shape[0], keep.shape[1]
    frame, pitches, side = work.shape
    halo = (frame - 2 * block) // 2
    vregs = pitches // 8
    flip = lax.axis_index("inner") % 2
    places, start = [], 0
    for i in range(n_own):
        step = ins[i].shape[1]
        places.append((i, step, halo + start))
        places.append((n_own + i, step, halo + 2 * block - start - step))
        if i < n_halo:
            places.append((2 * n_own + i, step, halo + 2 * block + start))
            places.append((2 * n_own + n_halo + i, step, halo - start - step))
        start += step

    def fetch(g, slot):
        copies = []
        for i, step, place in places:
            at = jnp.where(flip == 0, place, frame - place - step)
            copies.append(
                pltpu.make_async_copy(
                    ins[i].at[first_tile + g], field.at[slot, pl.ds(at, step)], in_sems.at[slot, i]
                )
            )
        return copies

    def store(g, slot):
        copies = [
            pltpu.make_async_copy(
                done.at[slot, pl.ds(flip * block, block)], keep.at[g], out_sems.at[slot, n_send]
            )
        ]
        first = (1 - flip) * block
        for k in range(n_send):
            step = sends[k].shape[1]
            copies.append(
                pltpu.make_async_copy(
                    done.at[slot, pl.ds(first, step)], sends[k].at[g], out_sems.at[slot, k]
                )
            )
            first = first + step
        return copies

    for copy in fetch(0, 0):
        copy.start()

    @pl.loop(0, tiles)
    def _(g):
        slot = g % 2

        @pl.when(g + 1 < tiles)
        def _():
            for copy in fetch(g + 1, 1 - slot):
                copy.start()

        for copy in fetch(g, slot):
            copy.wait()

        @pl.when(g >= 2)
        def _():
            for copy in store(g - 2, slot):
                copy.wait()

        rate = rate_ref[first_tile + g]

        def rows_of(ref, e):
            return [ref[e, 8 * v : 8 * v + 8, :] for v in range(vregs)]

        def write_work(e, rows):
            for v in range(vregs):
                work[e, 8 * v : 8 * v + 8, :] = rows[v]

        def read_work(e):
            return rows_of(work, e)

        def read_field(e):
            return [field[slot, e, pl.ds(v, 8, stride=vregs), :] for v in range(vregs)]

        def write_done(e, rows):
            for v in range(vregs):
                done[slot, e - halo, pl.ds(v, 8, stride=vregs), :] = rows[v]

        def scaled(e):
            ra = [rate * x for x in rows_of(a_ref, e)]
            rb = [rate * x for x in rows_of(b_ref, e)]
            for v in range(vregs):
                ra_ref[e, 8 * v : 8 * v + 8, :] = ra[v]
                rb_ref[e, 8 * v : 8 * v + 8, :] = rb[v]
            return ra, rb

        def ready(e):
            return rows_of(ra_ref, e), rows_of(rb_ref, e)

        def sweep(first, count, read, write, rates, wide):
            def energy(e, here, below):
                after = read(e + 1)
                ra, rb = rates(e)
                above = [ra[v] * (after[v] - here[v]) for v in range(vregs)]
                nearby = here[1:] + [pltpu.roll(here[0], 7, 0)]
                pitch = [rb[v] * (nearby[v] - here[v]) for v in range(vregs)]
                before = [pltpu.roll(pitch[-1], 1, 0)] + pitch[:-1]
                write(
                    e,
                    [
                        here[v] + ((above[v] - below[v]) + (pitch[v] - before[v]))
                        for v in range(vregs)
                    ],
                )
                return after, above

            def several(e, carry, n):
                here, below = list(carry[:vregs]), list(carry[vregs:])
                for i in range(n):
                    here, below = energy(e + i, here, below)
                return (*here, *below)

            edge = read(first - 1)
            here = read(first)
            ra = rates(first - 1)[0]
            below = [ra[v] * (here[v] - edge[v]) for v in range(vregs)]
            carry = lax.fori_loop(
                0,
                count // wide,
                lambda i, carry: several(first + wide * i, carry, wide),
                (*here, *below),
            )
            for left in range(2, wide, 2):

                @pl.when(count % wide == left)
                def _(left=left):
                    several(first + count - left, carry, left)

        sweep(1, frame - 2, read_field, write_work, scaled, 2)

        @pl.loop(1, PASSES - 1)
        def _(n):
            sweep(n + 1, frame - 2 - 2 * n, read_work, write_work, ready, 4)

        sweep(PASSES, frame - 2 * PASSES, read_work, write_done, ready, 4)

        for copy in store(g, slot):
            copy.start()

    for g in range(max(0, tiles - 2), tiles):
        for copy in store(g, g % 2):
            copy.wait()


def diffuse(rate, a, b, own, got, own_halo, got_halo, steps, first_tile, tiles):
    pitches, side = own[0].shape[2:]
    frame = a.shape[0]
    block = sum(steps)
    ins = [*own, *got, *own_halo, *got_halo]
    out = pl.pallas_call(
        functools.partial(diffusion_kernel, len(own), len(own_halo), len(steps), first_tile),
        out_shape=[
            jax.ShapeDtypeStruct((tiles, step, pitches, side), F32) for step in (block, *steps)
        ],
        in_specs=[VMEM] * 3 + [ANY] * len(ins),
        out_specs=[ANY] * (1 + len(steps)),
        scratch_shapes=[
            pltpu.VMEM((2, frame, pitches, side), F32),
            pltpu.VMEM((frame, pitches, side), F32),
            pltpu.VMEM((frame, pitches, side), F32),
            pltpu.VMEM((frame, pitches, side), F32),
            pltpu.VMEM((2, 2 * block, pitches, side), F32),
            pltpu.SemaphoreType.DMA((2, len(ins))),
            pltpu.SemaphoreType.DMA((2, len(steps) + 1)),
        ],
        compiler_params=params(),
        cost_estimate=cost(),
        name="diffuse_tiles",
    )(rate, a, b, *ins)
    return out[0], out[1:]


def across_lanes(window, side):
    frame, pitches = window.shape
    turned = window.reshape(frame, 8, pitches // 8).transpose(0, 2, 1).reshape(frame, pitches)
    return jnp.broadcast_to(turned[:, :, None], (frame, pitches, side))


def paired_shards(
    density,
    source_sector,
    source_tile,
    matrix_id,
    cubic_weights,
    bin_cells,
    wave_level,
    energy_rate,
    pitch_rate,
):
    sectors, inner = lax.axis_size("sector"), lax.axis_size("inner")
    inner_here = lax.axis_index("inner")
    flip, group = inner_here % 2, inner_here // 2
    block, pitches, cell_count = density.shape
    side = cubic_weights.shape[1]
    tiles = cell_count // side
    half = tiles // 2
    quarter = block // 4
    first_steps = (quarter, quarter, quarter, quarter // 2, quarter - quarter // 2)
    halo_chunks = PASSES // quarter
    less = quarter - quarter // 4
    more = block // 2 - less
    last_steps = (less, more, more, less)
    cap = slots(tiles, sectors)
    tables = (source_sector, source_tile)
    near, far = [1], list(range(2, sectors))

    weights = split_weights(matrix_id, cubic_weights)

    energies = energy_rate.shape[0]
    frame = 2 * block + 2 * PASSES
    energy_pad = jnp.pad(energy_rate[: energies - 1], ((PASSES, PASSES + 1), (0, 0)))
    pitch_pad = jnp.pad(pitch_rate[:, : pitches - 1], ((PASSES, PASSES), (0, 1)))
    first_energy = group * 2 * block
    a = across_lanes(lax.dynamic_slice_in_dim(energy_pad, first_energy, frame, 0), side)
    b = across_lanes(lax.dynamic_slice_in_dim(pitch_pad, first_energy, frame, 0), side)
    bin_ends = jnp.cumsum(bin_cells[0])
    cells = flip * (half * side) + jnp.arange(half * side, dtype=jnp.int32)
    bin_of = jnp.sum((bin_ends[None, :] <= cells[:, None]).astype(jnp.int32), axis=1)
    bins = jnp.arange(bin_ends.shape[0], dtype=jnp.int32)
    level = jnp.sum(jnp.where(bin_of[:, None] == bins[None, :], wave_level[0][None, :], 0.0), axis=1)
    rate = jnp.broadcast_to(level.reshape(half, 1, side), (half, 8, side))

    def at_lanes(t):
        return pl.ds(pl.multiple_of(t * side, side), side)

    def side_here():
        return lax.axis_index("inner") % 2

    swap = [(i, i ^ 1) for i in range(inner)]
    own_pairs, got_pairs = [], []
    for i in range(inner):
        for pairs, shift in ((own_pairs, -2 if i % 2 == 0 else 2), (got_pairs, 2 if i % 2 == 0 else -2)):
            if 0 <= i + shift < inner:
                pairs.append((i, i + shift))

    own, got, own_halo, got_halo = [], [], [], []
    packed = []
    start = 0
    for k, step in enumerate(first_steps):

        def first_of(start=start, step=step):
            here = side_here()
            return here * (block - start - step) + (1 - here) * start

        def find(field, first_of=first_of, step=step):
            first = first_of()
            return lambda t: [(t >= 0, lambda: field.at[pl.ds(first, step), :, at_lanes(t)])]

        def find_all(field):
            return lambda t: [(t >= 0, lambda: field.at[:, :, at_lanes(t)])]

        def receive(came, other, slot, first_of=first_of, step=step):
            if other == 2:
                return came.at[0, slot]
            return came.at[slot, pl.ds(first_of(), step)] if other == 1 else came.at[slot]

        def place(kept, sent):
            here = side_here()
            mine = lambda t: (t // half) == here
            return lambda t: [
                (mine(t), lambda: kept.at[t % half]),
                (jnp.logical_not(mine(t)), lambda: sent.at[t % half]),
            ]

        packed.append((start, step, find, receive, place))
        start += step

    def pack_first(k, after):
        start, step, find, _, _ = packed[k]
        groups = [(d, find, (step, pitches, side)) for d in far]
        if k == 0:
            groups += [(d, find_all, (block, pitches, side)) for d in near]
        return pack(groups, cap, tables, [density], after)

    sends = pack_first(0, ())
    beside = sector_exchange(sends[-1:], near)
    came = []
    far_queue(came, sends[0])
    token, tokens = None, []
    for k, (start, step, find, receive, place) in enumerate(packed):
        if k + 1 < len(packed):
            before = tokens[k - 1] if k else sends[0]
            far_queue(came, pack_first(k + 1, (before,))[0])
        if k == 1:
            came[k], (rate, a, b) = in_turn(came[k], [rate, a, b])
        part = jax.ShapeDtypeStruct((half, step, pitches, side), F32)
        piece = (step, pitches, side)
        after = [] if token is None else [token]
        kept, sent, token = drift(
            find, place, receive, tables, weights, [density], beside + came[k], [part, part], piece, after
        )
        tokens.append(token)
        own.append(kept)
        if k > 0:
            (sent,), (got[k - 1],) = in_turn([sent], [got[k - 1]])
        got.append(lax.ppermute(sent, "inner", swap))
        if 0 < k <= halo_chunks:
            forward = got[k - 1]
            if k > 1:
                (forward,), (got_halo[k - 2],) = in_turn([forward], [got_halo[k - 2]])
            got_halo.append(lax.ppermute(forward, "inner", got_pairs))
        if k < halo_chunks:
            if k > 0:
                (kept,), (own_halo[k - 1],) = in_turn([kept], [own_halo[k - 1]])
            own_halo.append(lax.ppermute(kept, "inner", own_pairs))

    fields = (rate, a, b, own, got, own_halo, got_halo)
    quad = half // 2
    kept_low, low = diffuse(*fields, (last_steps[0] + last_steps[1], *last_steps[2:]), 0, quad)
    kept_high, high = diffuse(*fields, last_steps, quad, quad)

    ready, out, start = [], (), 0
    for k, step in enumerate(last_steps):

        def find(mine_low, mine_high, their_low, their_high, k=k, start=start, step=step):
            here, there = pl.ds(start, step), pl.ds(start if k < 2 else 0, step)

            def pieces(t):
                ours = (t // half) == side_here()
                rank = t % half
                lower = rank < quad
                both, theirs = jnp.logical_and, jnp.logical_not(ours)
                upper = jnp.logical_not(lower)
                return [
                    (both(ours, lower), lambda: mine_low.at[rank % quad, here]),
                    (both(ours, upper), lambda: mine_high.at[rank % quad, here]),
                    (both(theirs, lower), lambda: their_low.at[rank % quad, there]),
                    (both(theirs, upper), lambda: their_high.at[rank % quad]),
                ]

            return pieces

        def place(result, start=start, step=step):
            return lambda t: [(t >= 0, lambda: result.at[pl.ds(start, step), :, at_lanes(t)])]

        ready.append((find, place, (step, pitches, side)))
        start += step

    def receive_slot(came, other, slot):
        return came.at[0, slot] if other == 2 else came.at[slot]

    def pack_last(k, after):
        find, _, piece = ready[k]
        local = [kept_low, kept_high, backs_low[k], backs_high[k]]
        sends = pack([(d, find, piece) for d in far + near], cap, tables, local, after)
        return sends[1:], sends[0]

    whole = [jax.ShapeDtypeStruct(density.shape, F32)]
    early = lax.ppermute(low[0], "inner", swap)
    (last,), (early,) = in_turn([high[0]], [early])
    backs_low, backs_high = [early, early], [lax.ppermute(last, "inner", swap)]
    (last,), (backs_high[0],) = in_turn([high[1]], [backs_high[0]])
    backs_high.append(lax.ppermute(last, "inner", swap))
    sends, far_sends = pack_last(0, ())
    came = []
    far_queue(came, far_sends)
    beside = sector_exchange(sends, near)
    token = None
    for k, (find, place, piece) in enumerate(ready):
        after = [] if token is None else [token]
        if k + 1 < len(ready):
            sends, far_sends = pack_last(k + 1, after)
            far_queue(came, far_sends)
            beside_next = sector_exchange(sends, near)
        if k + 2 < len(ready):
            pair, (backs_high[k + 1], came[k][0]) = in_turn(
                [low[k + 1], high[k + 2]], [backs_high[k + 1], came[k][0]]
            )
            backs_low.append(lax.ppermute(pair[0], "inner", swap))
            backs_high.append(lax.ppermute(pair[1], "inner", swap))
        local = [kept_low, kept_high, backs_low[k], backs_high[k]]
        *out, token = drift(
            find, place, receive_slot, tables, weights, local, beside + came[k], whole, piece, after, out
        )
        beside = beside_next
    return out[0]


def slots(tiles, sectors):
    return max(2, (3 * tiles + 2 * sectors - 1) // (2 * sectors))


def order_within(sources):
    tile_count = sources.shape[1]
    same = sources[:, :, None] == sources[:, None, :]
    earlier = jnp.arange(tile_count)[None, :] < jnp.arange(tile_count)[:, None]
    return jnp.sum((same & earlier[None]).astype(jnp.int32), axis=2)


def drift_step(density, source_sector, source_tile, matrix_id, cubic_weights):
    sectors = lax.axis_size("sector")
    sector_here = lax.axis_index("sector")
    energies, pitches, cell_count = density.shape
    tile_len = cubic_weights.shape[1]
    tile_count = cell_count // tile_len
    slot_count = max(2, (3 * tile_count + 2 * sectors - 1) // (2 * sectors))
    sources = source_sector[0]
    picked_tiles = source_tile[0]
    matrix_ids = matrix_id[0]
    tile_ranks = order_within(sources)
    slot_rank = jnp.arange(slot_count, dtype=jnp.int32)
    matched = (sources[:, None, :] == sector_here) & (
        tile_ranks[:, None, :] == slot_rank[None, :, None]
    )
    chosen = jnp.sum(jnp.where(matched, picked_tiles[:, None, :], 0), axis=2).reshape(-1)
    filled = jnp.any(matched, axis=2).reshape(-1).astype(jnp.float32)
    blocks = density.reshape(energies, pitches, tile_count, tile_len)
    outgoing = jnp.take(blocks, chosen, axis=2) * filled[None, None, :, None]
    incoming = lax.all_to_all(outgoing, "sector", split_axis=2, concat_axis=2, tiled=True)
    own_sources = sources[sector_here]
    own_ranks = tile_ranks[sector_here]
    own_ids = matrix_ids[sector_here]
    where_from = own_sources * slot_count + own_ranks
    departing = jnp.take(incoming, where_from, axis=2)
    matrices = jnp.take(cubic_weights, own_ids, axis=0)
    drifted = jnp.einsum("eptj,tij->epti", departing, matrices, precision=lax.Precision.HIGHEST)
    return drifted.reshape(energies, pitches, cell_count)


def one_pass(field, rate_cell, energy_rate, pitch_rate):
    flux_e = energy_rate[:-1, :, None] * (field[1:] - field[:-1])
    flux_p = pitch_rate[:, :-1, None] * (field[:, 1:] - field[:, :-1])
    change_e = jnp.pad(flux_e, ((0, 1), (0, 0), (0, 0))) - jnp.pad(flux_e, ((1, 0), (0, 0), (0, 0)))
    change_p = jnp.pad(flux_p, ((0, 0), (0, 1), (0, 0))) - jnp.pad(flux_p, ((0, 0), (1, 0), (0, 0)))
    return field + rate_cell[None, None, :] * (change_e + change_p)


def shards(
    density,
    source_sector,
    source_tile,
    matrix_id,
    cubic_weights,
    bin_cells,
    wave_level,
    energy_rate,
    pitch_rate,
):
    first = drift_step(density, source_sector, source_tile, matrix_id, cubic_weights)
    inner_count = lax.axis_size("inner")
    inner_here = lax.axis_index("inner")
    cell_count = first.shape[2]
    lengths = bin_cells[0]
    per_device = cell_count // inner_count
    owner_cells = jnp.full((inner_count,), per_device, jnp.int32)
    owner_ends = jnp.cumsum(owner_cells)
    owner_starts = owner_ends - owner_cells
    offsets = jnp.arange(per_device, dtype=jnp.int32)
    cell_index = owner_starts[:, None] + offsets[None, :]
    valid = (offsets[None, :] < owner_cells[:, None]).reshape(-1).astype(jnp.float32)
    clipped = jnp.minimum(cell_index, cell_count - 1).reshape(-1)
    packed = jnp.take(first, clipped, axis=2) * valid[None, None, :]
    cellwise = lax.all_to_all(packed, "inner", split_axis=2, concat_axis=0, tiled=True)
    bin_ends = jnp.cumsum(lengths)
    global_cells = owner_starts[inner_here] + offsets
    is_live = (offsets < owner_cells[inner_here]).astype(jnp.float32)
    bin_of = jnp.sum((bin_ends[None, :] <= global_cells[:, None]).astype(jnp.int32), axis=1)
    onehot = bin_of[:, None] == jnp.arange(inner_count, dtype=jnp.int32)[None, :]
    cell_level = jnp.sum(jnp.where(onehot, wave_level[0][None, :], 0.0), axis=1) * is_live

    def loop_body(step, current):
        return one_pass(current, cell_level, energy_rate, pitch_rate)

    diffused = lax.fori_loop(0, PASSES, loop_body, cellwise)
    returned = lax.all_to_all(diffused, "inner", split_axis=0, concat_axis=2, tiled=True)
    every_cell = jnp.arange(cell_count, dtype=jnp.int32)
    owner_index = jnp.sum((owner_ends[None, :] <= every_cell[:, None]).astype(jnp.int32), axis=1)
    offset = every_cell - owner_starts[owner_index]
    position = owner_index * per_device + offset
    restored = jnp.take(returned, position, axis=2)
    return drift_step(restored, source_sector, source_tile, matrix_id, cubic_weights)


def pairs_fit(mesh, energies, pitches, cells, side):
    sectors, inner = mesh.shape["sector"], mesh.shape["inner"]
    block = energies // inner
    tiles = cells // sectors // side
    return (
        sectors == 4
        and inner % 2 == 0
        and tiles % 4 == 0
        and pitches % 16 == 0
        and side % 128 == 0
        and block % 16 == 0
        and 4 * PASSES == 3 * block
    )


def solution(mesh):
    specs = (
        P("inner", None, "sector"),
        P("inner", None, None),
        P("inner", None, None),
        P("inner", None, None),
        P(),
        P("sector", None),
        P("sector", None),
        P(),
        P(),
    )

    def whole(*arrays):
        energies, pitches, cells = arrays[0].shape
        fits = pairs_fit(mesh, energies, pitches, cells, arrays[4].shape[1])
        return jax.shard_map(
            paired_shards if fits else shards,
            mesh=mesh,
            in_specs=specs,
            out_specs=P("inner", None, "sector"),
            check_vma=False,
        )(*arrays)

    return whole
```

```python
import functools

import jax
import jax.numpy as jnp
from jax import lax
from jax.experimental import pallas as pl
from jax.experimental.pallas import tpu as pltpu
from jax.sharding import PartitionSpec as P

PASSES = 12
VMEM_LIMIT = 64 * 1024 * 1024 - 128 * 1024
ANY = pl.BlockSpec(memory_space=pltpu.HBM)
SMEM = pl.BlockSpec(memory_space=pltpu.SMEM)
VMEM = pl.BlockSpec(memory_space=pltpu.VMEM)
F32 = jnp.float32
BF16 = jnp.bfloat16


def params():
    return pltpu.CompilerParams(vmem_limit_bytes=VMEM_LIMIT)


def cost():
    return pl.CostEstimate(flops=0, bytes_accessed=1024, transcendentals=0)


def weights_kernel(mid_ref, w_ref, out_ref, raw, sems):
    tiles, side = raw.shape[0], raw.shape[1]
    me = lax.axis_index("sector")

    def copy(t):
        return pltpu.make_async_copy(w_ref.at[mid_ref[0, me, t]], raw.at[t], sems.at[t])

    @pl.loop(0, tiles)
    def _(t):
        copy(t).start()

    @pl.loop(0, tiles)
    def _(t):
        copy(t).wait()
        turned = jnp.transpose(raw[t])
        high = turned.astype(BF16)
        low = (turned - high.astype(F32)).astype(BF16)
        out_ref[t, :side, :side] = high
        out_ref[t, side:, :side] = high
        out_ref[t, :side, side:] = low
        out_ref[t, side:, side:] = jnp.zeros((side, side), BF16)


def split_weights(matrix_id, cubic_weights):
    tiles, side = matrix_id.shape[2], cubic_weights.shape[1]
    return pl.pallas_call(
        weights_kernel,
        out_shape=jax.ShapeDtypeStruct((tiles, 2 * side, 2 * side), BF16),
        in_specs=[SMEM, ANY],
        out_specs=VMEM,
        scratch_shapes=[
            pltpu.VMEM((tiles, side, side), F32),
            pltpu.SemaphoreType.DMA((tiles,)),
        ],
        compiler_params=params(),
        cost_estimate=cost(),
        name="split_weights",
    )(matrix_id, cubic_weights)


def pack_kernel(offsets, finds, n_far, n_arrays, sec_ref, til_ref, *refs):
    tiles, n = sec_ref.shape[2], len(offsets)
    near = n - n_far
    sends, rooms = refs[-n - 2 - (near + (n_far > 0)) : -n - 2], refs[-n - 2 : -2]
    if n_far:
        sends = [sends[0].at[i] for i in range(n_far)] + list(sends[1:])
    in_sems, out_sems = refs[-2:]
    me = lax.axis_index("sector")
    counts = []
    for i, d in enumerate(offsets):
        dest = me ^ d
        pieces = finds[i](*refs[:n_arrays])

        def body(t, count, i=i, dest=dest, pieces=pieces):
            hit = sec_ref[0, dest, t] == me

            @pl.when(hit)
            def _():
                for guard, piece in pieces(til_ref[0, dest, t]):

                    @pl.when(guard)
                    def _():
                        pltpu.make_async_copy(piece(), rooms[i].at[count], in_sems.at[i, count]).start()

            return count + hit.astype(jnp.int32)

        counts.append(lax.fori_loop(0, tiles, body, jnp.int32(0)))
    for i in range(n):

        @pl.loop(0, counts[i])
        def _(slot, i=i):
            here = rooms[i].at[slot]
            pltpu.make_async_copy(here, here, in_sems.at[i, slot]).wait()
            pltpu.make_async_copy(here, sends[i].at[slot], out_sems.at[i, slot]).start()

    for i in range(n):

        @pl.loop(0, counts[i])
        def _(slot, i=i):
            pltpu.make_async_copy(rooms[i].at[slot], sends[i].at[slot], out_sems.at[i, slot]).wait()


def pack(groups, cap, tables, arrays, after=()):
    n = len(groups)
    offsets, finds, shapes = zip(*groups)
    n_far = sum(d > 1 for d in offsets)
    outs = [(n_far, cap) + shapes[0]] * (n_far > 0) + [(cap,) + shape for shape in shapes[n_far:]]
    return pl.pallas_call(
        functools.partial(pack_kernel, offsets, finds, n_far, len(arrays)),
        out_shape=[jax.ShapeDtypeStruct(out, F32) for out in outs],
        in_specs=[SMEM, SMEM] + [ANY] * (len(arrays) + len(after)),
        out_specs=[ANY] * len(outs),
        scratch_shapes=[
            *[pltpu.VMEM((cap,) + shape, F32) for shape in shapes],
            pltpu.SemaphoreType.DMA((n, cap)),
            pltpu.SemaphoreType.DMA((n, cap)),
        ],
        compiler_params=params(),
        cost_estimate=cost(),
        name="pack_tiles",
    )(*tables, *arrays, *after)


def sector_exchange(sends, offsets):
    sectors = lax.axis_size("sector")
    return [
        lax.ppermute(send, "sector", [(s, s ^ d) for s in range(sectors)])
        for d, send in zip(offsets, sends)
    ]


def far_queue(came, send):
    if len(came) > 1:
        (send,), (came[-2][0],) = in_turn([send], [came[-2][0]])
    sectors = lax.axis_size("sector")
    whole = lax.ppermute(send, "sector", [(s, s ^ 2) for s in range(sectors)])
    came.append([whole, lax.ppermute(whole[1], "sector", [(s, s ^ 1) for s in range(sectors)])])


def in_turn(later, earlier):
    both = lax.optimization_barrier((*later, *earlier))
    return list(both[: len(later)]), list(both[len(later) :])


def drift_kernel(find, place, receive, n_local, n_extra, sec_ref, til_ref, w_ref, *refs):
    sectors, tiles = sec_ref.shape[1], sec_ref.shape[2]
    local, recvs = refs[:n_local], refs[n_local : n_local + sectors - 1]
    outs = refs[n_local + sectors - 1 + n_extra : -7]
    token, taken, made, w_room, in_sems, out_sems, w_sems = refs[-7:]
    pieces = find(*local)
    put = place(*outs)
    me = lax.axis_index("sector")
    rows, side = taken.shape[1] * taken.shape[2], taken.shape[3]
    token[...] = jnp.zeros(token.shape, F32)

    def matrix(t):
        return pltpu.make_async_copy(w_ref.at[t], w_room.at[t], w_sems.at[t])

    def fetch(t, counts):
        matrix(t).start()
        d = sec_ref[0, me, t] ^ me

        @pl.when(d == 0)
        def _():
            for guard, piece in pieces(til_ref[0, me, t]):

                @pl.when(guard)
                def _():
                    pltpu.make_async_copy(piece(), taken.at[t], in_sems.at[t]).start()

        for other in range(1, sectors):

            @pl.when(d == other)
            def _(other=other):
                came = receive(recvs[other - 1], other, counts[other - 1])
                pltpu.make_async_copy(came, taken.at[t], in_sems.at[t]).start()

        return tuple(c + (d == i + 1).astype(jnp.int32) for i, c in enumerate(counts))

    lax.fori_loop(0, tiles, fetch, (jnp.int32(0),) * (sectors - 1))

    @pl.loop(0, tiles, unroll=4)
    def _(t):
        matrix(t).wait()
        pltpu.make_async_copy(taken.at[t], taken.at[t], in_sems.at[t]).wait()
        value = taken[t].reshape(rows, side)
        high = value.astype(BF16)
        low = (value - high.astype(F32)).astype(BF16)
        both = jnp.dot(jnp.concatenate([high, low], axis=1), w_room[t], preferred_element_type=F32)
        made[t] = (both[:, :side] + both[:, side:]).reshape(taken.shape[1:])
        for guard, there in put(t):

            @pl.when(guard)
            def _():
                pltpu.make_async_copy(made.at[t], there(), out_sems.at[t]).start()

    @pl.loop(0, tiles)
    def _(t):
        pltpu.make_async_copy(made.at[t], made.at[t], out_sems.at[t]).wait()


def drift(find, place, receive, tables, weights, local, recvs, outs, piece, after=(), carried=()):
    sectors, tiles = tables[0].shape[1], tables[0].shape[2]
    n_local = len(local)
    ins = [*tables, weights, *local, *recvs, *after, *carried]
    n_extra = len(after) + len(carried)
    return pl.pallas_call(
        functools.partial(drift_kernel, find, place, receive, n_local, n_extra),
        out_shape=[*outs, jax.ShapeDtypeStruct((8, 128), F32)],
        in_specs=[SMEM, SMEM] + [ANY] * (len(ins) - 2),
        out_specs=[ANY] * len(outs) + [VMEM],
        scratch_shapes=[
            pltpu.VMEM((tiles,) + piece, F32),
            pltpu.VMEM((tiles,) + piece, F32),
            pltpu.VMEM(weights.shape, BF16),
            pltpu.SemaphoreType.DMA((tiles,)),
            pltpu.SemaphoreType.DMA((tiles,)),
            pltpu.SemaphoreType.DMA((tiles,)),
        ],
        input_output_aliases={len(ins) - 1: 0} if carried else {},
        compiler_params=params(),
        cost_estimate=cost(),
        name="drift_chunk",
    )(*ins)


def diffusion_kernel(n_own, n_halo, n_send, first_tile, rate_ref, a_ref, b_ref, *refs):
    n_in = 2 * n_own + 2 * n_halo
    ins, keep, sends = refs[:n_in], refs[n_in], refs[n_in + 1 : n_in + 1 + n_send]
    field, work, ra_ref, rb_ref, done, in_sems, out_sems = refs[n_in + 1 + n_send :]
    tiles, block = keep.shape[0], keep.shape[1]
    frame, pitches, side = work.shape
    halo = (frame - 2 * block) // 2
    vregs = pitches // 8
    flip = lax.axis_index("inner") % 2
    places, start = [], 0
    for i in range(n_own):
        step = ins[i].shape[1]
        places.append((i, step, halo + start))
        places.append((n_own + i, step, halo + 2 * block - start - step))
        if i < n_halo:
            places.append((2 * n_own + i, step, halo + 2 * block + start))
            places.append((2 * n_own + n_halo + i, step, halo - start - step))
        start += step

    def fetch(g, slot):
        copies = []
        for i, step, place in places:
            at = jnp.where(flip == 0, place, frame - place - step)
            copies.append(
                pltpu.make_async_copy(
                    ins[i].at[first_tile + g], field.at[slot, pl.ds(at, step)], in_sems.at[slot, i]
                )
            )
        return copies

    def store(g, slot):
        copies = [
            pltpu.make_async_copy(
                done.at[slot, pl.ds(flip * block, block)], keep.at[g], out_sems.at[slot, n_send]
            )
        ]
        first = (1 - flip) * block
        for k in range(n_send):
            step = sends[k].shape[1]
            copies.append(
                pltpu.make_async_copy(
                    done.at[slot, pl.ds(first, step)], sends[k].at[g], out_sems.at[slot, k]
                )
            )
            first = first + step
        return copies

    for copy in fetch(0, 0):
        copy.start()

    @pl.loop(0, tiles)
    def _(g):
        slot = g % 2

        @pl.when(g + 1 < tiles)
        def _():
            for copy in fetch(g + 1, 1 - slot):
                copy.start()

        for copy in fetch(g, slot):
            copy.wait()

        @pl.when(g >= 2)
        def _():
            for copy in store(g - 2, slot):
                copy.wait()

        rate = rate_ref[first_tile + g]

        def rows_of(ref, e):
            return [ref[e, 8 * v : 8 * v + 8, :] for v in range(vregs)]

        def write_work(e, rows):
            for v in range(vregs):
                work[e, 8 * v : 8 * v + 8, :] = rows[v]

        def read_work(e):
            return rows_of(work, e)

        def read_field(e):
            return [field[slot, e, pl.ds(v, 8, stride=vregs), :] for v in range(vregs)]

        def write_done(e, rows):
            for v in range(vregs):
                done[slot, e - halo, pl.ds(v, 8, stride=vregs), :] = rows[v]

        def scaled(e):
            ra = [rate * x for x in rows_of(a_ref, e)]
            rb = [rate * x for x in rows_of(b_ref, e)]
            for v in range(vregs):
                ra_ref[e, 8 * v : 8 * v + 8, :] = ra[v]
                rb_ref[e, 8 * v : 8 * v + 8, :] = rb[v]
            return ra, rb

        def ready(e):
            return rows_of(ra_ref, e), rows_of(rb_ref, e)

        def sweep(first, count, read, write, rates, wide):
            def energy(e, here, below):
                after = read(e + 1)
                ra, rb = rates(e)
                above = [ra[v] * (after[v] - here[v]) for v in range(vregs)]
                nearby = here[1:] + [pltpu.roll(here[0], 7, 0)]
                pitch = [rb[v] * (nearby[v] - here[v]) for v in range(vregs)]
                before = [pltpu.roll(pitch[-1], 1, 0)] + pitch[:-1]
                write(
                    e,
                    [
                        here[v] + ((above[v] - below[v]) + (pitch[v] - before[v]))
                        for v in range(vregs)
                    ],
                )
                return after, above

            def several(e, carry, n):
                here, below = list(carry[:vregs]), list(carry[vregs:])
                for i in range(n):
                    here, below = energy(e + i, here, below)
                return (*here, *below)

            edge = read(first - 1)
            here = read(first)
            ra = rates(first - 1)[0]
            below = [ra[v] * (here[v] - edge[v]) for v in range(vregs)]
            carry = lax.fori_loop(
                0,
                count // wide,
                lambda i, carry: several(first + wide * i, carry, wide),
                (*here, *below),
            )
            for left in range(2, wide, 2):

                @pl.when(count % wide == left)
                def _(left=left):
                    several(first + count - left, carry, left)

        sweep(1, frame - 2, read_field, write_work, scaled, 2)

        @pl.loop(1, PASSES - 1)
        def _(n):
            sweep(n + 1, frame - 2 - 2 * n, read_work, write_work, ready, 4)

        sweep(PASSES, frame - 2 * PASSES, read_work, write_done, ready, 4)

        for copy in store(g, slot):
            copy.start()

    for g in range(max(0, tiles - 2), tiles):
        for copy in store(g, g % 2):
            copy.wait()


def diffuse(rate, a, b, own, got, own_halo, got_halo, steps, first_tile, tiles):
    pitches, side = own[0].shape[2:]
    frame = a.shape[0]
    block = sum(steps)
    ins = [*own, *got, *own_halo, *got_halo]
    out = pl.pallas_call(
        functools.partial(diffusion_kernel, len(own), len(own_halo), len(steps), first_tile),
        out_shape=[
            jax.ShapeDtypeStruct((tiles, step, pitches, side), F32) for step in (block, *steps)
        ],
        in_specs=[VMEM] * 3 + [ANY] * len(ins),
        out_specs=[ANY] * (1 + len(steps)),
        scratch_shapes=[
            pltpu.VMEM((2, frame, pitches, side), F32),
            pltpu.VMEM((frame, pitches, side), F32),
            pltpu.VMEM((frame, pitches, side), F32),
            pltpu.VMEM((frame, pitches, side), F32),
            pltpu.VMEM((2, 2 * block, pitches, side), F32),
            pltpu.SemaphoreType.DMA((2, len(ins))),
            pltpu.SemaphoreType.DMA((2, len(steps) + 1)),
        ],
        compiler_params=params(),
        cost_estimate=cost(),
        name="diffuse_tiles",
    )(rate, a, b, *ins)
    return out[0], out[1:]


def across_lanes(window, side):
    frame, pitches = window.shape
    turned = window.reshape(frame, 8, pitches // 8).transpose(0, 2, 1).reshape(frame, pitches)
    return jnp.broadcast_to(turned[:, :, None], (frame, pitches, side))


def paired_shards(
    density,
    source_sector,
    source_tile,
    matrix_id,
    cubic_weights,
    bin_cells,
    wave_level,
    energy_rate,
    pitch_rate,
):
    sectors, inner = lax.axis_size("sector"), lax.axis_size("inner")
    inner_here = lax.axis_index("inner")
    flip, group = inner_here % 2, inner_here // 2
    block, pitches, cell_count = density.shape
    side = cubic_weights.shape[1]
    tiles = cell_count // side
    half = tiles // 2
    quarter = block // 4
    first_steps = (quarter, quarter, quarter, quarter // 2, quarter - quarter // 2)
    halo_chunks = PASSES // quarter
    less = quarter - quarter // 4
    more = block // 2 - less
    last_steps = (less, more, more, less)
    cap = slots(tiles, sectors)
    tables = (source_sector, source_tile)
    near, far = [1], list(range(2, sectors))

    weights = split_weights(matrix_id, cubic_weights)

    energies = energy_rate.shape[0]
    frame = 2 * block + 2 * PASSES
    energy_pad = jnp.pad(energy_rate[: energies - 1], ((PASSES, PASSES + 1), (0, 0)))
    pitch_pad = jnp.pad(pitch_rate[:, : pitches - 1], ((PASSES, PASSES), (0, 1)))
    first_energy = group * 2 * block
    a = across_lanes(lax.dynamic_slice_in_dim(energy_pad, first_energy, frame, 0), side)
    b = across_lanes(lax.dynamic_slice_in_dim(pitch_pad, first_energy, frame, 0), side)
    bin_ends = jnp.cumsum(bin_cells[0])
    cells = flip * (half * side) + jnp.arange(half * side, dtype=jnp.int32)
    bin_of = jnp.sum((bin_ends[None, :] <= cells[:, None]).astype(jnp.int32), axis=1)
    bins = jnp.arange(bin_ends.shape[0], dtype=jnp.int32)
    level = jnp.sum(jnp.where(bin_of[:, None] == bins[None, :], wave_level[0][None, :], 0.0), axis=1)
    rate = jnp.broadcast_to(level.reshape(half, 1, side), (half, 8, side))

    def at_lanes(t):
        return pl.ds(pl.multiple_of(t * side, side), side)

    def side_here():
        return lax.axis_index("inner") % 2

    swap = [(i, i ^ 1) for i in range(inner)]
    own_pairs, got_pairs = [], []
    for i in range(inner):
        for pairs, shift in ((own_pairs, -2 if i % 2 == 0 else 2), (got_pairs, 2 if i % 2 == 0 else -2)):
            if 0 <= i + shift < inner:
                pairs.append((i, i + shift))

    own, got, own_halo, got_halo = [], [], [], []
    packed = []
    start = 0
    for k, step in enumerate(first_steps):

        def first_of(start=start, step=step):
            here = side_here()
            return here * (block - start - step) + (1 - here) * start

        def find(field, first_of=first_of, step=step):
            first = first_of()
            return lambda t: [(t >= 0, lambda: field.at[pl.ds(first, step), :, at_lanes(t)])]

        def find_all(field):
            return lambda t: [(t >= 0, lambda: field.at[:, :, at_lanes(t)])]

        def receive(came, other, slot, first_of=first_of, step=step):
            if other == 2:
                return came.at[0, slot]
            return came.at[slot, pl.ds(first_of(), step)] if other == 1 else came.at[slot]

        def place(kept, sent):
            here = side_here()
            mine = lambda t: (t // half) == here
            return lambda t: [
                (mine(t), lambda: kept.at[t % half]),
                (jnp.logical_not(mine(t)), lambda: sent.at[t % half]),
            ]

        packed.append((start, step, find, receive, place))
        start += step

    def pack_first(k, after):
        start, step, find, _, _ = packed[k]
        groups = [(d, find, (step, pitches, side)) for d in far]
        if k == 0:
            groups += [(d, find_all, (block, pitches, side)) for d in near]
        return pack(groups, cap, tables, [density], after)

    sends = pack_first(0, ())
    beside = sector_exchange(sends[-1:], near)
    came = []
    far_queue(came, sends[0])
    token, tokens = None, []
    for k, (start, step, find, receive, place) in enumerate(packed):
        if k + 1 < len(packed):
            before = tokens[k - 1] if k else sends[0]
            far_queue(came, pack_first(k + 1, (before,))[0])
        if k == 1:
            came[k], (rate, a, b) = in_turn(came[k], [rate, a, b])
        part = jax.ShapeDtypeStruct((half, step, pitches, side), F32)
        piece = (step, pitches, side)
        after = ([] if token is None else [token]) + own_halo * (k == 1)
        kept, sent, token = drift(
            find, place, receive, tables, weights, [density], beside + came[k], [part, part], piece, after
        )
        tokens.append(token)
        own.append(kept)
        if k > 0:
            (sent,), (got[k - 1],) = in_turn([sent], [got[k - 1]])
        got.append(lax.ppermute(sent, "inner", swap))
        if 0 < k <= halo_chunks:
            forward = got[k - 1]
            if k > 1:
                (forward,), (got_halo[k - 2],) = in_turn([forward], [got_halo[k - 2]])
            got_halo.append(lax.ppermute(forward, "inner", got_pairs))
        if k < halo_chunks:
            if k > 0:
                (kept,), (own_halo[k - 1],) = in_turn([kept], [own_halo[k - 1]])
            own_halo.append(lax.ppermute(kept, "inner", own_pairs))

    fields = (rate, a, b, own, got, own_halo, got_halo)
    quad = half // 2
    kept_low, low = diffuse(*fields, (last_steps[0] + last_steps[1], *last_steps[2:]), 0, quad)
    kept_high, high = diffuse(*fields, last_steps, quad, quad)

    ready, out, start = [], (), 0
    for k, step in enumerate(last_steps):

        def find(mine_low, mine_high, their_low, their_high, k=k, start=start, step=step):
            here, there = pl.ds(start, step), pl.ds(start if k < 2 else 0, step)

            def pieces(t):
                ours = (t // half) == side_here()
                rank = t % half
                lower = rank < quad
                both, theirs = jnp.logical_and, jnp.logical_not(ours)
                upper = jnp.logical_not(lower)
                return [
                    (both(ours, lower), lambda: mine_low.at[rank % quad, here]),
                    (both(ours, upper), lambda: mine_high.at[rank % quad, here]),
                    (both(theirs, lower), lambda: their_low.at[rank % quad, there]),
                    (both(theirs, upper), lambda: their_high.at[rank % quad]),
                ]

            return pieces

        def place(result, start=start, step=step):
            return lambda t: [(t >= 0, lambda: result.at[pl.ds(start, step), :, at_lanes(t)])]

        ready.append((find, place, (step, pitches, side)))
        start += step

    def receive_slot(came, other, slot):
        return came.at[0, slot] if other == 2 else came.at[slot]

    def pack_last(k, after):
        find, _, piece = ready[k]
        local = [kept_low, kept_high, backs_low[k], backs_high[k]]
        sends = pack([(d, find, piece) for d in far + near], cap, tables, local, after)
        return sends[1:], sends[0]

    whole = [jax.ShapeDtypeStruct(density.shape, F32)]
    early = lax.ppermute(low[0], "inner", swap)
    (last,), (early,) = in_turn([high[0]], [early])
    backs_low, backs_high = [early, early], [lax.ppermute(last, "inner", swap)]
    (last,), (backs_high[0],) = in_turn([high[1]], [backs_high[0]])
    backs_high.append(lax.ppermute(last, "inner", swap))
    sends, far_sends = pack_last(0, ())
    came = []
    far_queue(came, far_sends)
    beside = sector_exchange(sends, near)
    token = None
    for k, (find, place, piece) in enumerate(ready):
        after = [] if token is None else [token]
        if k + 1 < len(ready):
            sends, far_sends = pack_last(k + 1, after)
            far_queue(came, far_sends)
            beside_next = sector_exchange(sends, near)
        if k + 2 < len(ready):
            pair, (backs_high[k + 1], came[k][0]) = in_turn(
                [low[k + 1], high[k + 2]], [backs_high[k + 1], came[k][0]]
            )
            backs_low.append(lax.ppermute(pair[0], "inner", swap))
            backs_high.append(lax.ppermute(pair[1], "inner", swap))
        local = [kept_low, kept_high, backs_low[k], backs_high[k]]
        *out, token = drift(
            find, place, receive_slot, tables, weights, local, beside + came[k], whole, piece, after, out
        )
        beside = beside_next
    return out[0]


def slots(tiles, sectors):
    return max(2, (3 * tiles + 2 * sectors - 1) // (2 * sectors))


def order_within(sources):
    tile_count = sources.shape[1]
    same = sources[:, :, None] == sources[:, None, :]
    earlier = jnp.arange(tile_count)[None, :] < jnp.arange(tile_count)[:, None]
    return jnp.sum((same & earlier[None]).astype(jnp.int32), axis=2)


def drift_step(density, source_sector, source_tile, matrix_id, cubic_weights):
    sectors = lax.axis_size("sector")
    sector_here = lax.axis_index("sector")
    energies, pitches, cell_count = density.shape
    tile_len = cubic_weights.shape[1]
    tile_count = cell_count // tile_len
    slot_count = max(2, (3 * tile_count + 2 * sectors - 1) // (2 * sectors))
    sources = source_sector[0]
    picked_tiles = source_tile[0]
    matrix_ids = matrix_id[0]
    tile_ranks = order_within(sources)
    slot_rank = jnp.arange(slot_count, dtype=jnp.int32)
    matched = (sources[:, None, :] == sector_here) & (
        tile_ranks[:, None, :] == slot_rank[None, :, None]
    )
    chosen = jnp.sum(jnp.where(matched, picked_tiles[:, None, :], 0), axis=2).reshape(-1)
    filled = jnp.any(matched, axis=2).reshape(-1).astype(jnp.float32)
    blocks = density.reshape(energies, pitches, tile_count, tile_len)
    outgoing = jnp.take(blocks, chosen, axis=2) * filled[None, None, :, None]
    incoming = lax.all_to_all(outgoing, "sector", split_axis=2, concat_axis=2, tiled=True)
    own_sources = sources[sector_here]
    own_ranks = tile_ranks[sector_here]
    own_ids = matrix_ids[sector_here]
    where_from = own_sources * slot_count + own_ranks
    departing = jnp.take(incoming, where_from, axis=2)
    matrices = jnp.take(cubic_weights, own_ids, axis=0)
    drifted = jnp.einsum("eptj,tij->epti", departing, matrices, precision=lax.Precision.HIGHEST)
    return drifted.reshape(energies, pitches, cell_count)


def one_pass(field, rate_cell, energy_rate, pitch_rate):
    flux_e = energy_rate[:-1, :, None] * (field[1:] - field[:-1])
    flux_p = pitch_rate[:, :-1, None] * (field[:, 1:] - field[:, :-1])
    change_e = jnp.pad(flux_e, ((0, 1), (0, 0), (0, 0))) - jnp.pad(flux_e, ((1, 0), (0, 0), (0, 0)))
    change_p = jnp.pad(flux_p, ((0, 0), (0, 1), (0, 0))) - jnp.pad(flux_p, ((0, 0), (1, 0), (0, 0)))
    return field + rate_cell[None, None, :] * (change_e + change_p)


def shards(
    density,
    source_sector,
    source_tile,
    matrix_id,
    cubic_weights,
    bin_cells,
    wave_level,
    energy_rate,
    pitch_rate,
):
    first = drift_step(density, source_sector, source_tile, matrix_id, cubic_weights)
    inner_count = lax.axis_size("inner")
    inner_here = lax.axis_index("inner")
    cell_count = first.shape[2]
    lengths = bin_cells[0]
    per_device = cell_count // inner_count
    owner_cells = jnp.full((inner_count,), per_device, jnp.int32)
    owner_ends = jnp.cumsum(owner_cells)
    owner_starts = owner_ends - owner_cells
    offsets = jnp.arange(per_device, dtype=jnp.int32)
    cell_index = owner_starts[:, None] + offsets[None, :]
    valid = (offsets[None, :] < owner_cells[:, None]).reshape(-1).astype(jnp.float32)
    clipped = jnp.minimum(cell_index, cell_count - 1).reshape(-1)
    packed = jnp.take(first, clipped, axis=2) * valid[None, None, :]
    cellwise = lax.all_to_all(packed, "inner", split_axis=2, concat_axis=0, tiled=True)
    bin_ends = jnp.cumsum(lengths)
    global_cells = owner_starts[inner_here] + offsets
    is_live = (offsets < owner_cells[inner_here]).astype(jnp.float32)
    bin_of = jnp.sum((bin_ends[None, :] <= global_cells[:, None]).astype(jnp.int32), axis=1)
    onehot = bin_of[:, None] == jnp.arange(inner_count, dtype=jnp.int32)[None, :]
    cell_level = jnp.sum(jnp.where(onehot, wave_level[0][None, :], 0.0), axis=1) * is_live

    def loop_body(step, current):
        return one_pass(current, cell_level, energy_rate, pitch_rate)

    diffused = lax.fori_loop(0, PASSES, loop_body, cellwise)
    returned = lax.all_to_all(diffused, "inner", split_axis=0, concat_axis=2, tiled=True)
    every_cell = jnp.arange(cell_count, dtype=jnp.int32)
    owner_index = jnp.sum((owner_ends[None, :] <= every_cell[:, None]).astype(jnp.int32), axis=1)
    offset = every_cell - owner_starts[owner_index]
    position = owner_index * per_device + offset
    restored = jnp.take(returned, position, axis=2)
    return drift_step(restored, source_sector, source_tile, matrix_id, cubic_weights)


def pairs_fit(mesh, energies, pitches, cells, side):
    sectors, inner = mesh.shape["sector"], mesh.shape["inner"]
    block = energies // inner
    tiles = cells // sectors // side
    return (
        sectors == 4
        and inner % 2 == 0
        and tiles % 4 == 0
        and pitches % 16 == 0
        and side % 128 == 0
        and block % 16 == 0
        and 4 * PASSES == 3 * block
    )


def solution(mesh):
    specs = (
        P("inner", None, "sector"),
        P("inner", None, None),
        P("inner", None, None),
        P("inner", None, None),
        P(),
        P("sector", None),
        P("sector", None),
        P(),
        P(),
    )

    def whole(*arrays):
        energies, pitches, cells = arrays[0].shape
        fits = pairs_fit(mesh, energies, pitches, cells, arrays[4].shape[1])
        return jax.shard_map(
            paired_shards if fits else shards,
            mesh=mesh,
            in_specs=specs,
            out_specs=P("inner", None, "sector"),
            check_vma=False,
        )(*arrays)

    return whole
```

```python
import functools

import jax
import jax.numpy as jnp
from jax import lax
from jax.experimental import pallas as pl
from jax.experimental.pallas import tpu as pltpu
from jax.sharding import PartitionSpec as P

PASSES = 12
VMEM_LIMIT = 64 * 1024 * 1024 - 128 * 1024
ANY = pl.BlockSpec(memory_space=pltpu.HBM)
SMEM = pl.BlockSpec(memory_space=pltpu.SMEM)
VMEM = pl.BlockSpec(memory_space=pltpu.VMEM)
F32 = jnp.float32
BF16 = jnp.bfloat16


def params():
    return pltpu.CompilerParams(vmem_limit_bytes=VMEM_LIMIT)


def cost():
    return pl.CostEstimate(flops=0, bytes_accessed=1024, transcendentals=0)


def weights_kernel(mid_ref, w_ref, out_ref, raw, sems):
    tiles, side = raw.shape[0], raw.shape[1]
    me = lax.axis_index("sector")

    def copy(t):
        return pltpu.make_async_copy(w_ref.at[mid_ref[0, me, t]], raw.at[t], sems.at[t])

    @pl.loop(0, tiles)
    def _(t):
        copy(t).start()

    @pl.loop(0, tiles)
    def _(t):
        copy(t).wait()
        turned = jnp.transpose(raw[t])
        high = turned.astype(BF16)
        low = (turned - high.astype(F32)).astype(BF16)
        out_ref[t, :side, :side] = high
        out_ref[t, side:, :side] = high
        out_ref[t, :side, side:] = low
        out_ref[t, side:, side:] = jnp.zeros((side, side), BF16)


def split_weights(matrix_id, cubic_weights):
    tiles, side = matrix_id.shape[2], cubic_weights.shape[1]
    return pl.pallas_call(
        weights_kernel,
        out_shape=jax.ShapeDtypeStruct((tiles, 2 * side, 2 * side), BF16),
        in_specs=[SMEM, ANY],
        out_specs=VMEM,
        scratch_shapes=[
            pltpu.VMEM((tiles, side, side), F32),
            pltpu.SemaphoreType.DMA((tiles,)),
        ],
        compiler_params=params(),
        cost_estimate=cost(),
        name="split_weights",
    )(matrix_id, cubic_weights)


def pack_kernel(offsets, finds, n_far, n_arrays, sec_ref, til_ref, *refs):
    tiles, n = sec_ref.shape[2], len(offsets)
    near = n - n_far
    sends, rooms = refs[-n - 2 - (near + (n_far > 0)) : -n - 2], refs[-n - 2 : -2]
    if n_far:
        sends = [sends[0].at[i] for i in range(n_far)] + list(sends[1:])
    in_sems, out_sems = refs[-2:]
    me = lax.axis_index("sector")
    counts = []
    for i, d in enumerate(offsets):
        dest = me ^ d
        pieces = finds[i](*refs[:n_arrays])

        def body(t, count, i=i, dest=dest, pieces=pieces):
            hit = sec_ref[0, dest, t] == me

            @pl.when(hit)
            def _():
                for guard, piece in pieces(til_ref[0, dest, t]):

                    @pl.when(guard)
                    def _():
                        pltpu.make_async_copy(piece(), rooms[i].at[count], in_sems.at[i, count]).start()

            return count + hit.astype(jnp.int32)

        counts.append(lax.fori_loop(0, tiles, body, jnp.int32(0)))
    for i in range(n):

        @pl.loop(0, counts[i])
        def _(slot, i=i):
            here = rooms[i].at[slot]
            pltpu.make_async_copy(here, here, in_sems.at[i, slot]).wait()
            pltpu.make_async_copy(here, sends[i].at[slot], out_sems.at[i, slot]).start()

    for i in range(n):

        @pl.loop(0, counts[i])
        def _(slot, i=i):
            pltpu.make_async_copy(rooms[i].at[slot], sends[i].at[slot], out_sems.at[i, slot]).wait()


def pack(groups, cap, tables, arrays, after=()):
    n = len(groups)
    offsets, finds, shapes = zip(*groups)
    n_far = sum(d > 1 for d in offsets)
    outs = [(n_far, cap) + shapes[0]] * (n_far > 0) + [(cap,) + shape for shape in shapes[n_far:]]
    return pl.pallas_call(
        functools.partial(pack_kernel, offsets, finds, n_far, len(arrays)),
        out_shape=[jax.ShapeDtypeStruct(out, F32) for out in outs],
        in_specs=[SMEM, SMEM] + [ANY] * (len(arrays) + len(after)),
        out_specs=[ANY] * len(outs),
        scratch_shapes=[
            *[pltpu.VMEM((cap,) + shape, F32) for shape in shapes],
            pltpu.SemaphoreType.DMA((n, cap)),
            pltpu.SemaphoreType.DMA((n, cap)),
        ],
        compiler_params=params(),
        cost_estimate=cost(),
        name="pack_tiles",
    )(*tables, *arrays, *after)


def sector_exchange(sends, offsets):
    sectors = lax.axis_size("sector")
    return [
        lax.ppermute(send, "sector", [(s, s ^ d) for s in range(sectors)])
        for d, send in zip(offsets, sends)
    ]


def far_queue(came, send):
    if len(came) > 1:
        (send,), (came[-2][0],) = in_turn([send], [came[-2][0]])
    sectors = lax.axis_size("sector")
    whole = lax.ppermute(send, "sector", [(s, s ^ 2) for s in range(sectors)])
    came.append([whole, lax.ppermute(whole[1], "sector", [(s, s ^ 1) for s in range(sectors)])])


def in_turn(later, earlier):
    both = lax.optimization_barrier((*later, *earlier))
    return list(both[: len(later)]), list(both[len(later) :])


def drift_kernel(find, place, receive, n_local, n_extra, sec_ref, til_ref, w_ref, *refs):
    sectors, tiles = sec_ref.shape[1], sec_ref.shape[2]
    local, recvs = refs[:n_local], refs[n_local : n_local + sectors - 1]
    outs = refs[n_local + sectors - 1 + n_extra : -7]
    token, taken, made, w_room, in_sems, out_sems, w_sems = refs[-7:]
    pieces = find(*local)
    put = place(*outs)
    me = lax.axis_index("sector")
    rows, side = taken.shape[1] * taken.shape[2], taken.shape[3]
    token[...] = jnp.zeros(token.shape, F32)

    def matrix(t):
        return pltpu.make_async_copy(w_ref.at[t], w_room.at[t], w_sems.at[t])

    def fetch(t, counts):
        matrix(t).start()
        d = sec_ref[0, me, t] ^ me

        @pl.when(d == 0)
        def _():
            for guard, piece in pieces(til_ref[0, me, t]):

                @pl.when(guard)
                def _():
                    pltpu.make_async_copy(piece(), taken.at[t], in_sems.at[t]).start()

        for other in range(1, sectors):

            @pl.when(d == other)
            def _(other=other):
                came = receive(recvs[other - 1], other, counts[other - 1])
                pltpu.make_async_copy(came, taken.at[t], in_sems.at[t]).start()

        return tuple(c + (d == i + 1).astype(jnp.int32) for i, c in enumerate(counts))

    lax.fori_loop(0, tiles, fetch, (jnp.int32(0),) * (sectors - 1))

    @pl.loop(0, tiles, unroll=4)
    def _(t):
        matrix(t).wait()
        pltpu.make_async_copy(taken.at[t], taken.at[t], in_sems.at[t]).wait()
        value = taken[t].reshape(rows, side)
        high = value.astype(BF16)
        low = (value - high.astype(F32)).astype(BF16)
        both = jnp.dot(jnp.concatenate([high, low], axis=1), w_room[t], preferred_element_type=F32)
        made[t] = (both[:, :side] + both[:, side:]).reshape(taken.shape[1:])
        for guard, there in put(t):

            @pl.when(guard)
            def _():
                pltpu.make_async_copy(made.at[t], there(), out_sems.at[t]).start()

    @pl.loop(0, tiles)
    def _(t):
        pltpu.make_async_copy(made.at[t], made.at[t], out_sems.at[t]).wait()


def drift(find, place, receive, tables, weights, local, recvs, outs, piece, after=(), carried=()):
    sectors, tiles = tables[0].shape[1], tables[0].shape[2]
    n_local = len(local)
    ins = [*tables, weights, *local, *recvs, *after, *carried]
    n_extra = len(after) + len(carried)
    return pl.pallas_call(
        functools.partial(drift_kernel, find, place, receive, n_local, n_extra),
        out_shape=[*outs, jax.ShapeDtypeStruct((8, 128), F32)],
        in_specs=[SMEM, SMEM] + [ANY] * (len(ins) - 2),
        out_specs=[ANY] * len(outs) + [VMEM],
        scratch_shapes=[
            pltpu.VMEM((tiles,) + piece, F32),
            pltpu.VMEM((tiles,) + piece, F32),
            pltpu.VMEM(weights.shape, BF16),
            pltpu.SemaphoreType.DMA((tiles,)),
            pltpu.SemaphoreType.DMA((tiles,)),
            pltpu.SemaphoreType.DMA((tiles,)),
        ],
        input_output_aliases={len(ins) - 1: 0} if carried else {},
        compiler_params=params(),
        cost_estimate=cost(),
        name="drift_chunk",
    )(*ins)


def diffusion_kernel(n_own, n_halo, n_send, first_tile, rate_ref, a_ref, b_ref, *refs):
    n_in = 2 * n_own + 2 * n_halo
    ins, keep, sends = refs[:n_in], refs[n_in], refs[n_in + 1 : n_in + 1 + n_send]
    field, work, ra_ref, rb_ref, done, in_sems, out_sems = refs[n_in + 1 + n_send :]
    tiles, block = keep.shape[0], keep.shape[1]
    frame, pitches, side = work.shape
    halo = (frame - 2 * block) // 2
    vregs = pitches // 8
    flip = lax.axis_index("inner") % 2
    places, start = [], 0
    for i in range(n_own):
        step = ins[i].shape[1]
        places.append((i, step, halo + start))
        places.append((n_own + i, step, halo + 2 * block - start - step))
        if i < n_halo:
            places.append((2 * n_own + i, step, halo + 2 * block + start))
            places.append((2 * n_own + n_halo + i, step, halo - start - step))
        start += step

    def fetch(g, slot):
        copies = []
        for i, step, place in places:
            at = jnp.where(flip == 0, place, frame - place - step)
            copies.append(
                pltpu.make_async_copy(
                    ins[i].at[first_tile + g], field.at[slot, pl.ds(at, step)], in_sems.at[slot, i]
                )
            )
        return copies

    def store(g, slot):
        copies = [
            pltpu.make_async_copy(
                done.at[slot, pl.ds(flip * block, block)], keep.at[g], out_sems.at[slot, n_send]
            )
        ]
        first = (1 - flip) * block
        for k in range(n_send):
            step = sends[k].shape[1]
            copies.append(
                pltpu.make_async_copy(
                    done.at[slot, pl.ds(first, step)], sends[k].at[g], out_sems.at[slot, k]
                )
            )
            first = first + step
        return copies

    for copy in fetch(0, 0):
        copy.start()

    @pl.loop(0, tiles)
    def _(g):
        slot = g % 2

        @pl.when(g + 1 < tiles)
        def _():
            for copy in fetch(g + 1, 1 - slot):
                copy.start()

        for copy in fetch(g, slot):
            copy.wait()

        @pl.when(g >= 2)
        def _():
            for copy in store(g - 2, slot):
                copy.wait()

        rate = rate_ref[first_tile + g]

        def rows_of(ref, e):
            return [ref[e, 8 * v : 8 * v + 8, :] for v in range(vregs)]

        def write_work(e, rows):
            for v in range(vregs):
                work[e, 8 * v : 8 * v + 8, :] = rows[v]

        def read_work(e):
            return rows_of(work, e)

        def read_field(e):
            return [field[slot, e, pl.ds(v, 8, stride=vregs), :] for v in range(vregs)]

        def write_done(e, rows):
            for v in range(vregs):
                done[slot, e - halo, pl.ds(v, 8, stride=vregs), :] = rows[v]

        def scaled(e):
            ra = [rate * x for x in rows_of(a_ref, e)]
            rb = [rate * x for x in rows_of(b_ref, e)]
            for v in range(vregs):
                ra_ref[e, 8 * v : 8 * v + 8, :] = ra[v]
                rb_ref[e, 8 * v : 8 * v + 8, :] = rb[v]
            return ra, rb

        def ready(e):
            return rows_of(ra_ref, e), rows_of(rb_ref, e)

        def sweep(first, count, read, write, rates, wide):
            def energy(e, here, below):
                after = read(e + 1)
                ra, rb = rates(e)
                above = [ra[v] * (after[v] - here[v]) for v in range(vregs)]
                nearby = here[1:] + [pltpu.roll(here[0], 7, 0)]
                pitch = [rb[v] * (nearby[v] - here[v]) for v in range(vregs)]
                before = [pltpu.roll(pitch[-1], 1, 0)] + pitch[:-1]
                write(
                    e,
                    [
                        here[v] + ((above[v] - below[v]) + (pitch[v] - before[v]))
                        for v in range(vregs)
                    ],
                )
                return after, above

            def several(e, carry, n):
                here, below = list(carry[:vregs]), list(carry[vregs:])
                for i in range(n):
                    here, below = energy(e + i, here, below)
                return (*here, *below)

            edge = read(first - 1)
            here = read(first)
            ra = rates(first - 1)[0]
            below = [ra[v] * (here[v] - edge[v]) for v in range(vregs)]
            carry = lax.fori_loop(
                0,
                count // wide,
                lambda i, carry: several(first + wide * i, carry, wide),
                (*here, *below),
            )
            for left in range(2, wide, 2):

                @pl.when(count % wide == left)
                def _(left=left):
                    several(first + count - left, carry, left)

        sweep(1, frame - 2, read_field, write_work, scaled, 2)

        @pl.loop(1, PASSES - 1)
        def _(n):
            sweep(n + 1, frame - 2 - 2 * n, read_work, write_work, ready, 4)

        sweep(PASSES, frame - 2 * PASSES, read_work, write_done, ready, 4)

        for copy in store(g, slot):
            copy.start()

    for g in range(max(0, tiles - 2), tiles):
        for copy in store(g, g % 2):
            copy.wait()


def diffuse(rate, a, b, own, got, own_halo, got_halo, steps, first_tile, tiles):
    pitches, side = own[0].shape[2:]
    frame = a.shape[0]
    block = sum(steps)
    ins = [*own, *got, *own_halo, *got_halo]
    out = pl.pallas_call(
        functools.partial(diffusion_kernel, len(own), len(own_halo), len(steps), first_tile),
        out_shape=[
            jax.ShapeDtypeStruct((tiles, step, pitches, side), F32) for step in (block, *steps)
        ],
        in_specs=[VMEM] * 3 + [ANY] * len(ins),
        out_specs=[ANY] * (1 + len(steps)),
        scratch_shapes=[
            pltpu.VMEM((2, frame, pitches, side), F32),
            pltpu.VMEM((frame, pitches, side), F32),
            pltpu.VMEM((frame, pitches, side), F32),
            pltpu.VMEM((frame, pitches, side), F32),
            pltpu.VMEM((2, 2 * block, pitches, side), F32),
            pltpu.SemaphoreType.DMA((2, len(ins))),
            pltpu.SemaphoreType.DMA((2, len(steps) + 1)),
        ],
        compiler_params=params(),
        cost_estimate=cost(),
        name="diffuse_tiles",
    )(rate, a, b, *ins)
    return out[0], out[1:]


def across_lanes(window, side):
    frame, pitches = window.shape
    turned = window.reshape(frame, 8, pitches // 8).transpose(0, 2, 1).reshape(frame, pitches)
    return jnp.broadcast_to(turned[:, :, None], (frame, pitches, side))


def paired_shards(
    density,
    source_sector,
    source_tile,
    matrix_id,
    cubic_weights,
    bin_cells,
    wave_level,
    energy_rate,
    pitch_rate,
):
    sectors, inner = lax.axis_size("sector"), lax.axis_size("inner")
    inner_here = lax.axis_index("inner")
    flip, group = inner_here % 2, inner_here // 2
    block, pitches, cell_count = density.shape
    side = cubic_weights.shape[1]
    tiles = cell_count // side
    half = tiles // 2
    quarter = block // 4
    first_steps = (quarter, quarter, quarter, quarter - quarter // 4, quarter // 4)
    halo_chunks = PASSES // quarter
    less = quarter - quarter // 4
    more = block // 2 - less
    last_steps = (less, more, more, less)
    cap = slots(tiles, sectors)
    tables = (source_sector, source_tile)
    near, far = [1], list(range(2, sectors))

    weights = split_weights(matrix_id, cubic_weights)

    energies = energy_rate.shape[0]
    frame = 2 * block + 2 * PASSES
    energy_pad = jnp.pad(energy_rate[: energies - 1], ((PASSES, PASSES + 1), (0, 0)))
    pitch_pad = jnp.pad(pitch_rate[:, : pitches - 1], ((PASSES, PASSES), (0, 1)))
    first_energy = group * 2 * block
    a = across_lanes(lax.dynamic_slice_in_dim(energy_pad, first_energy, frame, 0), side)
    b = across_lanes(lax.dynamic_slice_in_dim(pitch_pad, first_energy, frame, 0), side)
    bin_ends = jnp.cumsum(bin_cells[0])
    cells = flip * (half * side) + jnp.arange(half * side, dtype=jnp.int32)
    bin_of = jnp.sum((bin_ends[None, :] <= cells[:, None]).astype(jnp.int32), axis=1)
    bins = jnp.arange(bin_ends.shape[0], dtype=jnp.int32)
    level = jnp.sum(jnp.where(bin_of[:, None] == bins[None, :], wave_level[0][None, :], 0.0), axis=1)
    rate = jnp.broadcast_to(level.reshape(half, 1, side), (half, 8, side))

    def at_lanes(t):
        return pl.ds(pl.multiple_of(t * side, side), side)

    def side_here():
        return lax.axis_index("inner") % 2

    swap = [(i, i ^ 1) for i in range(inner)]
    own_pairs, got_pairs = [], []
    for i in range(inner):
        for pairs, shift in ((own_pairs, -2 if i % 2 == 0 else 2), (got_pairs, 2 if i % 2 == 0 else -2)):
            if 0 <= i + shift < inner:
                pairs.append((i, i + shift))

    own, got, own_halo, got_halo = [], [], [], []
    packed = []
    start = 0
    for k, step in enumerate(first_steps):

        def first_of(start=start, step=step):
            here = side_here()
            return here * (block - start - step) + (1 - here) * start

        def find(field, first_of=first_of, step=step):
            first = first_of()
            return lambda t: [(t >= 0, lambda: field.at[pl.ds(first, step), :, at_lanes(t)])]

        def find_all(field):
            return lambda t: [(t >= 0, lambda: field.at[:, :, at_lanes(t)])]

        def receive(came, other, slot, first_of=first_of, step=step):
            if other == 2:
                return came.at[0, slot]
            return came.at[slot, pl.ds(first_of(), step)] if other == 1 else came.at[slot]

        def place(kept, sent):
            here = side_here()
            mine = lambda t: (t // half) == here
            return lambda t: [
                (mine(t), lambda: kept.at[t % half]),
                (jnp.logical_not(mine(t)), lambda: sent.at[t % half]),
            ]

        packed.append((start, step, find, receive, place))
        start += step

    def pack_first(k, after):
        start, step, find, _, _ = packed[k]
        groups = [(d, find, (step, pitches, side)) for d in far]
        if k == 0:
            groups += [(d, find_all, (block, pitches, side)) for d in near]
        return pack(groups, cap, tables, [density], after)

    sends = pack_first(0, ())
    beside = sector_exchange(sends[-1:], near)
    came = []
    far_queue(came, sends[0])
    token, tokens = None, []
    for k, (start, step, find, receive, place) in enumerate(packed):
        if k + 1 < len(packed):
            before = tokens[k - 1] if k else sends[0]
            far_queue(came, pack_first(k + 1, (before,))[0])
        if k == 1:
            came[k], (rate, a, b) = in_turn(came[k], [rate, a, b])
        part = jax.ShapeDtypeStruct((half, step, pitches, side), F32)
        piece = (step, pitches, side)
        after = ([] if token is None else [token]) + own_halo * (k == 1)
        kept, sent, token = drift(
            find, place, receive, tables, weights, [density], beside + came[k], [part, part], piece, after
        )
        tokens.append(token)
        own.append(kept)
        if k > 0:
            (sent,), (got[k - 1],) = in_turn([sent], [got[k - 1]])
        got.append(lax.ppermute(sent, "inner", swap))
        if 0 < k <= halo_chunks:
            forward = got[k - 1]
            if k > 1:
                (forward,), (got_halo[k - 2],) = in_turn([forward], [got_halo[k - 2]])
            got_halo.append(lax.ppermute(forward, "inner", got_pairs))
        if k < halo_chunks:
            if k > 0:
                (kept,), (own_halo[k - 1],) = in_turn([kept], [own_halo[k - 1]])
            own_halo.append(lax.ppermute(kept, "inner", own_pairs))

    fields = (rate, a, b, own, got, own_halo, got_halo)
    quad = half // 2
    kept_low, low = diffuse(*fields, (last_steps[0] + last_steps[1], *last_steps[2:]), 0, quad)
    kept_high, high = diffuse(*fields, last_steps, quad, quad)

    ready, out, start = [], (), 0
    for k, step in enumerate(last_steps):

        def find(mine_low, mine_high, their_low, their_high, k=k, start=start, step=step):
            here, there = pl.ds(start, step), pl.ds(start if k < 2 else 0, step)

            def pieces(t):
                ours = (t // half) == side_here()
                rank = t % half
                lower = rank < quad
                both, theirs = jnp.logical_and, jnp.logical_not(ours)
                upper = jnp.logical_not(lower)
                return [
                    (both(ours, lower), lambda: mine_low.at[rank % quad, here]),
                    (both(ours, upper), lambda: mine_high.at[rank % quad, here]),
                    (both(theirs, lower), lambda: their_low.at[rank % quad, there]),
                    (both(theirs, upper), lambda: their_high.at[rank % quad]),
                ]

            return pieces

        def place(result, start=start, step=step):
            return lambda t: [(t >= 0, lambda: result.at[pl.ds(start, step), :, at_lanes(t)])]

        ready.append((find, place, (step, pitches, side)))
        start += step

    def receive_slot(came, other, slot):
        return came.at[0, slot] if other == 2 else came.at[slot]

    def pack_last(k, after):
        find, _, piece = ready[k]
        local = [kept_low, kept_high, backs_low[k], backs_high[k]]
        sends = pack([(d, find, piece) for d in far + near], cap, tables, local, after)
        return sends[1:], sends[0]

    whole = [jax.ShapeDtypeStruct(density.shape, F32)]
    early = lax.ppermute(low[0], "inner", swap)
    (last,), (early,) = in_turn([high[0]], [early])
    backs_low, backs_high = [early, early], [lax.ppermute(last, "inner", swap)]
    (last,), (backs_high[0],) = in_turn([high[1]], [backs_high[0]])
    backs_high.append(lax.ppermute(last, "inner", swap))
    sends, far_sends = pack_last(0, ())
    came = []
    far_queue(came, far_sends)
    beside = sector_exchange(sends, near)
    token = None
    for k, (find, place, piece) in enumerate(ready):
        after = [] if token is None else [token]
        if k + 1 < len(ready):
            sends, far_sends = pack_last(k + 1, after)
            far_queue(came, far_sends)
            beside_next = sector_exchange(sends, near)
        if k + 2 < len(ready):
            pair, (backs_high[k + 1], came[k][0]) = in_turn(
                [low[k + 1], high[k + 2]], [backs_high[k + 1], came[k][0]]
            )
            backs_low.append(lax.ppermute(pair[0], "inner", swap))
            backs_high.append(lax.ppermute(pair[1], "inner", swap))
        local = [kept_low, kept_high, backs_low[k], backs_high[k]]
        *out, token = drift(
            find, place, receive_slot, tables, weights, local, beside + came[k], whole, piece, after, out
        )
        beside = beside_next
    return out[0]


def slots(tiles, sectors):
    return max(2, (3 * tiles + 2 * sectors - 1) // (2 * sectors))


def order_within(sources):
    tile_count = sources.shape[1]
    same = sources[:, :, None] == sources[:, None, :]
    earlier = jnp.arange(tile_count)[None, :] < jnp.arange(tile_count)[:, None]
    return jnp.sum((same & earlier[None]).astype(jnp.int32), axis=2)


def drift_step(density, source_sector, source_tile, matrix_id, cubic_weights):
    sectors = lax.axis_size("sector")
    sector_here = lax.axis_index("sector")
    energies, pitches, cell_count = density.shape
    tile_len = cubic_weights.shape[1]
    tile_count = cell_count // tile_len
    slot_count = max(2, (3 * tile_count + 2 * sectors - 1) // (2 * sectors))
    sources = source_sector[0]
    picked_tiles = source_tile[0]
    matrix_ids = matrix_id[0]
    tile_ranks = order_within(sources)
    slot_rank = jnp.arange(slot_count, dtype=jnp.int32)
    matched = (sources[:, None, :] == sector_here) & (
        tile_ranks[:, None, :] == slot_rank[None, :, None]
    )
    chosen = jnp.sum(jnp.where(matched, picked_tiles[:, None, :], 0), axis=2).reshape(-1)
    filled = jnp.any(matched, axis=2).reshape(-1).astype(jnp.float32)
    blocks = density.reshape(energies, pitches, tile_count, tile_len)
    outgoing = jnp.take(blocks, chosen, axis=2) * filled[None, None, :, None]
    incoming = lax.all_to_all(outgoing, "sector", split_axis=2, concat_axis=2, tiled=True)
    own_sources = sources[sector_here]
    own_ranks = tile_ranks[sector_here]
    own_ids = matrix_ids[sector_here]
    where_from = own_sources * slot_count + own_ranks
    departing = jnp.take(incoming, where_from, axis=2)
    matrices = jnp.take(cubic_weights, own_ids, axis=0)
    drifted = jnp.einsum("eptj,tij->epti", departing, matrices, precision=lax.Precision.HIGHEST)
    return drifted.reshape(energies, pitches, cell_count)


def one_pass(field, rate_cell, energy_rate, pitch_rate):
    flux_e = energy_rate[:-1, :, None] * (field[1:] - field[:-1])
    flux_p = pitch_rate[:, :-1, None] * (field[:, 1:] - field[:, :-1])
    change_e = jnp.pad(flux_e, ((0, 1), (0, 0), (0, 0))) - jnp.pad(flux_e, ((1, 0), (0, 0), (0, 0)))
    change_p = jnp.pad(flux_p, ((0, 0), (0, 1), (0, 0))) - jnp.pad(flux_p, ((0, 0), (1, 0), (0, 0)))
    return field + rate_cell[None, None, :] * (change_e + change_p)


def shards(
    density,
    source_sector,
    source_tile,
    matrix_id,
    cubic_weights,
    bin_cells,
    wave_level,
    energy_rate,
    pitch_rate,
):
    first = drift_step(density, source_sector, source_tile, matrix_id, cubic_weights)
    inner_count = lax.axis_size("inner")
    inner_here = lax.axis_index("inner")
    cell_count = first.shape[2]
    lengths = bin_cells[0]
    per_device = cell_count // inner_count
    owner_cells = jnp.full((inner_count,), per_device, jnp.int32)
    owner_ends = jnp.cumsum(owner_cells)
    owner_starts = owner_ends - owner_cells
    offsets = jnp.arange(per_device, dtype=jnp.int32)
    cell_index = owner_starts[:, None] + offsets[None, :]
    valid = (offsets[None, :] < owner_cells[:, None]).reshape(-1).astype(jnp.float32)
    clipped = jnp.minimum(cell_index, cell_count - 1).reshape(-1)
    packed = jnp.take(first, clipped, axis=2) * valid[None, None, :]
    cellwise = lax.all_to_all(packed, "inner", split_axis=2, concat_axis=0, tiled=True)
    bin_ends = jnp.cumsum(lengths)
    global_cells = owner_starts[inner_here] + offsets
    is_live = (offsets < owner_cells[inner_here]).astype(jnp.float32)
    bin_of = jnp.sum((bin_ends[None, :] <= global_cells[:, None]).astype(jnp.int32), axis=1)
    onehot = bin_of[:, None] == jnp.arange(inner_count, dtype=jnp.int32)[None, :]
    cell_level = jnp.sum(jnp.where(onehot, wave_level[0][None, :], 0.0), axis=1) * is_live

    def loop_body(step, current):
        return one_pass(current, cell_level, energy_rate, pitch_rate)

    diffused = lax.fori_loop(0, PASSES, loop_body, cellwise)
    returned = lax.all_to_all(diffused, "inner", split_axis=0, concat_axis=2, tiled=True)
    every_cell = jnp.arange(cell_count, dtype=jnp.int32)
    owner_index = jnp.sum((owner_ends[None, :] <= every_cell[:, None]).astype(jnp.int32), axis=1)
    offset = every_cell - owner_starts[owner_index]
    position = owner_index * per_device + offset
    restored = jnp.take(returned, position, axis=2)
    return drift_step(restored, source_sector, source_tile, matrix_id, cubic_weights)


def pairs_fit(mesh, energies, pitches, cells, side):
    sectors, inner = mesh.shape["sector"], mesh.shape["inner"]
    block = energies // inner
    tiles = cells // sectors // side
    return (
        sectors == 4
        and inner % 2 == 0
        and tiles % 4 == 0
        and pitches % 16 == 0
        and side % 128 == 0
        and block % 16 == 0
        and 4 * PASSES == 3 * block
    )


def solution(mesh):
    specs = (
        P("inner", None, "sector"),
        P("inner", None, None),
        P("inner", None, None),
        P("inner", None, None),
        P(),
        P("sector", None),
        P("sector", None),
        P(),
        P(),
    )

    def whole(*arrays):
        energies, pitches, cells = arrays[0].shape
        fits = pairs_fit(mesh, energies, pitches, cells, arrays[4].shape[1])
        return jax.shard_map(
            paired_shards if fits else shards,
            mesh=mesh,
            in_specs=specs,
            out_specs=P("inner", None, "sector"),
            check_vma=False,
        )(*arrays)

    return whole
```
